32 devices in a mesh: cgrp: 4 (over z), dev: 8 (over y, x, core).
Axes of the slice: x: 2, y: 2, z: 4, core: 2. Of those that a mesh axis runs over, the one named last changes fastest.
Arguments:
- docs: bfloat16 [16384, 1024], P('dev'), may hold values from -140 to 140
- centroids: float32 [1024, 1024], P(('cgrp', 'dev')), may hold values from -6 to 6
Outputs:
- centroids_next: float32 [1024, 1024], P(('cgrp', 'dev'))
- mass: float32 [1024], P(('cgrp', 'dev'))
- doc_lse: float32 [16384], P('dev')
The draws below stay inside these ranges and needn't reach their ends.
All inputs are finite; a program needn't handle non-finite values.
Results may differ from the reference program's by a relative error of at most 0.012.
The reference program's roundings to bfloat16 on the way (of `rounded`) count: a program that leaves them out, or rounds other values in their place, can miss the bound.
Values may be sent and summed in bfloat16 or wider, within the bound.
No kernel may reach another device: no remote copies, remote signals or barrier semaphores. Data moves between devices by JAX's collectives and lax.ppermute only.
A program may use at most 64 MiB of HBM per device.

```python
import math
import jax
import jax.numpy as jnp
from jax import lax

D = 1024
DOCS = 16384
K = 1024


def centroid_table(key):
    first_key = jax.random.fold_in(key, 11)
    return jnp.clip(jax.random.normal(first_key, (K, D)), -6.0, 6.0).astype(jnp.float32)


def draw_centroids(key, part):
    return centroid_table(key)


def draw_docs(key, part):
    table = centroid_table(key)
    key = jax.random.fold_in(key, 5)
    base = jnp.clip(jax.random.normal(jax.random.fold_in(key, 23), (DOCS, D)), -6.0, 6.0)
    first = jax.random.randint(jax.random.fold_in(key, 31), (DOCS,), 0, K)
    second = (first + jax.random.randint(jax.random.fold_in(key, 37), (DOCS,), 1, K)) % K
    levels = jnp.array([210.0, 260.0, 320.0], jnp.float32)
    target = levels[jax.random.randint(jax.random.fold_in(key, 41), (DOCS,), 0, 3)]
    strength = 0.5 + target / (4.0 * math.sqrt(D))
    beta = 4.0 / math.sqrt(D)
    delta = 2.0 / (beta * strength * D)
    aligned = strength[:, None] * (table[first] + (1.0 + delta)[:, None] * table[second])
    chosen = jnp.arange(DOCS) % 8 == 0
    base = jnp.where(chosen[:, None], aligned, base)
    return jnp.clip(base, -140.0, 140.0).astype(jnp.float32).astype(jnp.bfloat16)


def setup_inputs(seed: int = 0) -> dict:
    streams_of = jax.random.split(jax.random.key(seed), 3)
    docs = draw_docs(jax.random.fold_in(streams_of[2], 71), 0)
    centroids = draw_centroids(jax.random.fold_in(streams_of[2], 71), 0)
    return dict(docs=docs, centroids=centroids)


def block_scores(docs, cent_block):
    scale = 4.0 / math.sqrt(docs.shape[1])
    rounded = cent_block.astype(jnp.bfloat16)
    wide = rounded.astype(jnp.float32)
    norms = lax.optimization_barrier(jnp.sum(wide * wide, axis=1))
    dots = jnp.dot(docs, rounded.T, preferred_element_type=jnp.float32)
    return (dots - 0.5 * norms[None, :]) * scale

def reference(docs, centroids):
    width = 2048 if K >= 2048 else K
    blocks = centroids.reshape(K // width, width, D)
    docs_wide = docs.astype(jnp.float32)

    def stat_step(carry, cent_block):
        run_max, run_sum = carry
        scores = block_scores(docs, cent_block)
        new_max = jnp.maximum(run_max, lax.optimization_barrier(jnp.max(scores, axis=1)))
        run_sum = run_sum * jnp.exp(run_max - new_max) + lax.optimization_barrier(jnp.sum(jnp.exp(scores - new_max[:, None]), axis=1))
        return ((new_max, run_sum), None)
    start = (jnp.full((DOCS,), -1e+30, jnp.float32), jnp.zeros((DOCS,), jnp.float32))
    (run_max, run_sum), unused = lax.scan(stat_step, start, blocks)
    doc_lse = run_max + jnp.log(run_sum)

    def update(cent_block):
        scores = block_scores(docs, cent_block)
        resp = jnp.exp(scores - doc_lse[:, None])
        mass = lax.optimization_barrier(jnp.sum(resp, axis=0))
        weighted = jnp.dot(resp.T, docs_wide, preferred_element_type=jnp.float32, precision=lax.Precision.HIGHEST)
        return ((weighted + cent_block) / (mass[:, None] + 1.0), mass)
    new_blocks, masses = lax.map(update, blocks)
    return (new_blocks.reshape(K, D), masses.reshape(K), doc_lse)
```

```python
import math

import jax
import jax.numpy as jnp
from jax import lax
from jax.sharding import PartitionSpec as P


def swap(x, axis, size, mask):
    return lax.ppermute(x, axis, [(i, i ^ mask) for i in range(size)])


def tree(parts, op):
    while len(parts) > 1:
        parts = [op(parts[i], parts[i + 1]) for i in range(0, len(parts), 2)]
    return parts[0]


def make_body(n, g):
    def body(docs, centroids):
        rows, width = centroids.shape
        scale = 4.0 / math.sqrt(width)
        rounded = centroids.astype(jnp.bfloat16)
        mine = jnp.concatenate(
            [rounded] + [swap(rounded, "dev", n, m) for m in range(2, n, 2)], axis=0
        )
        theirs = swap(mine, "dev", n, 1)
        table = jnp.concatenate([mine, theirs], axis=0)
        wide = table.astype(jnp.float32)
        norms = jnp.sum(wide * wide, axis=1)
        dots = lax.dot_general(
            docs, table, (((1,), (1,)), ((), ())), preferred_element_type=jnp.float32
        )
        scores = (dots - 0.5 * norms[None, :]) * scale
        top = jnp.max(scores, axis=1)
        group_lse = top + jnp.log(jnp.sum(jnp.exp(scores - top[:, None]), axis=1))
        all_lse = [group_lse] + [swap(group_lse, "cgrp", g, m) for m in range(1, g)]
        best = tree(all_lse, jnp.maximum)
        doc_lse = best + jnp.log(tree([jnp.exp(x - best) for x in all_lse], jnp.add))
        resp = jnp.exp(scores - doc_lse[:, None])
        mass = jnp.sum(resp, axis=0)
        term = lax.dot_general(
            resp.astype(jnp.bfloat16), docs, (((0,), (0,)), ((), ())),
            preferred_element_type=jnp.float32,
        )
        lane = lax.broadcasted_iota(jnp.int32, (1, 128), 1)

        def pack(term, mass):
            high = mass.astype(jnp.bfloat16)
            low = (mass - high.astype(jnp.float32)).astype(jnp.bfloat16)
            extra = jnp.where(
                lane == 0, high[:, None], jnp.where(lane == 1, low[:, None], 0)
            ).astype(jnp.bfloat16)
            return jnp.concatenate([term.astype(jnp.bfloat16), extra], axis=1)

        def unpack(x):
            wide = x.astype(jnp.float32)
            return wide[:, :width], wide[:, width] + wide[:, width + 1]

        half = table.shape[0] // 2
        got = swap(pack(term[half:], mass[half:]), "dev", n, 1)
        got_term, got_mass = unpack(got)
        term = term[:half] + got_term
        mass = mass[:half] + got_mass
        packed = pack(term[rows:], mass[rows:])
        arrived = [
            unpack(swap(packed[(j - 1) * rows : j * rows], "dev", n, 2 * j))
            for j in range(1, n // 2)
        ]
        weighted = tree([term[:rows]] + [a for a, _ in arrived], jnp.add)
        mass = tree([mass[:rows]] + [b for _, b in arrived], jnp.add)
        return ((weighted + centroids) / (mass[:, None] + 1.0), mass, doc_lse)

    return body


def solution(mesh):
    in_specs = (P("dev", None), P(("cgrp", "dev"), None))
    out_specs = (P(("cgrp", "dev"), None), P(("cgrp", "dev")), P("dev"))
    return jax.shard_map(
        make_body(mesh.shape["dev"], mesh.shape["cgrp"]),
        mesh=mesh, in_specs=in_specs, out_specs=out_specs, check_vma=False,
    )
```

```python
import math

import jax
import jax.numpy as jnp
from jax import lax
from jax.sharding import PartitionSpec as P


def make_body(n, g):
    def body(docs, centroids):
        rows, width = centroids.shape
        scale = 4.0 / math.sqrt(width)
        rounded = centroids.astype(jnp.bfloat16)
        table = lax.all_to_all(jnp.tile(rounded, (n, 1)), "dev", 0, 0, tiled=True)
        wide = table.astype(jnp.float32)
        norms = jnp.sum(wide * wide, axis=1)
        dots = lax.dot_general(
            docs, table, (((1,), (1,)), ((), ())), preferred_element_type=jnp.float32
        )
        scores = (dots - 0.5 * norms[None, :]) * scale
        top = jnp.max(scores, axis=1)
        group_lse = top + jnp.log(jnp.sum(jnp.exp(scores - top[:, None]), axis=1))
        everyone = jnp.tile(group_lse.reshape(1, -1, 128), (g, 1, 1))
        all_lse = lax.all_to_all(everyone, "cgrp", 0, 0, tiled=True).reshape(g, -1)
        best = jnp.max(all_lse, axis=0)
        doc_lse = best + jnp.log(jnp.sum(jnp.exp(all_lse - best), axis=0))
        resp = jnp.exp(scores - doc_lse[:, None])
        mass = jnp.sum(resp, axis=0)
        term = lax.dot_general(
            resp.astype(jnp.bfloat16), docs, (((0,), (0,)), ((), ())),
            preferred_element_type=jnp.float32,
        )
        lane = lax.broadcasted_iota(jnp.int32, (1, 128), 1)

        def pack(term, mass):
            high = mass.astype(jnp.bfloat16)
            low = (mass - high.astype(jnp.float32)).astype(jnp.bfloat16)
            extra = jnp.where(
                lane == 0, high[:, None], jnp.where(lane == 1, low[:, None], 0)
            ).astype(jnp.bfloat16)
            return jnp.concatenate([term.astype(jnp.bfloat16), extra], axis=1)

        def unpack(x):
            wide = x.astype(jnp.float32)
            return wide[:, :width], wide[:, width] + wide[:, width + 1]

        arrived = lax.all_to_all(pack(term, mass), "dev", 0, 0, tiled=True)
        arrived_term, arrived_mass = unpack(arrived)
        weighted = jnp.sum(arrived_term.reshape(n, rows, width), axis=0)
        mass = jnp.sum(arrived_mass.reshape(n, rows), axis=0)
        return ((weighted + centroids) / (mass[:, None] + 1.0), mass, doc_lse)

    return body


def solution(mesh):
    in_specs = (P("dev", None), P(("cgrp", "dev"), None))
    out_specs = (P(("cgrp", "dev"), None), P(("cgrp", "dev")), P("dev"))
    return jax.shard_map(
        make_body(mesh.shape["dev"], mesh.shape["cgrp"]),
        mesh=mesh, in_specs=in_specs, out_specs=out_specs, check_vma=False,
    )
```

```python
import math

import jax
import jax.numpy as jnp
from jax import lax
from jax.sharding import PartitionSpec as P


def chip_step(x, n, step):
    bits = (n // 2).bit_length() - 1
    pairs = []
    for i in range(n):
        bit = step if i % 2 == 0 else bits - 1 - step
        pairs.append((i, i ^ (2 << bit)))
    return lax.ppermute(x, "dev", pairs)


def core_swap(x, n):
    return lax.ppermute(x, "dev", [(i, i ^ 1) for i in range(n)])


def group_swap(x, g, mask):
    return lax.ppermute(x, "cgrp", [(i, i ^ mask) for i in range(g)])


def log_add(a, b):
    top = jnp.maximum(a, b)
    return top + jnp.log(jnp.exp(a - top) + jnp.exp(b - top))


def make_body(n, g):
    steps = (n // 2).bit_length() - 1

    def body(docs, centroids):
        rows, width = centroids.shape
        scale = 4.0 / math.sqrt(width)
        mine = centroids.astype(jnp.bfloat16)
        for step in range(steps):
            mine = jnp.concatenate([mine, chip_step(mine, n, step)], axis=0)
        table = jnp.concatenate([mine, core_swap(mine, n)], axis=0)
        wide = table.astype(jnp.float32)
        norms = jnp.sum(wide * wide, axis=1)
        dots = lax.dot_general(
            docs, table, (((1,), (1,)), ((), ())), preferred_element_type=jnp.float32
        )
        scores = (dots - 0.5 * norms[None, :]) * scale
        top = jnp.max(scores, axis=1)
        doc_lse = top + jnp.log(jnp.sum(jnp.exp(scores - top[:, None]), axis=1))
        mask = 1
        while mask < g:
            doc_lse = log_add(doc_lse, group_swap(doc_lse, g, mask))
            mask *= 2
        resp = jnp.exp(scores - doc_lse[:, None])
        mass = jnp.sum(resp, axis=0)
        term = lax.dot_general(
            resp.astype(jnp.bfloat16), docs, (((0,), (0,)), ((), ())),
            preferred_element_type=jnp.float32,
        )
        lane = lax.broadcasted_iota(jnp.int32, (1, 128), 1)

        def pack(term, mass):
            high = mass.astype(jnp.bfloat16)
            low = (mass - high.astype(jnp.float32)).astype(jnp.bfloat16)
            extra = jnp.where(
                lane == 0, high[:, None], jnp.where(lane == 1, low[:, None], 0)
            ).astype(jnp.bfloat16)
            return jnp.concatenate([term.astype(jnp.bfloat16), extra], axis=1)

        def fold(term, mass, swap):
            half = term.shape[0] // 2
            got = swap(pack(term[half:], mass[half:])).astype(jnp.float32)
            term = term[:half] + got[:, :width]
            mass = mass[:half] + (got[:, width] + got[:, width + 1])
            return term, mass

        term, mass = fold(term, mass, lambda x: core_swap(x, n))
        for step in reversed(range(steps)):
            term, mass = fold(term, mass, lambda x: chip_step(x, n, step))
        return ((term + centroids) / (mass[:, None] + 1.0), mass, doc_lse)

    return body


def solution(mesh):
    in_specs = (P("dev", None), P(("cgrp", "dev"), None))
    out_specs = (P(("cgrp", "dev"), None), P(("cgrp", "dev")), P("dev"))
    return jax.shard_map(
        make_body(mesh.shape["dev"], mesh.shape["cgrp"]),
        mesh=mesh, in_specs=in_specs, out_specs=out_specs, check_vma=False,
    )
```

```python
import functools
import math

import jax
import jax.numpy as jnp
from jax import lax
from jax.experimental import pallas as pl
from jax.experimental.pallas import tpu as pltpu
from jax.sharding import PartitionSpec as P

LANES = 128
VMEM = pl.BlockSpec(memory_space=pltpu.VMEM)
PARAMS = pltpu.CompilerParams(vmem_limit_bytes=40 * 1024 * 1024)


def swap(x, axis, size, mask):
    return lax.ppermute(x, axis, [(i, i ^ mask) for i in range(size)])


def tree(parts, op):
    while len(parts) > 1:
        parts = [op(parts[i], parts[i + 1]) for i in range(0, len(parts), 2)]
    return parts[0]


def scores_kernel(chunk, docs_ref, mine_ref, theirs_ref, part_ref, top_ref, lse_ref):
    count, width = docs_ref.shape
    scale = 4.0 / math.sqrt(width)
    table = jnp.concatenate([mine_ref[...], theirs_ref[...]], axis=0)
    wide = table.astype(jnp.float32)
    half_norms = 0.5 * jnp.sum(wide * wide, axis=1, keepdims=True)
    for start in range(0, count, chunk):
        cols = slice(start, start + chunk)
        dots = lax.dot_general(
            table, docs_ref[cols, :], (((1,), (1,)), ((), ())),
            preferred_element_type=jnp.float32,
        )
        scores = (dots - half_norms) * scale
        top = jnp.max(scores, axis=0, keepdims=True)
        part = jnp.exp(scores - top)
        part_ref[:, cols] = part
        top_ref[:, cols] = top
        lse_ref[:, cols] = top + jnp.log(jnp.sum(part, axis=0, keepdims=True))


def with_mass(term, mass):
    high = mass.astype(jnp.bfloat16).astype(jnp.float32)
    lane = lax.broadcasted_iota(jnp.int32, (term.shape[0], LANES), 1)
    extra = jnp.where(lane == 0, high, jnp.where(lane == 1, mass - high, 0.0))
    return jnp.concatenate([term, extra], axis=1).astype(jnp.bfloat16)


def read_rows(rows, width):
    wide = rows.astype(jnp.float32)
    return wide[:, :width], wide[:, width:width + 1] + wide[:, width + 1:width + 2]


def weights_kernel(groups, chunk, *refs):
    lse_refs = refs[:groups]
    docs_ref, part_ref, top_ref = refs[groups:groups + 3]
    doc_lse_ref, keep_ref, keep_mass_ref, send_ref, resp_ref = refs[groups + 3:]
    parts = [r[...] for r in lse_refs]
    best = tree(parts, jnp.maximum)
    doc_lse = best + jnp.log(tree([jnp.exp(x - best) for x in parts], jnp.add))
    doc_lse_ref[...] = doc_lse
    factor = jnp.exp(top_ref[...] - doc_lse)
    rows, count = part_ref.shape
    half, width = keep_ref.shape
    mass = jnp.zeros((rows, 1), jnp.float32)
    for start in range(0, count, chunk):
        cols = slice(start, start + chunk)
        resp = part_ref[:, cols] * factor[:, cols]
        mass += jnp.sum(resp, axis=1, keepdims=True)
        resp_ref[:, cols] = resp.astype(jnp.bfloat16)
    keep_mass_ref[...] = jnp.broadcast_to(mass[:half], keep_mass_ref.shape)
    high = mass[half:].astype(jnp.bfloat16).astype(jnp.float32)
    lane = lax.broadcasted_iota(jnp.int32, (half, LANES), 1)
    extra = jnp.where(lane == 0, high, jnp.where(lane == 1, mass[half:] - high, 0.0))
    send_ref[:, width:] = extra.astype(jnp.bfloat16)
    for start in range(0, width, chunk):
        cols = slice(start, start + chunk)
        term = jnp.dot(resp_ref[...], docs_ref[:, cols], preferred_element_type=jnp.float32)
        keep_ref[:, cols] = term[:half]
        send_ref[:, cols] = term[half:].astype(jnp.bfloat16)


def fold_kernel(keep_ref, keep_mass_ref, got_ref, own_ref, own_mass_ref, *send_refs):
    rows, width = own_ref.shape
    for slot in range(keep_ref.shape[0] // rows):
        here = slice(slot * rows, (slot + 1) * rows)
        got, got_mass = read_rows(got_ref[here], width)
        term = keep_ref[here] + got
        mass = keep_mass_ref[here, :1] + got_mass
        if slot == 0:
            own_ref[...] = term
            own_mass_ref[...] = jnp.broadcast_to(mass, own_mass_ref.shape)
        else:
            send_refs[slot - 1][...] = with_mass(term, mass)


def final_kernel(own_ref, own_mass_ref, cent_ref, *refs):
    *got_refs, next_ref, mass_ref = refs
    width = own_ref.shape[1]
    got = [read_rows(r[...], width) for r in got_refs]
    term = tree([own_ref[...]] + [a for a, _ in got], jnp.add)
    mass = tree([own_mass_ref[:, :1]] + [b for _, b in got], jnp.add)
    next_ref[...] = (term + cent_ref[...]) / (mass + 1.0)
    mass_ref[...] = mass


def shape(dims, dtype=jnp.float32):
    return jax.ShapeDtypeStruct(dims, dtype)


def call(kernel, outs, *args, scratch=()):
    return pl.pallas_call(
        kernel,
        out_shape=outs,
        in_specs=[VMEM] * len(args),
        out_specs=[VMEM] * len(outs),
        scratch_shapes=scratch,
        compiler_params=PARAMS,
    )(*args)


def make_body(n, g):
    def body(docs, centroids):
        rows, width = centroids.shape
        count = docs.shape[0]
        group, half = rows * n, rows * n // 2
        chunk = 256
        rounded = centroids.astype(jnp.bfloat16)
        mine = jnp.concatenate(
            [rounded] + [swap(rounded, "dev", n, m) for m in range(2, n, 2)], axis=0
        )
        theirs = swap(mine, "dev", n, 1)
        part, top, lse = call(
            functools.partial(scores_kernel, chunk),
            [shape((group, count)), shape((1, count)), shape((1, count))],
            docs, mine, theirs,
        )
        all_lse = [lse] + [swap(lse, "cgrp", g, m) for m in range(1, g)]
        doc_lse, keep, keep_mass, send = call(
            functools.partial(weights_kernel, g, chunk),
            [shape((1, count)), shape((half, width)), shape((half, LANES)),
             shape((half, width + LANES), jnp.bfloat16)],
            *all_lse, docs, part, top,
            scratch=[pltpu.VMEM((group, count), jnp.bfloat16)],
        )
        got = swap(send, "dev", n, 1)
        own, own_mass, *sends = call(
            fold_kernel,
            [shape((rows, width)), shape((rows, LANES))]
            + [shape((rows, width + LANES), jnp.bfloat16)] * (n // 2 - 1),
            keep, keep_mass, got,
        )
        arrived = [swap(x, "dev", n, 2 * (j + 1)) for j, x in enumerate(sends)]
        result, mass = call(
            final_kernel, [shape((rows, width)), shape((rows, 1))],
            own, own_mass, centroids, *arrived,
        )
        return (result, mass.reshape(rows), doc_lse.reshape(count))

    return body


def solution(mesh):
    in_specs = (P("dev", None), P(("cgrp", "dev"), None))
    out_specs = (P(("cgrp", "dev"), None), P(("cgrp", "dev")), P("dev"))
    return jax.shard_map(
        make_body(mesh.shape["dev"], mesh.shape["cgrp"]),
        mesh=mesh, in_specs=in_specs, out_specs=out_specs, check_vma=False,
    )
```

```python
import functools
import math

import jax
import jax.numpy as jnp
from jax import lax
from jax.experimental import pallas as pl
from jax.experimental.pallas import tpu as pltpu
from jax.sharding import PartitionSpec as P

LANES = 128
VMEM = pl.BlockSpec(memory_space=pltpu.VMEM)
SMEM = pl.BlockSpec(memory_space=pltpu.SMEM)
PARAMS = pltpu.CompilerParams(vmem_limit_bytes=40 * 1024 * 1024)


def swap(x, axis, size, mask):
    return lax.ppermute(x, axis, [(i, i ^ mask) for i in range(size)])


def exchange(x, axis, plan):
    return [lax.ppermute(x, axis, pairs) for pairs in plan]


def group_plan(g):
    if g == 4:
        return [
            [(0, 2), (2, 3)],
            [(0, 1), (1, 3), (3, 2)],
            [(0, 3), (1, 2), (2, 0), (3, 1)],
            [(3, 0)],
            [(1, 0), (2, 1)],
        ]
    return [[(i, i ^ m) for i in range(g)] for m in range(1, g)]


def tree(parts, op):
    while len(parts) > 1:
        parts = [op(parts[i], parts[i + 1]) for i in range(0, len(parts), 2)]
    return parts[0]


def scores_kernel(chunk, docs_ref, mine_ref, theirs_ref, part_ref, top_ref, lse_ref):
    count, width = docs_ref.shape
    scale = 4.0 / math.sqrt(width)
    table = jnp.concatenate([mine_ref[...], theirs_ref[...]], axis=0)
    wide = table.astype(jnp.float32)
    half_norms = 0.5 * jnp.sum(wide * wide, axis=1, keepdims=True)
    for start in range(0, count, chunk):
        cols = slice(start, start + chunk)
        dots = lax.dot_general(
            table, docs_ref[cols, :], (((1,), (1,)), ((), ())),
            preferred_element_type=jnp.float32,
        )
        scores = (dots - half_norms) * scale
        top = jnp.max(scores, axis=0, keepdims=True)
        part = jnp.exp(scores - top)
        part_ref[:, cols] = part
        top_ref[:, cols] = top
        lse_ref[:, cols] = top + jnp.log(jnp.sum(part, axis=0, keepdims=True))


def with_mass(term, mass):
    high = mass.astype(jnp.bfloat16).astype(jnp.float32)
    lane = lax.broadcasted_iota(jnp.int32, (term.shape[0], LANES), 1)
    extra = jnp.where(lane == 0, high, jnp.where(lane == 1, mass - high, 0.0))
    return jnp.concatenate([term, extra], axis=1).astype(jnp.bfloat16)


def read_rows(rows, width):
    wide = rows.astype(jnp.float32)
    return wide[:, :width], wide[:, width:width + 1] + wide[:, width + 1:width + 2]


def weights_kernel(groups, plan, chunk, me_ref, own_ref, *refs):
    got_refs = refs[:len(plan)]
    docs_ref, part_ref, top_ref = refs[len(plan):len(plan) + 3]
    doc_lse_ref, keep_ref, keep_mass_ref, send_ref, resp_ref = refs[len(plan) + 3:]
    me = me_ref[0]
    parts = [own_ref[...]] * groups
    for got_ref, pairs in zip(got_refs, plan):
        got = got_ref[...]
        for source, target in pairs:
            parts[source] = jnp.where(me == target, got, parts[source])
    best = tree(parts, jnp.maximum)
    doc_lse = best + jnp.log(tree([jnp.exp(x - best) for x in parts], jnp.add))
    doc_lse_ref[...] = doc_lse
    factor = jnp.exp(top_ref[...] - doc_lse)
    rows, count = part_ref.shape
    half, width = keep_ref.shape
    mass = jnp.zeros((rows, 1), jnp.float32)
    for start in range(0, count, chunk):
        cols = slice(start, start + chunk)
        resp = part_ref[:, cols] * factor[:, cols]
        mass += jnp.sum(resp, axis=1, keepdims=True)
        resp_ref[:, cols] = resp.astype(jnp.bfloat16)
    keep_mass_ref[...] = jnp.broadcast_to(mass[:half], keep_mass_ref.shape)
    high = mass[half:].astype(jnp.bfloat16).astype(jnp.float32)
    lane = lax.broadcasted_iota(jnp.int32, (half, LANES), 1)
    extra = jnp.where(lane == 0, high, jnp.where(lane == 1, mass[half:] - high, 0.0))
    send_ref[:, width:] = extra.astype(jnp.bfloat16)
    for start in range(0, width, chunk):
        cols = slice(start, start + chunk)
        term = jnp.dot(resp_ref[...], docs_ref[:, cols], preferred_element_type=jnp.float32)
        keep_ref[:, cols] = term[:half]
        send_ref[:, cols] = term[half:].astype(jnp.bfloat16)


def fold_kernel(keep_ref, keep_mass_ref, got_ref, own_ref, own_mass_ref, *send_refs):
    rows, width = own_ref.shape
    for slot in range(keep_ref.shape[0] // rows):
        here = slice(slot * rows, (slot + 1) * rows)
        got, got_mass = read_rows(got_ref[here], width)
        term = keep_ref[here] + got
        mass = keep_mass_ref[here, :1] + got_mass
        if slot == 0:
            own_ref[...] = term
            own_mass_ref[...] = jnp.broadcast_to(mass, own_mass_ref.shape)
        else:
            send_refs[slot - 1][...] = with_mass(term, mass)


def final_kernel(own_ref, own_mass_ref, cent_ref, *refs):
    *got_refs, next_ref, mass_ref = refs
    width = own_ref.shape[1]
    got = [read_rows(r[...], width) for r in got_refs]
    term = tree([own_ref[...]] + [a for a, _ in got], jnp.add)
    mass = tree([own_mass_ref[:, :1]] + [b for _, b in got], jnp.add)
    next_ref[...] = (term + cent_ref[...]) / (mass + 1.0)
    mass_ref[...] = jnp.broadcast_to(mass, (mass.shape[0], LANES)).T[:1]


def after_docs_kernel(docs_ref, rounded_ref, own_ref):
    own_ref[...] = rounded_ref[...]


def after_docs(docs, rounded):
    own, = call(after_docs_kernel, [shape(rounded.shape, rounded.dtype)], docs, rounded)
    return own


def shape(dims, dtype=jnp.float32):
    return jax.ShapeDtypeStruct(dims, dtype)


def call(kernel, outs, *args, scratch=()):
    return pl.pallas_call(
        kernel,
        out_shape=outs,
        in_specs=[SMEM if x.dtype == jnp.int32 else VMEM for x in args],
        out_specs=[VMEM] * len(outs),
        scratch_shapes=scratch,
        compiler_params=PARAMS,
    )(*args)


def make_body(n, g):
    def body(docs, centroids):
        rows, width = centroids.shape
        count = docs.shape[0]
        group, half = rows * n, rows * n // 2
        chunk = 256
        plan = group_plan(g)
        rounded = centroids.astype(jnp.bfloat16)
        blocks = [swap(rounded, "dev", n, m) for m in range(2, n, 2)]
        rounded = after_docs(docs, rounded)
        mine = jnp.concatenate([rounded] + blocks, axis=0)
        theirs = swap(mine, "dev", n, 1)
        part, top, lse = call(
            functools.partial(scores_kernel, chunk),
            [shape((group, count)), shape((1, count)), shape((1, count))],
            docs, mine, theirs,
        )
        others = exchange(lse, "cgrp", plan)
        doc_lse, keep, keep_mass, send = call(
            functools.partial(weights_kernel, g, plan, chunk),
            [shape((1, count)), shape((half, width)), shape((half, LANES)),
             shape((half, width + LANES), jnp.bfloat16)],
            lax.axis_index("cgrp").reshape(1), lse, *others, docs, part, top,
            scratch=[pltpu.VMEM((group, count), jnp.bfloat16)],
        )
        got = swap(send, "dev", n, 1)
        own, own_mass, *sends = call(
            fold_kernel,
            [shape((rows, width)), shape((rows, LANES))]
            + [shape((rows, width + LANES), jnp.bfloat16)] * (n // 2 - 1),
            keep, keep_mass, got,
        )
        arrived = [swap(x, "dev", n, 2 * (j + 1)) for j, x in enumerate(sends)]
        result, mass = call(
            final_kernel, [shape((rows, width)), shape((1, rows))],
            own, own_mass, centroids, *arrived,
        )
        return (result, mass.reshape(rows), doc_lse.reshape(count))

    return body


def solution(mesh):
    in_specs = (P("dev", None), P(("cgrp", "dev"), None))
    out_specs = (P(("cgrp", "dev"), None), P(("cgrp", "dev")), P("dev"))
    return jax.shard_map(
        make_body(mesh.shape["dev"], mesh.shape["cgrp"]),
        mesh=mesh, in_specs=in_specs, out_specs=out_specs, check_vma=False,
    )
```

```python
import functools
import math

import jax
import jax.numpy as jnp
from jax import lax
from jax.experimental import pallas as pl
from jax.experimental.pallas import tpu as pltpu
from jax.sharding import PartitionSpec as P

LANES = 128
VMEM = pl.BlockSpec(memory_space=pltpu.VMEM)
SMEM = pl.BlockSpec(memory_space=pltpu.SMEM)


def swap(x, axis, size, mask):
    return lax.ppermute(x, axis, [(i, i ^ mask) for i in range(size)])


def group_plan(g):
    if g == 4:
        return [
            [(0, 1), (1, 0), (2, 3), (3, 2)],
            [(0, 3), (1, 2), (2, 0), (3, 1)],
            [(0, 2), (1, 3), (2, 1), (3, 0)],
        ]
    return [[(i, i ^ m) for i in range(g)] for m in range(1, g)]


def tree(parts, op):
    while len(parts) > 1:
        parts = [op(parts[i], parts[i + 1]) for i in range(0, len(parts), 2)]
    return parts[0]


def after_docs_kernel(docs_ref, rounded_ref, own_ref):
    own_ref[...] = rounded_ref[...]


def scores_kernel(chunk, docs_ref, table_ref, part_ref, top_ref, sum_ref):
    count, width = docs_ref.shape
    scale = 4.0 / math.sqrt(width)
    table = table_ref[...]
    wide = table.astype(jnp.float32)
    half_norms = 0.5 * jnp.sum(wide * wide, axis=1, keepdims=True)
    for start in range(0, count, chunk):
        cols = slice(start, start + chunk)
        dots = lax.dot_general(
            table, docs_ref[cols, :], (((1,), (1,)), ((), ())),
            preferred_element_type=jnp.float32,
        )
        scores = (dots - half_norms) * scale
        top = jnp.max(scores, axis=0, keepdims=True)
        part = jnp.exp(scores - top)
        part_ref[:, cols] = part
        top_ref[:, cols] = top
        sum_ref[:, cols] = jnp.sum(part, axis=0, keepdims=True)


def last_scores_kernel(
    chunk, docs_ref, table_ref, first_top_ref, first_sum_ref, part_ref, top_ref, lse_ref
):
    scores_kernel(chunk, docs_ref, table_ref, part_ref, top_ref, lse_ref)
    top = jnp.maximum(first_top_ref[...], top_ref[...])
    total = first_sum_ref[...] * jnp.exp(first_top_ref[...] - top)
    total += lse_ref[...] * jnp.exp(top_ref[...] - top)
    lse_ref[...] = top + jnp.log(total)


def weighted_sums(chunk, factor, docs_ref, part_ref, resp_ref, store):
    rows, count = part_ref.shape
    mass = jnp.zeros((rows, 1), jnp.float32)
    for start in range(0, count, chunk):
        cols = slice(start, start + chunk)
        resp = part_ref[:, cols] * factor[:, cols]
        mass += jnp.sum(resp, axis=1, keepdims=True)
        resp_ref[:, cols] = resp.astype(jnp.bfloat16)
    for start in range(0, docs_ref.shape[1], chunk):
        cols = slice(start, start + chunk)
        store(cols, jnp.dot(resp_ref[...], docs_ref[:, cols], preferred_element_type=jnp.float32))
    return mass


def mass_lanes(mass):
    high = mass.astype(jnp.bfloat16).astype(jnp.float32)
    lane = lax.broadcasted_iota(jnp.int32, (mass.shape[0], LANES), 1)
    lanes = jnp.where(lane == 0, high, jnp.where(lane == 1, mass - high, 0.0))
    return lanes.astype(jnp.bfloat16)


def read_rows(rows, width):
    wide = rows.astype(jnp.float32)
    return wide[:, :width], wide[:, width:width + 1] + wide[:, width + 1:width + 2]


def send_kernel(groups, plan, chunk, me_ref, lse_ref, *refs):
    got_refs = refs[:len(plan)]
    docs_ref, part_ref, top_ref, keep_top_ref = refs[len(plan):len(plan) + 4]
    doc_lse_ref, factor_ref, send_ref, resp_ref = refs[len(plan) + 4:]
    me = me_ref[0]
    parts = [lse_ref[...]] * groups
    for got_ref, pairs in zip(got_refs, plan):
        got = got_ref[...]
        for source, target in pairs:
            parts[source] = jnp.where(me == target, got, parts[source])
    best = tree(parts, jnp.maximum)
    doc_lse = best + jnp.log(tree([jnp.exp(x - best) for x in parts], jnp.add))
    doc_lse_ref[...] = doc_lse
    factor_ref[...] = jnp.exp(keep_top_ref[...] - doc_lse)
    factor = jnp.exp(top_ref[...] - doc_lse)

    def store(cols, term):
        send_ref[:, cols] = term.astype(jnp.bfloat16)

    mass = weighted_sums(chunk, factor, docs_ref, part_ref, resp_ref, store)
    send_ref[:, docs_ref.shape[1]:] = mass_lanes(mass)


def keep_kernel(chunk, factor_ref, docs_ref, part_ref, keep_ref, keep_mass_ref, resp_ref):
    def store(cols, term):
        keep_ref[:, cols] = term

    mass = weighted_sums(chunk, factor_ref[...], docs_ref, part_ref, resp_ref, store)
    keep_mass_ref[...] = jnp.broadcast_to(mass, keep_mass_ref.shape)


def fold_kernel(keep_ref, keep_mass_ref, got_ref, own_ref, own_mass_ref, *send_refs):
    rows, width = own_ref.shape
    for slot in range(keep_ref.shape[0] // rows):
        here = slice(slot * rows, (slot + 1) * rows)
        got, got_mass = read_rows(got_ref[here], width)
        term = keep_ref[here] + got
        mass = keep_mass_ref[here, :1] + got_mass
        if slot == 0:
            own_ref[...] = term
            own_mass_ref[...] = jnp.broadcast_to(mass, own_mass_ref.shape)
        else:
            send_refs[slot - 1][:, :width] = term.astype(jnp.bfloat16)
            send_refs[slot - 1][:, width:] = mass_lanes(mass)


def final_kernel(own_ref, own_mass_ref, cent_ref, *refs):
    *got_refs, next_ref, mass_ref = refs
    width = own_ref.shape[1]
    got = [read_rows(r[...], width) for r in got_refs]
    term = tree([own_ref[...]] + [a for a, _ in got], jnp.add)
    mass = tree([own_mass_ref[:, :1]] + [b for _, b in got], jnp.add)
    next_ref[...] = (term + cent_ref[...]) / (mass + 1.0)
    mass_ref[...] = jnp.broadcast_to(mass, (mass.shape[0], LANES)).T[:1]


def shape(dims, dtype=jnp.float32):
    return jax.ShapeDtypeStruct(dims, dtype)


def make_body(n, g):
    def body(docs, centroids):
        rows, width = centroids.shape
        count = docs.shape[0]
        half = rows * n // 2
        chunk = 256
        plan = group_plan(g)
        limit = (4 << 20) + half * (48 << 10)

        def call(kernel, outs, *args, scratch=(), flops=0):
            nbytes = sum(x.nbytes for x in args)
            return pl.pallas_call(
                kernel,
                out_shape=outs,
                in_specs=[SMEM if x.dtype == jnp.int32 else VMEM for x in args],
                out_specs=[VMEM] * len(outs),
                scratch_shapes=scratch,
                compiler_params=pltpu.CompilerParams(vmem_limit_bytes=limit),
                cost_estimate=pl.CostEstimate(
                    flops=flops, bytes_accessed=nbytes, transcendentals=0
                ),
            )(*args)

        flops = 2 * half * count * width
        stats = [shape((half, count)), shape((1, count)), shape((1, count))]
        resp = [pltpu.VMEM((half, count), jnp.bfloat16)]
        rounded = centroids.astype(jnp.bfloat16)
        blocks = [swap(rounded, "dev", n, m) for m in range(2, n, 2)]
        own, = call(after_docs_kernel, [shape(rounded.shape, rounded.dtype)], docs, rounded)
        mine = jnp.concatenate([own] + blocks, axis=0)
        theirs = swap(mine, "dev", n, 1)
        part, top, total = call(
            functools.partial(scores_kernel, chunk), stats, docs, mine, flops=flops
        )
        other_part, other_top, lse = call(
            functools.partial(last_scores_kernel, chunk), stats,
            docs, theirs, top, total, flops=flops,
        )
        others = [lax.ppermute(lse, "cgrp", pairs) for pairs in plan]
        doc_lse, factor, send = call(
            functools.partial(send_kernel, g, plan, chunk),
            [shape((1, count)), shape((1, count)), shape((half, width + LANES), jnp.bfloat16)],
            lax.axis_index("cgrp").reshape(1), lse, *others, docs, other_part, other_top, top,
            scratch=resp, flops=flops,
        )
        got = swap(send, "dev", n, 1)
        keep, keep_mass = call(
            functools.partial(keep_kernel, chunk),
            [shape((half, width)), shape((half, LANES))],
            factor, docs, part, scratch=resp, flops=flops,
        )
        own, own_mass, *sends = call(
            fold_kernel,
            [shape((rows, width)), shape((rows, LANES))]
            + [shape((rows, width + LANES), jnp.bfloat16)] * (n // 2 - 1),
            keep, keep_mass, got,
        )
        far_first = sorted(range(1, n // 2), key=lambda j: (-j.bit_count(), j))
        arrived = [swap(sends[j - 1], "dev", n, 2 * j) for j in far_first]
        result, mass = call(
            final_kernel, [shape((rows, width)), shape((1, rows))],
            own, own_mass, centroids, *arrived,
        )
        return (result, mass.reshape(rows), doc_lse.reshape(count))

    return body


def solution(mesh):
    in_specs = (P("dev", None), P(("cgrp", "dev"), None))
    out_specs = (P(("cgrp", "dev"), None), P(("cgrp", "dev")), P("dev"))
    return jax.shard_map(
        make_body(mesh.shape["dev"], mesh.shape["cgrp"]),
        mesh=mesh, in_specs=in_specs, out_specs=out_specs, check_vma=False,
    )
```

```python
import functools
import math

import jax
import jax.numpy as jnp
from jax import lax
from jax.experimental import pallas as pl
from jax.experimental.pallas import tpu as pltpu
from jax.sharding import PartitionSpec as P

LANES = 128
VMEM = pl.BlockSpec(memory_space=pltpu.VMEM)
SMEM = pl.BlockSpec(memory_space=pltpu.SMEM)


def swap(x, axis, size, mask):
    return lax.ppermute(x, axis, [(i, i ^ mask) for i in range(size)])


def group_plan(g):
    if g == 4:
        return [
            [(0, 1), (1, 0), (2, 3), (3, 2)],
            [(0, 3), (1, 2), (2, 0), (3, 1)],
            [(0, 2), (1, 3), (2, 1), (3, 0)],
        ]
    return [[(i, i ^ m) for i in range(g)] for m in range(1, g)]


def tree(parts, op):
    while len(parts) > 1:
        parts = [op(parts[i], parts[i + 1]) for i in range(0, len(parts), 2)]
    return parts[0]


def load_kernel(source_ref, rounded_ref, docs_ref, own_ref, sem):
    copy = pltpu.make_async_copy(source_ref, docs_ref, sem)
    copy.start()
    own_ref[...] = rounded_ref[...]
    copy.wait()


def load(source, rounded):
    outs = [shape(source.shape, source.dtype), shape(rounded.shape, rounded.dtype)]
    return pl.pallas_call(
        load_kernel,
        out_shape=outs,
        in_specs=[pl.BlockSpec(memory_space=pltpu.HBM), VMEM],
        out_specs=[VMEM, VMEM],
        scratch_shapes=[pltpu.SemaphoreType.DMA],
        compiler_params=pltpu.CompilerParams(vmem_limit_bytes=4 << 20),
        cost_estimate=pl.CostEstimate(
            flops=0, bytes_accessed=2 * source.nbytes, transcendentals=0
        ),
    )(pltpu.with_memory_space_constraint(source, pltpu.HBM), rounded)


def scores_kernel(chunk, docs_ref, table_ref, part_ref, top_ref, sum_ref):
    count, width = docs_ref.shape
    scale = 4.0 / math.sqrt(width)
    table = table_ref[...].T
    wide = table.astype(jnp.float32)
    half_norms = 0.5 * jnp.sum(wide * wide, axis=0, keepdims=True)
    for start in range(0, count, chunk):
        cols = slice(start, start + chunk)
        dots = jnp.dot(docs_ref[cols, :], table, preferred_element_type=jnp.float32)
        scores = ((dots - half_norms) * scale).T
        top = jnp.max(scores, axis=0, keepdims=True)
        part = jnp.exp(scores - top)
        part_ref[:, cols] = part
        top_ref[:, cols] = top
        sum_ref[:, cols] = jnp.sum(part, axis=0, keepdims=True)


def last_scores_kernel(
    chunk, docs_ref, table_ref, first_top_ref, first_sum_ref, part_ref, top_ref, lse_ref
):
    scores_kernel(chunk, docs_ref, table_ref, part_ref, top_ref, lse_ref)
    top = jnp.maximum(first_top_ref[...], top_ref[...])
    total = first_sum_ref[...] * jnp.exp(first_top_ref[...] - top)
    total += lse_ref[...] * jnp.exp(top_ref[...] - top)
    lse_ref[...] = top + jnp.log(total)


def weighted_sums(chunk, factor, docs_ref, part_ref, resp_ref, store):
    rows, count = part_ref.shape
    mass = jnp.zeros((rows, 1), jnp.float32)
    for start in range(0, count, chunk):
        cols = slice(start, start + chunk)
        resp = part_ref[:, cols] * factor[:, cols]
        mass += jnp.sum(resp, axis=1, keepdims=True)
        resp_ref[:, cols] = resp.astype(jnp.bfloat16)
    for start in range(0, docs_ref.shape[1], chunk):
        cols = slice(start, start + chunk)
        store(cols, jnp.dot(resp_ref[...], docs_ref[:, cols], preferred_element_type=jnp.float32))
    return mass


def mass_lanes(mass):
    high = mass.astype(jnp.bfloat16).astype(jnp.float32)
    lane = lax.broadcasted_iota(jnp.int32, (mass.shape[0], LANES), 1)
    lanes = jnp.where(lane == 0, high, jnp.where(lane == 1, mass - high, 0.0))
    return lanes.astype(jnp.bfloat16)


def read_rows(rows, width):
    wide = rows.astype(jnp.float32)
    return wide[:, :width], wide[:, width:width + 1] + wide[:, width + 1:width + 2]


def send_kernel(groups, plan, chunk, me_ref, lse_ref, *refs):
    got_refs = refs[:len(plan)]
    docs_ref, part_ref, top_ref, keep_top_ref = refs[len(plan):len(plan) + 4]
    doc_lse_ref, factor_ref, send_ref, resp_ref = refs[len(plan) + 4:]
    me = me_ref[0]
    parts = [lse_ref[...]] * groups
    for got_ref, pairs in zip(got_refs, plan):
        got = got_ref[...]
        for source, target in pairs:
            parts[source] = jnp.where(me == target, got, parts[source])
    best = tree(parts, jnp.maximum)
    doc_lse = best + jnp.log(tree([jnp.exp(x - best) for x in parts], jnp.add))
    doc_lse_ref[...] = doc_lse
    factor_ref[...] = jnp.exp(keep_top_ref[...] - doc_lse)
    factor = jnp.exp(top_ref[...] - doc_lse)

    def store(cols, term):
        send_ref[:, cols] = term.astype(jnp.bfloat16)

    mass = weighted_sums(chunk, factor, docs_ref, part_ref, resp_ref, store)
    send_ref[:, docs_ref.shape[1]:] = mass_lanes(mass)


def keep_kernel(chunk, factor_ref, docs_ref, part_ref, keep_ref, keep_mass_ref, resp_ref):
    def store(cols, term):
        keep_ref[:, cols] = term

    mass = weighted_sums(chunk, factor_ref[...], docs_ref, part_ref, resp_ref, store)
    keep_mass_ref[...] = jnp.broadcast_to(mass, keep_mass_ref.shape)


def fold_kernel(keep_ref, keep_mass_ref, got_ref, own_ref, own_mass_ref, *send_refs):
    rows, width = own_ref.shape
    for slot in range(keep_ref.shape[0] // rows):
        here = slice(slot * rows, (slot + 1) * rows)
        got, got_mass = read_rows(got_ref[here], width)
        term = keep_ref[here] + got
        mass = keep_mass_ref[here, :1] + got_mass
        if slot == 0:
            own_ref[...] = term
            own_mass_ref[...] = jnp.broadcast_to(mass, own_mass_ref.shape)
        else:
            send_refs[slot - 1][:, :width] = term.astype(jnp.bfloat16)
            send_refs[slot - 1][:, width:] = mass_lanes(mass)


def final_kernel(own_ref, own_mass_ref, cent_ref, *refs):
    *got_refs, next_ref, mass_ref = refs
    width = own_ref.shape[1]
    got = [read_rows(r[...], width) for r in got_refs]
    term = tree([own_ref[...]] + [a for a, _ in got], jnp.add)
    mass = tree([own_mass_ref[:, :1]] + [b for _, b in got], jnp.add)
    next_ref[...] = (term + cent_ref[...]) / (mass + 1.0)
    mass_ref[...] = jnp.broadcast_to(mass, (mass.shape[0], LANES)).T[:1]


def shape(dims, dtype=jnp.float32):
    return jax.ShapeDtypeStruct(dims, dtype)


def make_body(n, g):
    def body(docs, centroids):
        rows, width = centroids.shape
        count = docs.shape[0]
        half = rows * n // 2
        chunk = 256
        plan = group_plan(g)
        limit = (4 << 20) + half * (48 << 10)

        def call(kernel, outs, *args, scratch=(), flops=0):
            nbytes = sum(x.nbytes for x in args)
            return pl.pallas_call(
                kernel,
                out_shape=outs,
                in_specs=[SMEM if x.dtype == jnp.int32 else VMEM for x in args],
                out_specs=[VMEM] * len(outs),
                scratch_shapes=scratch,
                compiler_params=pltpu.CompilerParams(vmem_limit_bytes=limit),
                cost_estimate=pl.CostEstimate(
                    flops=flops, bytes_accessed=nbytes, transcendentals=0
                ),
            )(*args)

        flops = 2 * half * count * width
        stats = [shape((half, count)), shape((1, count)), shape((1, count))]
        resp = [pltpu.VMEM((half, count), jnp.bfloat16)]
        rounded = centroids.astype(jnp.bfloat16)
        blocks = [swap(rounded, "dev", n, m) for m in range(2, n, 2)]
        docs, own = load(docs, rounded)
        mine = jnp.concatenate([own] + blocks, axis=0)
        theirs = swap(mine, "dev", n, 1)
        part, top, total = call(
            functools.partial(scores_kernel, 2 * chunk), stats, docs, mine, flops=flops
        )
        other_part, other_top, lse = call(
            functools.partial(last_scores_kernel, 2 * chunk), stats,
            docs, theirs, top, total, flops=flops,
        )
        others = [lax.ppermute(lse, "cgrp", pairs) for pairs in plan]
        doc_lse, factor, send = call(
            functools.partial(send_kernel, g, plan, chunk),
            [shape((1, count)), shape((1, count)), shape((half, width + LANES), jnp.bfloat16)],
            lax.axis_index("cgrp").reshape(1), lse, *others, docs, other_part, other_top, top,
            scratch=resp, flops=flops,
        )
        got = swap(send, "dev", n, 1)
        keep, keep_mass = call(
            functools.partial(keep_kernel, chunk),
            [shape((half, width)), shape((half, LANES))],
            factor, docs, part, scratch=resp, flops=flops,
        )
        own, own_mass, *sends = call(
            fold_kernel,
            [shape((rows, width)), shape((rows, LANES))]
            + [shape((rows, width + LANES), jnp.bfloat16)] * (n // 2 - 1),
            keep, keep_mass, got,
        )
        far_first = sorted(range(1, n // 2), key=lambda j: (-j.bit_count(), j))
        arrived = [swap(sends[j - 1], "dev", n, 2 * j) for j in far_first]
        result, mass = call(
            final_kernel, [shape((rows, width)), shape((1, rows))],
            own, own_mass, centroids, *arrived,
        )
        return (result, mass.reshape(rows), doc_lse.reshape(count))

    return body


def solution(mesh):
    in_specs = (P("dev", None), P(("cgrp", "dev"), None))
    out_specs = (P(("cgrp", "dev"), None), P(("cgrp", "dev")), P("dev"))
    return jax.shard_map(
        make_body(mesh.shape["dev"], mesh.shape["cgrp"]),
        mesh=mesh, in_specs=in_specs, out_specs=out_specs, check_vma=False,
    )
```

```python
import functools
import math

import jax
import jax.numpy as jnp
from jax import lax
from jax.experimental import pallas as pl
from jax.experimental.pallas import tpu as pltpu
from jax.sharding import PartitionSpec as P

LANES = 128
VMEM = pl.BlockSpec(memory_space=pltpu.VMEM)
SMEM = pl.BlockSpec(memory_space=pltpu.SMEM)


def swap(x, axis, size, mask):
    return lax.ppermute(x, axis, [(i, i ^ mask) for i in range(size)])


def group_plan(g):
    if g == 4:
        return [
            [(0, 1), (1, 0), (2, 3), (3, 2)],
            [(0, 3), (1, 2), (2, 0), (3, 1)],
            [(0, 2), (1, 3), (2, 1), (3, 0)],
        ]
    return [[(i, i ^ m) for i in range(g)] for m in range(1, g)]


def tree(parts, op):
    while len(parts) > 1:
        parts = [op(parts[i], parts[i + 1]) for i in range(0, len(parts), 2)]
    return parts[0]


def transpose_kernel(chunk, source_ref, follow_ref, docs_ref, own_ref, landing, sems):
    copies = []
    for i, start in enumerate(range(0, source_ref.shape[0], chunk)):
        here = pl.ds(start, chunk)
        copies.append(pltpu.make_async_copy(source_ref.at[here], landing.at[here], sems.at[i]))
        copies[-1].start()
    own_ref[...] = follow_ref[...]
    for i, copy in enumerate(copies):
        copy.wait()
        here = slice(i * chunk, (i + 1) * chunk)
        docs_ref[:, here] = landing[here, :].T


def load_kernel(source_ref, follow_ref, docs_ref, own_ref, sem):
    copy = pltpu.make_async_copy(source_ref, docs_ref, sem)
    copy.start()
    own_ref[...] = follow_ref[...]
    copy.wait()


def load(source, follow, chunk=0):
    count, width = source.shape
    kernel, dims, scratch = load_kernel, (count, width), [pltpu.SemaphoreType.DMA]
    if chunk:
        kernel, dims = functools.partial(transpose_kernel, chunk), (width, count)
        scratch = [
            pltpu.VMEM((count, width), source.dtype),
            pltpu.SemaphoreType.DMA((count // chunk,)),
        ]
    return pl.pallas_call(
        kernel,
        out_shape=[shape(dims, source.dtype), shape(follow.shape, follow.dtype)],
        in_specs=[pl.BlockSpec(memory_space=pltpu.HBM), VMEM],
        out_specs=[VMEM, VMEM],
        scratch_shapes=scratch,
        compiler_params=pltpu.CompilerParams(
            vmem_limit_bytes=(4 << 20) + (2 * source.nbytes if chunk else 0)
        ),
        cost_estimate=pl.CostEstimate(
            flops=0, bytes_accessed=2 * source.nbytes, transcendentals=0
        ),
    )(pltpu.with_memory_space_constraint(source, pltpu.HBM), follow)


def scores_kernel(chunk, docs_ref, table_ref, part_ref, top_ref, sum_ref):
    width, count = docs_ref.shape
    scale = 4.0 / math.sqrt(width)
    table = table_ref[...]
    wide = table.astype(jnp.float32)
    half_norms = 0.5 * jnp.sum(wide * wide, axis=1, keepdims=True)
    for start in range(0, count, chunk):
        cols = slice(start, start + chunk)
        dots = jnp.dot(table, docs_ref[:, cols], preferred_element_type=jnp.float32)
        scores = (dots - half_norms) * scale
        top = jnp.max(scores, axis=0, keepdims=True)
        part = jnp.exp(scores - top)
        part_ref[:, cols] = part
        top_ref[:, cols] = top
        sum_ref[:, cols] = jnp.sum(part, axis=0, keepdims=True)


def last_scores_kernel(
    chunk, docs_ref, table_ref, first_top_ref, first_sum_ref, part_ref, top_ref, lse_ref
):
    scores_kernel(chunk, docs_ref, table_ref, part_ref, top_ref, lse_ref)
    top = jnp.maximum(first_top_ref[...], top_ref[...])
    total = first_sum_ref[...] * jnp.exp(first_top_ref[...] - top)
    total += lse_ref[...] * jnp.exp(top_ref[...] - top)
    lse_ref[...] = top + jnp.log(total)


def weighted_sums(chunk, factor, docs_ref, part_ref, resp_ref, store):
    rows, count = part_ref.shape
    mass = jnp.zeros((rows, 1), jnp.float32)
    for start in range(0, count, chunk):
        cols = slice(start, start + chunk)
        resp = part_ref[:, cols] * factor[:, cols]
        mass += jnp.sum(resp, axis=1, keepdims=True)
        resp_ref[:, cols] = resp.astype(jnp.bfloat16)
    for start in range(0, docs_ref.shape[1], chunk):
        cols = slice(start, start + chunk)
        store(cols, jnp.dot(resp_ref[...], docs_ref[:, cols], preferred_element_type=jnp.float32))
    return mass


def mass_lanes(mass):
    high = mass.astype(jnp.bfloat16).astype(jnp.float32)
    lane = lax.broadcasted_iota(jnp.int32, (mass.shape[0], LANES), 1)
    lanes = jnp.where(lane == 0, high, jnp.where(lane == 1, mass - high, 0.0))
    return lanes.astype(jnp.bfloat16)


def read_rows(rows, width):
    wide = rows.astype(jnp.float32)
    return wide[:, :width], wide[:, width:width + 1] + wide[:, width + 1:width + 2]


def send_kernel(groups, plan, chunk, me_ref, lse_ref, *refs):
    got_refs = refs[:len(plan)]
    docs_ref, part_ref, top_ref, keep_top_ref = refs[len(plan):len(plan) + 4]
    doc_lse_ref, factor_ref, send_ref, resp_ref = refs[len(plan) + 4:]
    me = me_ref[0]
    parts = [lse_ref[...]] * groups
    for got_ref, pairs in zip(got_refs, plan):
        got = got_ref[...]
        for source, target in pairs:
            parts[source] = jnp.where(me == target, got, parts[source])
    best = tree(parts, jnp.maximum)
    doc_lse = best + jnp.log(tree([jnp.exp(x - best) for x in parts], jnp.add))
    doc_lse_ref[...] = doc_lse
    factor_ref[...] = jnp.exp(keep_top_ref[...] - doc_lse)
    factor = jnp.exp(top_ref[...] - doc_lse)

    def store(cols, term):
        send_ref[:, cols] = term.astype(jnp.bfloat16)

    mass = weighted_sums(chunk, factor, docs_ref, part_ref, resp_ref, store)
    send_ref[:, docs_ref.shape[1]:] = mass_lanes(mass)


def keep_kernel(chunk, factor_ref, docs_ref, part_ref, keep_ref, keep_mass_ref, resp_ref):
    def store(cols, term):
        keep_ref[:, cols] = term

    mass = weighted_sums(chunk, factor_ref[...], docs_ref, part_ref, resp_ref, store)
    keep_mass_ref[...] = jnp.broadcast_to(mass, keep_mass_ref.shape)


def fold_kernel(keep_ref, keep_mass_ref, got_ref, own_ref, own_mass_ref, *send_refs):
    rows, width = own_ref.shape
    for slot in range(keep_ref.shape[0] // rows):
        here = slice(slot * rows, (slot + 1) * rows)
        got, got_mass = read_rows(got_ref[here], width)
        term = keep_ref[here] + got
        mass = keep_mass_ref[here, :1] + got_mass
        if slot == 0:
            own_ref[...] = term
            own_mass_ref[...] = jnp.broadcast_to(mass, own_mass_ref.shape)
        else:
            send_refs[slot - 1][:, :width] = term.astype(jnp.bfloat16)
            send_refs[slot - 1][:, width:] = mass_lanes(mass)


def final_kernel(own_ref, own_mass_ref, cent_ref, *refs):
    *got_refs, next_ref, mass_ref = refs
    width = own_ref.shape[1]
    got = [read_rows(r[...], width) for r in got_refs]
    term = tree([own_ref[...]] + [a for a, _ in got], jnp.add)
    mass = tree([own_mass_ref[:, :1]] + [b for _, b in got], jnp.add)
    next_ref[...] = (term + cent_ref[...]) / (mass + 1.0)
    mass_ref[...] = jnp.broadcast_to(mass, (mass.shape[0], LANES)).T[:1]


def shape(dims, dtype=jnp.float32):
    return jax.ShapeDtypeStruct(dims, dtype)


def make_body(n, g):
    def body(docs, centroids):
        rows, width = centroids.shape
        count = docs.shape[0]
        half = rows * n // 2
        chunk = 256
        plan = group_plan(g)
        limit = (4 << 20) + half * (48 << 10)

        def call(kernel, outs, *args, scratch=(), flops=0):
            nbytes = sum(x.nbytes for x in args)
            return pl.pallas_call(
                kernel,
                out_shape=outs,
                in_specs=[SMEM if x.dtype == jnp.int32 else VMEM for x in args],
                out_specs=[VMEM] * len(outs),
                scratch_shapes=scratch,
                compiler_params=pltpu.CompilerParams(vmem_limit_bytes=limit),
                cost_estimate=pl.CostEstimate(
                    flops=flops, bytes_accessed=nbytes, transcendentals=0
                ),
            )(*args)

        flops = 2 * half * count * width
        stats = [shape((half, count)), shape((1, count)), shape((1, count))]
        resp = [pltpu.VMEM((half, count), jnp.bfloat16)]
        rounded = centroids.astype(jnp.bfloat16)
        blocks = [swap(rounded, "dev", n, m) for m in range(2, n, 2)]
        docs_t, own = load(docs, rounded, chunk)
        mine = jnp.concatenate([own] + blocks, axis=0)
        theirs = swap(mine, "dev", n, 1)
        part, top, total = call(
            functools.partial(scores_kernel, chunk), stats, docs_t, mine, flops=flops
        )
        other_part, other_top, lse = call(
            functools.partial(last_scores_kernel, chunk), stats,
            docs_t, theirs, top, total, flops=flops,
        )
        others = [lax.ppermute(lse, "cgrp", pairs) for pairs in plan]
        docs, lse = load(docs, lse)
        doc_lse, factor, send = call(
            functools.partial(send_kernel, g, plan, chunk),
            [shape((1, count)), shape((1, count)), shape((half, width + LANES), jnp.bfloat16)],
            lax.axis_index("cgrp").reshape(1), lse, *others, docs, other_part, other_top, top,
            scratch=resp, flops=flops,
        )
        got = swap(send, "dev", n, 1)
        keep, keep_mass = call(
            functools.partial(keep_kernel, chunk),
            [shape((half, width)), shape((half, LANES))],
            factor, docs, part, scratch=resp, flops=flops,
        )
        own, own_mass, *sends = call(
            fold_kernel,
            [shape((rows, width)), shape((rows, LANES))]
            + [shape((rows, width + LANES), jnp.bfloat16)] * (n // 2 - 1),
            keep, keep_mass, got,
        )
        far_first = sorted(range(1, n // 2), key=lambda j: (-j.bit_count(), j))
        arrived = [swap(sends[j - 1], "dev", n, 2 * j) for j in far_first]
        result, mass = call(
            final_kernel, [shape((rows, width)), shape((1, rows))],
            own, own_mass, centroids, *arrived,
        )
        return (result, mass.reshape(rows), doc_lse.reshape(count))

    return body


def solution(mesh):
    in_specs = (P("dev", None), P(("cgrp", "dev"), None))
    out_specs = (P(("cgrp", "dev"), None), P(("cgrp", "dev")), P("dev"))
    return jax.shard_map(
        make_body(mesh.shape["dev"], mesh.shape["cgrp"]),
        mesh=mesh, in_specs=in_specs, out_specs=out_specs, check_vma=False,
    )
```

```python
import functools
import math

import jax
import jax.numpy as jnp
from jax import lax
from jax.experimental import pallas as pl
from jax.experimental.pallas import tpu as pltpu
from jax.sharding import PartitionSpec as P

LANES = 128
VMEM = pl.BlockSpec(memory_space=pltpu.VMEM)
SMEM = pl.BlockSpec(memory_space=pltpu.SMEM)


def swap(x, axis, size, mask):
    return lax.ppermute(x, axis, [(i, i ^ mask) for i in range(size)])


def group_plan(g):
    if g == 4:
        return [
            [(0, 1), (1, 0), (2, 3), (3, 2)],
            [(0, 3), (1, 2), (2, 0), (3, 1)],
            [(0, 2), (1, 3), (2, 1), (3, 0)],
        ]
    return [[(i, i ^ m) for i in range(g)] for m in range(1, g)]


def tree(parts, op):
    while len(parts) > 1:
        parts = [op(parts[i], parts[i + 1]) for i in range(0, len(parts), 2)]
    return parts[0]


def round_kernel(source_ref, out_ref, landing, sem):
    copy = pltpu.make_async_copy(source_ref, landing, sem)
    copy.start()
    copy.wait()
    out_ref[...] = landing[...].astype(out_ref.dtype)


def round_rows(x):
    return pl.pallas_call(
        round_kernel,
        out_shape=shape(x.shape, jnp.bfloat16),
        in_specs=[pl.BlockSpec(memory_space=pltpu.HBM)],
        out_specs=VMEM,
        scratch_shapes=[pltpu.VMEM(x.shape, x.dtype), pltpu.SemaphoreType.DMA],
    )(pltpu.with_memory_space_constraint(x, pltpu.HBM))


def transpose_kernel(chunk, source_ref, follow_ref, docs_ref, own_ref, landing, sems):
    copies = []
    for i, start in enumerate(range(0, source_ref.shape[0], chunk)):
        here = pl.ds(start, chunk)
        copies.append(pltpu.make_async_copy(source_ref.at[here], landing.at[here], sems.at[i]))
        copies[-1].start()
    own_ref[...] = follow_ref[...]
    for i, copy in enumerate(copies):
        copy.wait()
        here = slice(i * chunk, (i + 1) * chunk)
        docs_ref[:, here] = landing[here, :].T


def load_kernel(source_ref, follow_ref, docs_ref, own_ref, sem):
    copy = pltpu.make_async_copy(source_ref, docs_ref, sem)
    copy.start()
    own_ref[...] = follow_ref[...]
    copy.wait()


def load(source, follow, chunk=0):
    count, width = source.shape
    kernel, dims, scratch = load_kernel, (count, width), [pltpu.SemaphoreType.DMA]
    if chunk:
        kernel, dims = functools.partial(transpose_kernel, chunk), (width, count)
        scratch = [
            pltpu.VMEM((count, width), source.dtype),
            pltpu.SemaphoreType.DMA((count // chunk,)),
        ]
    return pl.pallas_call(
        kernel,
        out_shape=[shape(dims, source.dtype), shape(follow.shape, follow.dtype)],
        in_specs=[pl.BlockSpec(memory_space=pltpu.HBM), VMEM],
        out_specs=[VMEM, VMEM],
        scratch_shapes=scratch,
        compiler_params=pltpu.CompilerParams(
            vmem_limit_bytes=(4 << 20) + (2 * source.nbytes if chunk else 0)
        ),
        cost_estimate=pl.CostEstimate(
            flops=0, bytes_accessed=2 * source.nbytes, transcendentals=0
        ),
    )(pltpu.with_memory_space_constraint(source, pltpu.HBM), follow)


def scores_kernel(chunk, docs_ref, table_ref, part_ref, top_ref, sum_ref):
    width, count = docs_ref.shape
    scale = 4.0 / math.sqrt(width)
    table = table_ref[...]
    wide = table.astype(jnp.float32)
    half_norms = 0.5 * jnp.sum(wide * wide, axis=1, keepdims=True)
    for start in range(0, count, chunk):
        cols = slice(start, start + chunk)
        dots = jnp.dot(table, docs_ref[:, cols], preferred_element_type=jnp.float32)
        scores = (dots - half_norms) * scale
        top = jnp.max(scores, axis=0, keepdims=True)
        part = jnp.exp(scores - top)
        part_ref[:, cols] = part
        top_ref[:, cols] = top
        sum_ref[:, cols] = jnp.sum(part, axis=0, keepdims=True)


def last_scores_kernel(
    chunk, docs_ref, table_ref, first_top_ref, first_sum_ref, part_ref, top_ref, lse_ref
):
    scores_kernel(chunk, docs_ref, table_ref, part_ref, top_ref, lse_ref)
    top = jnp.maximum(first_top_ref[...], top_ref[...])
    total = first_sum_ref[...] * jnp.exp(first_top_ref[...] - top)
    total += lse_ref[...] * jnp.exp(top_ref[...] - top)
    lse_ref[...] = top + jnp.log(total)


def weighted_sums(chunk, pieces, docs_ref, resp_ref, store):
    masses, at = [], 0
    for part_ref, here, factor in pieces:
        rows = here.stop - here.start
        mass = jnp.zeros((rows, 1), jnp.float32)
        for start in range(0, part_ref.shape[1], chunk):
            cols = slice(start, start + chunk)
            resp = part_ref[here, cols] * factor[:, cols]
            mass += jnp.sum(resp, axis=1, keepdims=True)
            resp_ref[at:at + rows, cols] = resp.astype(jnp.bfloat16)
        masses.append(mass)
        at += rows
    for start in range(0, docs_ref.shape[1], chunk):
        cols = slice(start, start + chunk)
        store(cols, jnp.dot(resp_ref[...], docs_ref[:, cols], preferred_element_type=jnp.float32))
    return jnp.concatenate(masses, axis=0)


def mass_lanes(mass):
    high = mass.astype(jnp.bfloat16).astype(jnp.float32)
    lane = lax.broadcasted_iota(jnp.int32, (mass.shape[0], LANES), 1)
    lanes = jnp.where(lane == 0, high, jnp.where(lane == 1, mass - high, 0.0))
    return lanes.astype(jnp.bfloat16)


def read_rows(rows, width):
    wide = rows.astype(jnp.float32)
    return wide[:, :width], wide[:, width:width + 1] + wide[:, width + 1:width + 2]


def send_kernel(groups, plan, chunk, me_ref, lse_ref, *refs):
    got_refs = refs[:len(plan)]
    docs_ref, part_ref, top_ref, keep_part_ref, keep_top_ref = refs[len(plan):len(plan) + 5]
    doc_lse_ref, factor_ref, send_ref, resp_ref = refs[len(plan) + 5:]
    me = me_ref[0]
    parts = [lse_ref[...]] * groups
    for got_ref, pairs in zip(got_refs, plan):
        got = got_ref[...]
        for source, target in pairs:
            parts[source] = jnp.where(me == target, got, parts[source])
    best = tree(parts, jnp.maximum)
    doc_lse = best + jnp.log(tree([jnp.exp(x - best) for x in parts], jnp.add))
    doc_lse_ref[...] = doc_lse
    keep_factor = jnp.exp(keep_top_ref[...] - doc_lse)
    factor_ref[...] = keep_factor

    def store(cols, term):
        send_ref[:, cols] = term.astype(jnp.bfloat16)

    half, rows = part_ref.shape[0], send_ref.shape[0] - part_ref.shape[0]
    pieces = [
        (part_ref, slice(0, half), jnp.exp(top_ref[...] - doc_lse)),
        (keep_part_ref, slice(half - rows, half), keep_factor),
    ]
    mass = weighted_sums(chunk, pieces, docs_ref, resp_ref, store)
    send_ref[:, docs_ref.shape[1]:] = mass_lanes(mass)


def keep_kernel(chunk, factor_ref, docs_ref, part_ref, keep_ref, keep_mass_ref, resp_ref):
    def store(cols, term):
        keep_ref[:, cols] = term

    pieces = [(part_ref, slice(0, keep_ref.shape[0]), factor_ref[...])]
    mass = weighted_sums(chunk, pieces, docs_ref, resp_ref, store)
    keep_mass_ref[...] = jnp.broadcast_to(mass, keep_mass_ref.shape)


def fold_kernel(keep_ref, keep_mass_ref, sent_ref, got_ref, own_ref, own_mass_ref, *send_refs):
    rows, width = own_ref.shape
    *near_refs, far_ref = send_refs
    last = len(near_refs) + 1

    def slot(ref, i):
        return read_rows(ref[i * rows:(i + 1) * rows], width)

    for i in range(last):
        here = slice(i * rows, (i + 1) * rows)
        got, got_mass = slot(got_ref, i)
        term = keep_ref[here] + got
        mass = keep_mass_ref[here, :1] + got_mass
        if i == 0:
            own_ref[...] = term
            own_mass_ref[...] = jnp.broadcast_to(mass, own_mass_ref.shape)
        else:
            near_refs[i - 1][:, :width] = term.astype(jnp.bfloat16)
            near_refs[i - 1][:, width:] = mass_lanes(mass)
    for i, (mine, theirs) in enumerate(((last + 1, last), (last, last + 1))):
        here = slice(i * rows, (i + 1) * rows)
        (a, a_mass), (b, b_mass) = slot(sent_ref, mine), slot(got_ref, theirs)
        far_ref[here, :width] = (a + b).astype(jnp.bfloat16)
        far_ref[here, width:] = mass_lanes(a_mass + b_mass)


def final_kernel(odd_ref, own_ref, own_mass_ref, cent_ref, far_ref, passed_ref, *refs):
    *near_refs, next_ref, mass_ref = refs
    rows, width = own_ref.shape
    far = jnp.where(odd_ref[0] == 1, far_ref[:rows], passed_ref[...])
    got = [read_rows(x, width) for x in [r[...] for r in near_refs] + [far]]
    term = tree([own_ref[...]] + [a for a, _ in got], jnp.add)
    mass = tree([own_mass_ref[:, :1]] + [b for _, b in got], jnp.add)
    next_ref[...] = (term + cent_ref[...]) / (mass + 1.0)
    mass_ref[...] = jnp.broadcast_to(mass, (mass.shape[0], LANES)).T[:1]


def shape(dims, dtype=jnp.float32):
    return jax.ShapeDtypeStruct(dims, dtype)


def make_body(n, g):
    def body(docs, centroids):
        rows, width = centroids.shape
        count = docs.shape[0]
        half = rows * n // 2
        chunk = 256
        plan = group_plan(g)
        limit = (4 << 20) + half * (48 << 10)

        def call(kernel, outs, *args, scratch=(), flops=0):
            nbytes = sum(x.nbytes for x in args)
            return pl.pallas_call(
                kernel,
                out_shape=outs,
                in_specs=[SMEM if x.dtype == jnp.int32 else VMEM for x in args],
                out_specs=[VMEM] * len(outs),
                scratch_shapes=scratch,
                compiler_params=pltpu.CompilerParams(vmem_limit_bytes=limit),
                cost_estimate=pl.CostEstimate(
                    flops=flops, bytes_accessed=nbytes, transcendentals=0
                ),
            )(*args)

        flops = 2 * half * count * width
        stats = [shape((half, count)), shape((1, count)), shape((1, count))]
        rounded = round_rows(centroids)
        blocks = [swap(rounded, "dev", n, m) for m in range(2, n, 2)]
        docs_t, own = load(docs, rounded, chunk)
        mine = jnp.concatenate([own] + blocks, axis=0)
        theirs = swap(mine, "dev", n, 1)
        part, top, total = call(
            functools.partial(scores_kernel, chunk), stats, docs_t, mine, flops=flops
        )
        other_part, other_top, lse = call(
            functools.partial(last_scores_kernel, chunk), stats,
            docs_t, theirs, top, total, flops=flops,
        )
        others = [lax.ppermute(lse, "cgrp", pairs) for pairs in plan]
        docs, lse = load(docs, lse)
        sent = half + rows
        doc_lse, factor, send = call(
            functools.partial(send_kernel, g, plan, chunk),
            [shape((1, count)), shape((1, count)), shape((sent, width + LANES), jnp.bfloat16)],
            lax.axis_index("cgrp").reshape(1), lse, *others,
            docs, other_part, other_top, part, top,
            scratch=[pltpu.VMEM((sent, count), jnp.bfloat16)], flops=flops,
        )
        got = swap(send, "dev", n, 1)
        kept = half - rows
        keep, keep_mass = call(
            functools.partial(keep_kernel, chunk),
            [shape((kept, width)), shape((kept, LANES))],
            factor, docs, part,
            scratch=[pltpu.VMEM((kept, count), jnp.bfloat16)], flops=flops,
        )
        own, own_mass, *sends, far = call(
            fold_kernel,
            [shape((rows, width)), shape((rows, LANES))]
            + [shape((rows, width + LANES), jnp.bfloat16)] * (n // 2 - 2)
            + [shape((2 * rows, width + LANES), jnp.bfloat16)],
            keep, keep_mass, send, got,
        )
        far = lax.ppermute(far, "dev", [(i, i ^ (n - 2)) for i in range(1, n, 2)])
        passed = swap(far[rows:], "dev", n, 1)
        arrived = [swap(x, "dev", n, 2 * (j + 1)) for j, x in enumerate(sends)]
        result, mass = call(
            final_kernel, [shape((rows, width)), shape((1, rows))],
            (lax.axis_index("dev") % 2).reshape(1),
            own, own_mass, centroids, far, passed, *arrived,
        )
        return (result, mass.reshape(rows), doc_lse.reshape(count))

    return body


def solution(mesh):
    in_specs = (P("dev", None), P(("cgrp", "dev"), None))
    out_specs = (P(("cgrp", "dev"), None), P(("cgrp", "dev")), P("dev"))
    return jax.shard_map(
        make_body(mesh.shape["dev"], mesh.shape["cgrp"]),
        mesh=mesh, in_specs=in_specs, out_specs=out_specs, check_vma=False,
    )
```

```python
import functools
import math

import jax
import jax.numpy as jnp
from jax import lax
from jax.experimental import pallas as pl
from jax.experimental.pallas import tpu as pltpu
from jax.sharding import PartitionSpec as P

LANES = 128
VMEM = pl.BlockSpec(memory_space=pltpu.VMEM)
SMEM = pl.BlockSpec(memory_space=pltpu.SMEM)


def swap(x, axis, size, mask):
    return lax.ppermute(x, axis, [(i, i ^ mask) for i in range(size)])


def group_plan(g):
    if g == 4:
        return [
            [(0, 1), (1, 0), (2, 3), (3, 2)],
            [(0, 3), (1, 2), (2, 0), (3, 1)],
            [(0, 2), (1, 3), (2, 1), (3, 0)],
        ]
    return [[(i, i ^ m) for i in range(g)] for m in range(1, g)]


def tree(parts, op):
    while len(parts) > 1:
        parts = [op(parts[i], parts[i + 1]) for i in range(0, len(parts), 2)]
    return parts[0]


def transpose_kernel(chunk, source_ref, follow_ref, docs_ref, own_ref, landing, sems):
    copies = []
    for i, start in enumerate(range(0, source_ref.shape[0], chunk)):
        here = pl.ds(start, chunk)
        copies.append(pltpu.make_async_copy(source_ref.at[here], landing.at[here], sems.at[i]))
        copies[-1].start()
    own_ref[...] = follow_ref[...]
    for i, copy in enumerate(copies):
        copy.wait()
        here = slice(i * chunk, (i + 1) * chunk)
        docs_ref[:, here] = landing[here, :].T


def load_kernel(source_ref, follow_ref, docs_ref, own_ref, sem):
    copy = pltpu.make_async_copy(source_ref, docs_ref, sem)
    copy.start()
    own_ref[...] = follow_ref[...]
    copy.wait()


def load(source, follow, chunk=0):
    count, width = source.shape
    kernel, dims, scratch = load_kernel, (count, width), [pltpu.SemaphoreType.DMA]
    if chunk:
        kernel, dims = functools.partial(transpose_kernel, chunk), (width, count)
        scratch = [
            pltpu.VMEM((count, width), source.dtype),
            pltpu.SemaphoreType.DMA((count // chunk,)),
        ]
    return pl.pallas_call(
        kernel,
        out_shape=[shape(dims, source.dtype), shape(follow.shape, follow.dtype)],
        in_specs=[pl.BlockSpec(memory_space=pltpu.HBM), VMEM],
        out_specs=[VMEM, VMEM],
        scratch_shapes=scratch,
        compiler_params=pltpu.CompilerParams(
            vmem_limit_bytes=(4 << 20) + (2 * source.nbytes if chunk else 0)
        ),
        cost_estimate=pl.CostEstimate(
            flops=0, bytes_accessed=2 * source.nbytes, transcendentals=0
        ),
    )(pltpu.with_memory_space_constraint(source, pltpu.HBM), follow)


def scores_kernel(chunk, docs_ref, table_ref, part_ref, top_ref, sum_ref):
    width, count = docs_ref.shape
    scale = 4.0 / math.sqrt(width)
    table = table_ref[...]
    wide = table.astype(jnp.float32)
    half_norms = 0.5 * jnp.sum(wide * wide, axis=1, keepdims=True)
    for start in range(0, count, chunk):
        cols = slice(start, start + chunk)
        dots = jnp.dot(table, docs_ref[:, cols], preferred_element_type=jnp.float32)
        scores = (dots - half_norms) * scale
        top = jnp.max(scores, axis=0, keepdims=True)
        part = jnp.exp(scores - top)
        part_ref[:, cols] = part
        top_ref[:, cols] = top
        sum_ref[:, cols] = jnp.sum(part, axis=0, keepdims=True)


def last_scores_kernel(
    chunk, docs_ref, table_ref, first_top_ref, first_sum_ref, part_ref, top_ref, lse_ref
):
    scores_kernel(chunk, docs_ref, table_ref, part_ref, top_ref, lse_ref)
    top = jnp.maximum(first_top_ref[...], top_ref[...])
    total = first_sum_ref[...] * jnp.exp(first_top_ref[...] - top)
    total += lse_ref[...] * jnp.exp(top_ref[...] - top)
    lse_ref[...] = top + jnp.log(total)


def weighted_sums(chunk, pieces, docs_ref, resp_ref, store):
    masses, at = [], 0
    for part_ref, here, factor in pieces:
        rows = here.stop - here.start
        mass = jnp.zeros((rows, 1), jnp.float32)
        for start in range(0, part_ref.shape[1], chunk):
            cols = slice(start, start + chunk)
            resp = part_ref[here, cols] * factor[:, cols]
            mass += jnp.sum(resp, axis=1, keepdims=True)
            resp_ref[at:at + rows, cols] = resp.astype(jnp.bfloat16)
        masses.append(mass)
        at += rows
    for start in range(0, docs_ref.shape[1], chunk):
        cols = slice(start, start + chunk)
        store(cols, jnp.dot(resp_ref[...], docs_ref[:, cols], preferred_element_type=jnp.float32))
    return jnp.concatenate(masses, axis=0)


def mass_lanes(mass):
    high = mass.astype(jnp.bfloat16).astype(jnp.float32)
    lane = lax.broadcasted_iota(jnp.int32, (mass.shape[0], LANES), 1)
    lanes = jnp.where(lane == 0, high, jnp.where(lane == 1, mass - high, 0.0))
    return lanes.astype(jnp.bfloat16)


def read_rows(rows, width):
    wide = rows.astype(jnp.float32)
    return wide[:, :width], wide[:, width:width + 1] + wide[:, width + 1:width + 2]


def send_kernel(groups, plan, chunk, me_ref, lse_ref, *refs):
    got_refs = refs[:len(plan)]
    docs_ref, part_ref, top_ref, keep_part_ref, keep_top_ref = refs[len(plan):len(plan) + 5]
    doc_lse_ref, factor_ref, send_ref, resp_ref = refs[len(plan) + 5:]
    me = me_ref[0]
    parts = [lse_ref[...]] * groups
    for got_ref, pairs in zip(got_refs, plan):
        got = got_ref[...]
        for source, target in pairs:
            parts[source] = jnp.where(me == target, got, parts[source])
    best = tree(parts, jnp.maximum)
    doc_lse = best + jnp.log(tree([jnp.exp(x - best) for x in parts], jnp.add))
    doc_lse_ref[...] = doc_lse
    keep_factor = jnp.exp(keep_top_ref[...] - doc_lse)
    factor_ref[...] = keep_factor

    def store(cols, term):
        send_ref[:, cols] = term.astype(jnp.bfloat16)

    half, rows = part_ref.shape[0], send_ref.shape[0] - part_ref.shape[0]
    pieces = [
        (part_ref, slice(0, half), jnp.exp(top_ref[...] - doc_lse)),
        (keep_part_ref, slice(half - rows, half), keep_factor),
    ]
    mass = weighted_sums(chunk, pieces, docs_ref, resp_ref, store)
    send_ref[:, docs_ref.shape[1]:] = mass_lanes(mass)


def keep_kernel(chunk, factor_ref, docs_ref, part_ref, keep_ref, keep_mass_ref, resp_ref):
    def store(cols, term):
        keep_ref[:, cols] = term

    pieces = [(part_ref, slice(0, keep_ref.shape[0]), factor_ref[...])]
    mass = weighted_sums(chunk, pieces, docs_ref, resp_ref, store)
    keep_mass_ref[...] = jnp.broadcast_to(mass, keep_mass_ref.shape)


def scatter_masks(n, core):
    near = list(range(2, n - 2, 2))
    return [n - 2] + near if core else near + [0]


def fold_kernel(
    odd_ref, keep_ref, keep_mass_ref, sent_ref, got_ref, own_ref, own_mass_ref, *send_refs
):
    rows, width = own_ref.shape
    odd = odd_ref[0] == 1
    last = len(send_refs)

    def slot(ref, i):
        return read_rows(ref[i * rows:(i + 1) * rows], width)

    def put(ref, here, term, mass):
        ref[here, :width] = term.astype(jnp.bfloat16)
        ref[here, width:] = mass_lanes(mass)

    near = []
    for i in range(last):
        here = slice(i * rows, (i + 1) * rows)
        got, got_mass = slot(got_ref, i)
        near.append((keep_ref[here] + got, keep_mass_ref[here, :1] + got_mass))
    far = []
    for mine, theirs in ((last + 1, last), (last, last + 1)):
        (a, a_mass), (b, b_mass) = slot(sent_ref, mine), slot(got_ref, theirs)
        far.append((a + b, a_mass + b_mass))
    (own_ref[...], own_mass), *near = near
    own_mass_ref[...] = jnp.broadcast_to(own_mass, own_mass_ref.shape)
    for i, ref in enumerate(send_refs):
        on_odd = near[i - 1] if i else far[0]
        on_even = near[min(i, len(near) - 1)]
        picked = [jnp.where(odd, x, y) for x, y in zip(on_odd, on_even)]
        put(ref, slice(0, rows), *picked)
    put(send_refs[0], slice(rows, 2 * rows), *far[1])


def final_kernel(odd_ref, own_ref, own_mass_ref, cent_ref, passed_ref, *refs):
    *got_refs, next_ref, mass_ref = refs
    rows, width = own_ref.shape
    got = [r[:rows] for r in got_refs]
    got[-1] = jnp.where(odd_ref[0] == 1, got[-1], passed_ref[...])
    got = [read_rows(x, width) for x in got]
    term = tree([own_ref[...]] + [a for a, _ in got], jnp.add)
    mass = tree([own_mass_ref[:, :1]] + [b for _, b in got], jnp.add)
    next_ref[...] = (term + cent_ref[...]) / (mass + 1.0)
    mass_ref[...] = jnp.broadcast_to(mass, (mass.shape[0], LANES)).T[:1]


def shape(dims, dtype=jnp.float32):
    return jax.ShapeDtypeStruct(dims, dtype)


def make_body(n, g):
    def body(docs, centroids):
        rows, width = centroids.shape
        count = docs.shape[0]
        half = rows * n // 2
        chunk = 256
        plan = group_plan(g)
        limit = (4 << 20) + half * (48 << 10)

        def call(kernel, outs, *args, scratch=(), flops=0):
            nbytes = sum(x.nbytes for x in args)
            return pl.pallas_call(
                kernel,
                out_shape=outs,
                in_specs=[SMEM if x.dtype == jnp.int32 else VMEM for x in args],
                out_specs=[VMEM] * len(outs),
                scratch_shapes=scratch,
                compiler_params=pltpu.CompilerParams(vmem_limit_bytes=limit),
                cost_estimate=pl.CostEstimate(
                    flops=flops, bytes_accessed=nbytes, transcendentals=0
                ),
            )(*args)

        flops = 2 * half * count * width
        stats = [shape((half, count)), shape((1, count)), shape((1, count))]
        rounded = centroids.astype(jnp.bfloat16)
        blocks = [swap(rounded, "dev", n, m) for m in range(2, n, 2)]
        docs_t, own = load(docs, rounded, chunk)
        mine = jnp.concatenate([own] + blocks, axis=0)
        theirs = swap(mine, "dev", n, 1)
        part, top, total = call(
            functools.partial(scores_kernel, chunk), stats, docs_t, mine, flops=flops
        )
        other_part, other_top, lse = call(
            functools.partial(last_scores_kernel, chunk), stats,
            docs_t, theirs, top, total, flops=flops,
        )
        others = [lax.ppermute(lse, "cgrp", pairs) for pairs in plan]
        docs, lse = load(docs, lse)
        sent = half + rows
        doc_lse, factor, send = call(
            functools.partial(send_kernel, g, plan, chunk),
            [shape((1, count)), shape((1, count)), shape((sent, width + LANES), jnp.bfloat16)],
            lax.axis_index("cgrp").reshape(1), lse, *others,
            docs, other_part, other_top, part, top,
            scratch=[pltpu.VMEM((sent, count), jnp.bfloat16)], flops=flops,
        )
        got = swap(send, "dev", n, 1)
        kept = half - rows
        keep, keep_mass = call(
            functools.partial(keep_kernel, chunk),
            [shape((kept, width)), shape((kept, LANES))],
            factor, docs, part,
            scratch=[pltpu.VMEM((kept, count), jnp.bfloat16)], flops=flops,
        )
        odd = (lax.axis_index("dev") % 2).reshape(1)
        own, own_mass, *sends = call(
            fold_kernel,
            [shape((rows, width)), shape((rows, LANES)),
             shape((2 * rows, width + LANES), jnp.bfloat16)]
            + [shape((rows, width + LANES), jnp.bfloat16)] * (n // 2 - 2),
            odd, keep, keep_mass, send, got,
        )
        masks = list(zip(scatter_masks(n, 0), scatter_masks(n, 1)))
        arrived = [
            lax.ppermute(x, "dev", [(i, i ^ pair[i % 2]) for i in range(n)])
            for x, pair in zip(sends, masks)
        ]
        passed = swap(arrived[0][rows:], "dev", n, 1)
        result, mass = call(
            final_kernel, [shape((rows, width)), shape((1, rows))],
            odd, own, own_mass, centroids, passed, *arrived,
        )
        return (result, mass.reshape(rows), doc_lse.reshape(count))

    return body


def solution(mesh):
    in_specs = (P("dev", None), P(("cgrp", "dev"), None))
    out_specs = (P(("cgrp", "dev"), None), P(("cgrp", "dev")), P("dev"))
    return jax.shard_map(
        make_body(mesh.shape["dev"], mesh.shape["cgrp"]),
        mesh=mesh, in_specs=in_specs, out_specs=out_specs, check_vma=False,
    )
```

```python
import functools
import math

import jax
import jax.numpy as jnp
from jax import lax
from jax.experimental import pallas as pl
from jax.experimental.pallas import tpu as pltpu
from jax.sharding import PartitionSpec as P

LANES = 128
VMEM = pl.BlockSpec(memory_space=pltpu.VMEM)
SMEM = pl.BlockSpec(memory_space=pltpu.SMEM)


def swap(x, axis, size, mask):
    return lax.ppermute(x, axis, [(i, i ^ mask) for i in range(size)])


def group_plan(g):
    if g == 4:
        return [
            [(0, 2), (1, 0), (2, 3), (3, 1)],
            [(0, 3), (1, 2), (2, 1), (3, 0)],
            [(0, 1), (1, 3), (2, 0), (3, 2)],
        ]
    return [[(i, i ^ m) for i in range(g)] for m in range(1, g)]


def tree(parts, op):
    while len(parts) > 1:
        parts = [op(parts[i], parts[i + 1]) for i in range(0, len(parts), 2)]
    return parts[0]


def transpose_kernel(chunk, source_ref, follow_ref, docs_ref, own_ref, landing, sems):
    copies = []
    for i, start in enumerate(range(0, source_ref.shape[0], chunk)):
        here = pl.ds(start, chunk)
        copies.append(pltpu.make_async_copy(source_ref.at[here], landing.at[here], sems.at[i]))
        copies[-1].start()
    own_ref[...] = follow_ref[...]
    for i, copy in enumerate(copies):
        copy.wait()
        here = slice(i * chunk, (i + 1) * chunk)
        docs_ref[:, here] = landing[here, :].T


def load_kernel(source_ref, follow_ref, docs_ref, own_ref, sem):
    copy = pltpu.make_async_copy(source_ref, docs_ref, sem)
    copy.start()
    own_ref[...] = follow_ref[...]
    copy.wait()


def load(source, follow, chunk=0):
    count, width = source.shape
    kernel, dims, scratch = load_kernel, (count, width), [pltpu.SemaphoreType.DMA]
    if chunk:
        kernel, dims = functools.partial(transpose_kernel, chunk), (width, count)
        scratch = [
            pltpu.VMEM((count, width), source.dtype),
            pltpu.SemaphoreType.DMA((count // chunk,)),
        ]
    return pl.pallas_call(
        kernel,
        out_shape=[shape(dims, source.dtype), shape(follow.shape, follow.dtype)],
        in_specs=[pl.BlockSpec(memory_space=pltpu.HBM), VMEM],
        out_specs=[VMEM, VMEM],
        scratch_shapes=scratch,
        compiler_params=pltpu.CompilerParams(
            vmem_limit_bytes=(4 << 20) + (2 * source.nbytes if chunk else 0)
        ),
        cost_estimate=pl.CostEstimate(
            flops=0, bytes_accessed=2 * source.nbytes, transcendentals=0
        ),
    )(pltpu.with_memory_space_constraint(source, pltpu.HBM), follow)


def scores_kernel(chunk, docs_ref, table_ref, part_ref, top_ref, sum_ref):
    width, count = docs_ref.shape
    scale = 4.0 / math.sqrt(width)
    table = table_ref[...]
    wide = table.astype(jnp.float32)
    half_norms = 0.5 * jnp.sum(wide * wide, axis=1, keepdims=True)

    def product(start):
        cols = slice(start, start + chunk)
        return jnp.dot(table, docs_ref[:, cols], preferred_element_type=jnp.float32)

    ahead = product(0)
    for start in range(0, count, chunk):
        dots = ahead
        if start + chunk < count:
            ahead = product(start + chunk)
        cols = slice(start, start + chunk)
        scores = (dots - half_norms) * scale
        top = jnp.max(scores, axis=0, keepdims=True)
        part = jnp.exp(scores - top)
        part_ref[:, cols] = part
        top_ref[:, cols] = top
        sum_ref[:, cols] = jnp.sum(part, axis=0, keepdims=True)


def last_scores_kernel(
    chunk, docs_ref, table_ref, first_top_ref, first_sum_ref, part_ref, top_ref, lse_ref
):
    scores_kernel(chunk, docs_ref, table_ref, part_ref, top_ref, lse_ref)
    top = jnp.maximum(first_top_ref[...], top_ref[...])
    total = first_sum_ref[...] * jnp.exp(first_top_ref[...] - top)
    total += lse_ref[...] * jnp.exp(top_ref[...] - top)
    lse_ref[...] = top + jnp.log(total)


def responsibilities(chunk, factor, part_ref, resp_ref):
    rows, count = part_ref.shape
    mass = jnp.zeros((rows, 1), jnp.float32)
    for start in range(0, count, chunk):
        cols = slice(start, start + chunk)
        resp = part_ref[:, cols] * factor[:, cols]
        mass += jnp.sum(resp, axis=1, keepdims=True)
        resp_ref[:, cols] = resp.astype(jnp.bfloat16)
    return mass


def weighted_sums(chunk, resp_ref, docs_ref, first, out_ref, width):
    for start in range(0, width, chunk):
        cols = slice(first + start, first + start + chunk)
        term = jnp.dot(resp_ref[...], docs_ref[:, cols], preferred_element_type=jnp.float32)
        out_ref[:, start:start + chunk] = term.astype(out_ref.dtype)


def mass_lanes(mass):
    high = mass.astype(jnp.bfloat16).astype(jnp.float32)
    lane = lax.broadcasted_iota(jnp.int32, (mass.shape[0], LANES), 1)
    lanes = jnp.where(lane == 0, high, jnp.where(lane == 1, mass - high, 0.0))
    return lanes.astype(jnp.bfloat16)


def read_rows(rows, width):
    wide = rows.astype(jnp.float32)
    return wide[:, :width], wide[:, width:width + 1] + wide[:, width + 1:width + 2]


def send_kernel(groups, plan, chunk, me_ref, lse_ref, *refs):
    got_refs = refs[:len(plan)]
    docs_ref, part_ref, top_ref, keep_top_ref = refs[len(plan):len(plan) + 4]
    doc_lse_ref, factor_ref, send_ref, resp_ref = refs[len(plan) + 4:]
    me = me_ref[0]
    parts = [lse_ref[...]] * groups
    for got_ref, pairs in zip(got_refs, plan):
        got = got_ref[...]
        for source, target in pairs:
            parts[source] = jnp.where(me == target, got, parts[source])
    best = tree(parts, jnp.maximum)
    doc_lse = best + jnp.log(tree([jnp.exp(x - best) for x in parts], jnp.add))
    doc_lse_ref[...] = doc_lse
    factor_ref[...] = jnp.exp(keep_top_ref[...] - doc_lse)
    mass = responsibilities(chunk, jnp.exp(top_ref[...] - doc_lse), part_ref, resp_ref)
    first = send_ref.shape[1] - LANES
    weighted_sums(chunk, resp_ref, docs_ref, 0, send_ref, first)
    send_ref[:, first:] = mass_lanes(mass)


def send_rest_kernel(chunk, resp_ref, docs_ref, send_ref):
    rest = send_ref.shape[1]
    weighted_sums(chunk, resp_ref, docs_ref, docs_ref.shape[1] - rest, send_ref, rest)


def keep_kernel(chunk, factor_ref, docs_ref, part_ref, keep_ref, keep_mass_ref, resp_ref):
    mass = responsibilities(chunk, factor_ref[...], part_ref, resp_ref)
    weighted_sums(chunk, resp_ref, docs_ref, 0, keep_ref, docs_ref.shape[1])
    keep_mass_ref[...] = jnp.broadcast_to(mass, keep_mass_ref.shape)


def fold_kernel(keep_ref, keep_mass_ref, got_ref, rest_ref, own_ref, own_mass_ref, *send_refs):
    rows, width = own_ref.shape
    for slot in range(keep_ref.shape[0] // rows):
        here = slice(slot * rows, (slot + 1) * rows)
        got, got_mass = read_rows(got_ref[here], got_ref.shape[1] - LANES)
        got = jnp.concatenate([got, rest_ref[here].astype(jnp.float32)], axis=1)
        term = keep_ref[here] + got
        mass = keep_mass_ref[here, :1] + got_mass
        if slot == 0:
            own_ref[...] = term
            own_mass_ref[...] = jnp.broadcast_to(mass, own_mass_ref.shape)
        else:
            send_refs[slot - 1][:, :width] = term.astype(jnp.bfloat16)
            send_refs[slot - 1][:, width:] = mass_lanes(mass)


def final_kernel(own_ref, own_mass_ref, cent_ref, *refs):
    *got_refs, next_ref, mass_ref = refs
    width = own_ref.shape[1]
    got = [read_rows(r[...], width) for r in got_refs]
    term = tree([own_ref[...]] + [a for a, _ in got], jnp.add)
    mass = tree([own_mass_ref[:, :1]] + [b for _, b in got], jnp.add)
    next_ref[...] = (term + cent_ref[...]) / (mass + 1.0)
    mass_ref[...] = jnp.broadcast_to(mass, (mass.shape[0], LANES)).T[:1]


def shape(dims, dtype=jnp.float32):
    return jax.ShapeDtypeStruct(dims, dtype)


def make_body(n, g):
    def body(docs, centroids):
        rows, width = centroids.shape
        count = docs.shape[0]
        half = rows * n // 2
        chunk = 256
        plan = group_plan(g)
        limit = (4 << 20) + half * (48 << 10)

        def call(kernel, outs, *args, scratch=(), flops=0):
            nbytes = sum(x.nbytes for x in args)
            return pl.pallas_call(
                kernel,
                out_shape=outs,
                in_specs=[SMEM if x.dtype == jnp.int32 else VMEM for x in args],
                out_specs=[VMEM] * len(outs),
                scratch_shapes=scratch,
                compiler_params=pltpu.CompilerParams(vmem_limit_bytes=limit),
                cost_estimate=pl.CostEstimate(
                    flops=flops, bytes_accessed=nbytes, transcendentals=0
                ),
            )(*args)

        flops = 2 * half * count * width
        stats = [shape((half, count)), shape((1, count)), shape((1, count))]
        rounded = centroids.astype(jnp.bfloat16)
        blocks = [swap(rounded, "dev", n, m) for m in range(2, n, 2)]
        docs_t, own = load(docs, rounded, chunk)
        mine = jnp.concatenate([own] + blocks, axis=0)
        theirs = swap(mine, "dev", n, 1)
        part, top, total = call(
            functools.partial(scores_kernel, chunk), stats, docs_t, mine, flops=flops
        )
        other_part, other_top, lse = call(
            functools.partial(last_scores_kernel, chunk), stats,
            docs_t, theirs, top, total, flops=flops,
        )
        others = [lax.ppermute(lse, "cgrp", pairs) for pairs in plan]
        docs, lse = load(docs, lse)
        first = width // 2
        doc_lse, factor, send, resp = call(
            functools.partial(send_kernel, g, plan, chunk),
            [shape((1, count)), shape((1, count)),
             shape((half, first + LANES), jnp.bfloat16), shape((half, count), jnp.bfloat16)],
            lax.axis_index("cgrp").reshape(1), lse, *others, docs, other_part, other_top, top,
            flops=flops // 2,
        )
        got = swap(send, "dev", n, 1)
        rest, = call(
            functools.partial(send_rest_kernel, chunk),
            [shape((half, width - first), jnp.bfloat16)], resp, docs, flops=flops // 2,
        )
        rest = swap(rest, "dev", n, 1)
        keep, keep_mass = call(
            functools.partial(keep_kernel, chunk),
            [shape((half, width)), shape((half, LANES))], factor, docs, part,
            scratch=[pltpu.VMEM((half, count), jnp.bfloat16)], flops=flops,
        )
        own, own_mass, *sends = call(
            fold_kernel,
            [shape((rows, width)), shape((rows, LANES))]
            + [shape((rows, width + LANES), jnp.bfloat16)] * (n // 2 - 1),
            keep, keep_mass, got, rest,
        )
        far_first = sorted(range(1, n // 2), key=lambda j: (-j.bit_count(), j))
        arrived = [swap(sends[j - 1], "dev", n, 2 * j) for j in far_first]
        result, mass = call(
            final_kernel, [shape((rows, width)), shape((1, rows))],
            own, own_mass, centroids, *arrived,
        )
        return (result, mass.reshape(rows), doc_lse.reshape(count))

    return body


def solution(mesh):
    in_specs = (P("dev", None), P(("cgrp", "dev"), None))
    out_specs = (P(("cgrp", "dev"), None), P(("cgrp", "dev")), P("dev"))
    return jax.shard_map(
        make_body(mesh.shape["dev"], mesh.shape["cgrp"]),
        mesh=mesh, in_specs=in_specs, out_specs=out_specs, check_vma=False,
    )
```

```python
import functools
import math

import jax
import jax.numpy as jnp
from jax import lax
from jax.experimental import pallas as pl
from jax.experimental.pallas import tpu as pltpu
from jax.sharding import PartitionSpec as P

LANES = 128
VMEM = pl.BlockSpec(memory_space=pltpu.VMEM)
SMEM = pl.BlockSpec(memory_space=pltpu.SMEM)


def swap(x, axis, size, mask):
    return lax.ppermute(x, axis, [(i, i ^ mask) for i in range(size)])


def group_plan(g):
    if g == 4:
        return [
            [(0, 1), (1, 0), (2, 3), (3, 2)],
            [(0, 3), (1, 2), (2, 0), (3, 1)],
            [(0, 2), (1, 3), (2, 1), (3, 0)],
        ]
    return [[(i, i ^ m) for i in range(g)] for m in range(1, g)]


def tree(parts, op):
    while len(parts) > 1:
        parts = [op(parts[i], parts[i + 1]) for i in range(0, len(parts), 2)]
    return parts[0]


def transpose_kernel(chunk, source_ref, follow_ref, docs_ref, own_ref, landing, sems):
    copies = []
    for i, start in enumerate(range(0, source_ref.shape[0], chunk)):
        here = pl.ds(start, chunk)
        copies.append(pltpu.make_async_copy(source_ref.at[here], landing.at[here], sems.at[i]))
        copies[-1].start()
    own_ref[...] = follow_ref[...]
    for i, copy in enumerate(copies):
        copy.wait()
        here = slice(i * chunk, (i + 1) * chunk)
        docs_ref[:, here] = landing[here, :].T


def load_kernel(source_ref, follow_ref, docs_ref, own_ref, sem):
    copy = pltpu.make_async_copy(source_ref, docs_ref, sem)
    copy.start()
    own_ref[...] = follow_ref[...]
    copy.wait()


def load(source, follow, chunk=0):
    count, width = source.shape
    kernel, dims, scratch = load_kernel, (count, width), [pltpu.SemaphoreType.DMA]
    if chunk:
        kernel, dims = functools.partial(transpose_kernel, chunk), (width, count)
        scratch = [
            pltpu.VMEM((count, width), source.dtype),
            pltpu.SemaphoreType.DMA((count // chunk,)),
        ]
    return pl.pallas_call(
        kernel,
        out_shape=[shape(dims, source.dtype), shape(follow.shape, follow.dtype)],
        in_specs=[pl.BlockSpec(memory_space=pltpu.HBM), VMEM],
        out_specs=[VMEM, VMEM],
        scratch_shapes=scratch,
        compiler_params=pltpu.CompilerParams(
            vmem_limit_bytes=(4 << 20) + (2 * source.nbytes if chunk else 0)
        ),
        cost_estimate=pl.CostEstimate(
            flops=0, bytes_accessed=2 * source.nbytes, transcendentals=0
        ),
    )(pltpu.with_memory_space_constraint(source, pltpu.HBM), follow)


def scores_kernel(chunk, docs_ref, table_ref, part_ref, top_ref, sum_ref):
    width, count = docs_ref.shape
    scale = 4.0 / math.sqrt(width)
    table = table_ref[...]
    wide = table.astype(jnp.float32)
    half_norms = 0.5 * jnp.sum(wide * wide, axis=1, keepdims=True)
    for start in range(0, count, chunk):
        cols = slice(start, start + chunk)
        dots = jnp.dot(table, docs_ref[:, cols], preferred_element_type=jnp.float32)
        scores = (dots - half_norms) * scale
        top = jnp.max(scores, axis=0, keepdims=True)
        part = jnp.exp(scores - top)
        part_ref[:, cols] = part
        top_ref[:, cols] = top
        sum_ref[:, cols] = jnp.sum(part, axis=0, keepdims=True)


def last_scores_kernel(
    chunk, docs_ref, table_ref, first_top_ref, first_sum_ref, part_ref, top_ref, lse_ref
):
    scores_kernel(chunk, docs_ref, table_ref, part_ref, top_ref, lse_ref)
    top = jnp.maximum(first_top_ref[...], top_ref[...])
    total = first_sum_ref[...] * jnp.exp(first_top_ref[...] - top)
    total += lse_ref[...] * jnp.exp(top_ref[...] - top)
    lse_ref[...] = top + jnp.log(total)


def weighted_sums(chunk, factor, docs_ref, part_ref, resp_ref, store):
    rows, count = part_ref.shape
    mass = jnp.zeros((rows, 1), jnp.float32)
    for start in range(0, count, chunk):
        cols = slice(start, start + chunk)
        resp = part_ref[:, cols] * factor[:, cols]
        mass += jnp.sum(resp, axis=1, keepdims=True)
        resp_ref[:, cols] = resp.astype(jnp.bfloat16)
    for start in range(0, docs_ref.shape[1], chunk):
        cols = slice(start, start + chunk)
        store(cols, jnp.dot(resp_ref[...], docs_ref[:, cols], preferred_element_type=jnp.float32))
    return mass


def mass_lanes(mass):
    high = mass.astype(jnp.bfloat16).astype(jnp.float32)
    lane = lax.broadcasted_iota(jnp.int32, (mass.shape[0], LANES), 1)
    lanes = jnp.where(lane == 0, high, jnp.where(lane == 1, mass - high, 0.0))
    return lanes.astype(jnp.bfloat16)


def read_rows(rows, width):
    wide = rows.astype(jnp.float32)
    return wide[:, :width], wide[:, width:width + 1] + wide[:, width + 1:width + 2]


def send_kernel(groups, plan, chunk, me_ref, lse_ref, *refs):
    got_refs = refs[:len(plan)]
    docs_ref, part_ref, top_ref, keep_top_ref = refs[len(plan):len(plan) + 4]
    doc_lse_ref, factor_ref, send_ref, resp_ref = refs[len(plan) + 4:]
    me = me_ref[0]
    parts = [lse_ref[...]] * groups
    for got_ref, pairs in zip(got_refs, plan):
        got = got_ref[...]
        for source, target in pairs:
            parts[source] = jnp.where(me == target, got, parts[source])
    best = tree(parts, jnp.maximum)
    doc_lse = best + jnp.log(tree([jnp.exp(x - best) for x in parts], jnp.add))
    doc_lse_ref[...] = doc_lse
    factor_ref[...] = jnp.exp(keep_top_ref[...] - doc_lse)
    factor = jnp.exp(top_ref[...] - doc_lse)

    def store(cols, term):
        send_ref[:, cols] = term.astype(jnp.bfloat16)

    mass = weighted_sums(chunk, factor, docs_ref, part_ref, resp_ref, store)
    send_ref[:, docs_ref.shape[1]:] = mass_lanes(mass)


def keep_kernel(chunk, factor_ref, docs_ref, part_ref, keep_ref, keep_mass_ref, resp_ref):
    def store(cols, term):
        keep_ref[:, cols] = term

    mass = weighted_sums(chunk, factor_ref[...], docs_ref, part_ref, resp_ref, store)
    keep_mass_ref[...] = jnp.broadcast_to(mass, keep_mass_ref.shape)


def fold_kernel(keep_ref, keep_mass_ref, got_ref, own_ref, own_mass_ref, *send_refs):
    rows, width = own_ref.shape
    for slot in range(keep_ref.shape[0] // rows):
        here = slice(slot * rows, (slot + 1) * rows)
        got, got_mass = read_rows(got_ref[here], width)
        term = keep_ref[here] + got
        mass = keep_mass_ref[here, :1] + got_mass
        if slot == 0:
            own_ref[...] = term
            own_mass_ref[...] = jnp.broadcast_to(mass, own_mass_ref.shape)
        else:
            send_refs[slot - 1][:, :width] = term.astype(jnp.bfloat16)
            send_refs[slot - 1][:, width:] = mass_lanes(mass)


def final_kernel(own_ref, own_mass_ref, cent_ref, *refs):
    *got_refs, next_ref, mass_ref = refs
    width = own_ref.shape[1]
    got = [read_rows(r[...], width) for r in got_refs]
    term = tree([own_ref[...]] + [a for a, _ in got], jnp.add)
    mass = tree([own_mass_ref[:, :1]] + [b for _, b in got], jnp.add)
    next_ref[...] = (term + cent_ref[...]) / (mass + 1.0)
    mass_ref[...] = jnp.broadcast_to(mass, (mass.shape[0], LANES)).T[:1]


def shape(dims, dtype=jnp.float32):
    return jax.ShapeDtypeStruct(dims, dtype)


def make_body(n, g):
    def body(docs, centroids):
        rows, width = centroids.shape
        count = docs.shape[0]
        half = rows * n // 2
        chunk = 256
        plan = group_plan(g)
        limit = (4 << 20) + half * (48 << 10)

        def call(kernel, outs, *args, scratch=(), flops=0):
            nbytes = sum(x.nbytes for x in args)
            return pl.pallas_call(
                kernel,
                out_shape=outs,
                in_specs=[SMEM if x.dtype == jnp.int32 else VMEM for x in args],
                out_specs=[VMEM] * len(outs),
                scratch_shapes=scratch,
                compiler_params=pltpu.CompilerParams(vmem_limit_bytes=limit),
                cost_estimate=pl.CostEstimate(
                    flops=flops, bytes_accessed=nbytes, transcendentals=0
                ),
            )(*args)

        flops = 2 * half * count * width
        stats = [shape((half, count)), shape((1, count)), shape((1, count))]
        resp = [pltpu.VMEM((half, count), jnp.bfloat16)]
        rounded = centroids.astype(jnp.bfloat16)
        blocks = [swap(rounded, "dev", n, m + 1) for m in range(2, n, 2)]
        docs_t, own = load(docs, rounded, chunk)
        mine = jnp.concatenate([own] + blocks, axis=0)
        theirs = swap(mine, "dev", n, 1)
        part, top, total = call(
            functools.partial(scores_kernel, chunk), stats, docs_t, mine, flops=flops
        )
        other_part, other_top, lse = call(
            functools.partial(last_scores_kernel, chunk), stats,
            docs_t, theirs, top, total, flops=flops,
        )
        others = [lax.ppermute(lse, "cgrp", pairs) for pairs in plan]
        docs, lse = load(docs, lse)
        doc_lse, factor, send = call(
            functools.partial(send_kernel, g, plan, chunk),
            [shape((1, count)), shape((1, count)), shape((half, width + LANES), jnp.bfloat16)],
            lax.axis_index("cgrp").reshape(1), lse, *others, docs, other_part, other_top, top,
            scratch=resp, flops=flops,
        )
        got = swap(send, "dev", n, 1)
        keep, keep_mass = call(
            functools.partial(keep_kernel, chunk),
            [shape((half, width)), shape((half, LANES))],
            factor, docs, part, scratch=resp, flops=flops,
        )
        own, own_mass, *sends = call(
            fold_kernel,
            [shape((rows, width)), shape((rows, LANES))]
            + [shape((rows, width + LANES), jnp.bfloat16)] * (n // 2 - 1),
            keep, keep_mass, got,
        )
        far_first = sorted(range(1, n // 2), key=lambda j: (-j.bit_count(), j))
        arrived = [swap(sends[j - 1], "dev", n, 2 * j + 1) for j in far_first]
        result, mass = call(
            final_kernel, [shape((rows, width)), shape((1, rows))],
            own, own_mass, centroids, *arrived,
        )
        return (result, mass.reshape(rows), doc_lse.reshape(count))

    return body


def solution(mesh):
    in_specs = (P("dev", None), P(("cgrp", "dev"), None))
    out_specs = (P(("cgrp", "dev"), None), P(("cgrp", "dev")), P("dev"))
    return jax.shard_map(
        make_body(mesh.shape["dev"], mesh.shape["cgrp"]),
        mesh=mesh, in_specs=in_specs, out_specs=out_specs, check_vma=False,
    )
```

```python
import functools
import math

import jax
import jax.numpy as jnp
from jax import lax
from jax.experimental import pallas as pl
from jax.experimental.pallas import tpu as pltpu
from jax.sharding import PartitionSpec as P

LANES = 128
VMEM = pl.BlockSpec(memory_space=pltpu.VMEM)
SMEM = pl.BlockSpec(memory_space=pltpu.SMEM)


def swap(x, axis, size, mask):
    return lax.ppermute(x, axis, [(i, i ^ mask) for i in range(size)])


def chip_plan(n):
    near = list(range(2, n - 2, 2))
    turned = near[len(near) // 2:] + near[:len(near) // 2]
    masks = list(zip(near, turned)) + [(n - 2, n - 2)]
    return [[(i, i ^ pair[i % 2] ^ 1) for i in range(n)] for pair in masks]


def group_plan(g):
    if g == 4:
        return [
            [(0, 1), (1, 0), (2, 3), (3, 2)],
            [(0, 3), (1, 2), (2, 0), (3, 1)],
            [(0, 2), (1, 3), (2, 1), (3, 0)],
        ]
    return [[(i, i ^ m) for i in range(g)] for m in range(1, g)]


def tree(parts, op):
    while len(parts) > 1:
        parts = [op(parts[i], parts[i + 1]) for i in range(0, len(parts), 2)]
    return parts[0]


def transpose_kernel(chunk, source_ref, follow_ref, docs_ref, own_ref, landing, sems):
    copies = []
    for i, start in enumerate(range(0, source_ref.shape[0], chunk)):
        here = pl.ds(start, chunk)
        copies.append(pltpu.make_async_copy(source_ref.at[here], landing.at[here], sems.at[i]))
        copies[-1].start()
    own_ref[...] = follow_ref[...]
    for i, copy in enumerate(copies):
        copy.wait()
        here = slice(i * chunk, (i + 1) * chunk)
        docs_ref[:, here] = landing[here, :].T


def load_kernel(source_ref, follow_ref, docs_ref, own_ref, sem):
    copy = pltpu.make_async_copy(source_ref, docs_ref, sem)
    copy.start()
    own_ref[...] = follow_ref[...]
    copy.wait()


def load(source, follow, chunk=0):
    count, width = source.shape
    kernel, dims, scratch = load_kernel, (count, width), [pltpu.SemaphoreType.DMA]
    if chunk:
        kernel, dims = functools.partial(transpose_kernel, chunk), (width, count)
        scratch = [
            pltpu.VMEM((count, width), source.dtype),
            pltpu.SemaphoreType.DMA((count // chunk,)),
        ]
    return pl.pallas_call(
        kernel,
        out_shape=[shape(dims, source.dtype), shape(follow.shape, follow.dtype)],
        in_specs=[pl.BlockSpec(memory_space=pltpu.HBM), VMEM],
        out_specs=[VMEM, VMEM],
        scratch_shapes=scratch,
        compiler_params=pltpu.CompilerParams(
            vmem_limit_bytes=(4 << 20) + (2 * source.nbytes if chunk else 0)
        ),
        cost_estimate=pl.CostEstimate(
            flops=0, bytes_accessed=2 * source.nbytes, transcendentals=0
        ),
    )(pltpu.with_memory_space_constraint(source, pltpu.HBM), follow)


def scores_kernel(chunk, docs_ref, table_ref, part_ref, top_ref, sum_ref):
    width, count = docs_ref.shape
    scale = 4.0 / math.sqrt(width)
    table = table_ref[...]
    wide = table.astype(jnp.float32)
    half_norms = 0.5 * jnp.sum(wide * wide, axis=1, keepdims=True)
    for start in range(0, count, chunk):
        cols = slice(start, start + chunk)
        dots = jnp.dot(table, docs_ref[:, cols], preferred_element_type=jnp.float32)
        scores = (dots - half_norms) * scale
        top = jnp.max(scores, axis=0, keepdims=True)
        part = jnp.exp(scores - top)
        part_ref[:, cols] = part
        top_ref[:, cols] = top
        sum_ref[:, cols] = jnp.sum(part, axis=0, keepdims=True)


def last_scores_kernel(
    chunk, docs_ref, table_ref, first_top_ref, first_sum_ref, part_ref, top_ref, lse_ref
):
    scores_kernel(chunk, docs_ref, table_ref, part_ref, top_ref, lse_ref)
    top = jnp.maximum(first_top_ref[...], top_ref[...])
    total = first_sum_ref[...] * jnp.exp(first_top_ref[...] - top)
    total += lse_ref[...] * jnp.exp(top_ref[...] - top)
    lse_ref[...] = top + jnp.log(total)


def weighted_sums(chunk, factor, docs_ref, part_ref, resp_ref, store):
    rows, count = part_ref.shape
    mass = jnp.zeros((rows, 1), jnp.float32)
    for start in range(0, count, chunk):
        cols = slice(start, start + chunk)
        resp = part_ref[:, cols] * factor[:, cols]
        mass += jnp.sum(resp, axis=1, keepdims=True)
        resp_ref[:, cols] = resp.astype(jnp.bfloat16)
    for start in range(0, docs_ref.shape[1], chunk):
        cols = slice(start, start + chunk)
        store(cols, jnp.dot(resp_ref[...], docs_ref[:, cols], preferred_element_type=jnp.float32))
    return mass


def mass_lanes(mass):
    high = mass.astype(jnp.bfloat16).astype(jnp.float32)
    lane = lax.broadcasted_iota(jnp.int32, (mass.shape[0], LANES), 1)
    lanes = jnp.where(lane == 0, high, jnp.where(lane == 1, mass - high, 0.0))
    return lanes.astype(jnp.bfloat16)


def read_rows(rows, width):
    wide = rows.astype(jnp.float32)
    return wide[:, :width], wide[:, width:width + 1] + wide[:, width + 1:width + 2]


def send_kernel(groups, plan, chunk, me_ref, lse_ref, *refs):
    got_refs = refs[:len(plan)]
    docs_ref, part_ref, top_ref, keep_top_ref = refs[len(plan):len(plan) + 4]
    doc_lse_ref, factor_ref, send_ref, resp_ref = refs[len(plan) + 4:]
    me = me_ref[0]
    parts = [lse_ref[...]] * groups
    for got_ref, pairs in zip(got_refs, plan):
        got = got_ref[...]
        for source, target in pairs:
            parts[source] = jnp.where(me == target, got, parts[source])
    best = tree(parts, jnp.maximum)
    doc_lse = best + jnp.log(tree([jnp.exp(x - best) for x in parts], jnp.add))
    doc_lse_ref[...] = doc_lse
    factor_ref[...] = jnp.exp(keep_top_ref[...] - doc_lse)
    factor = jnp.exp(top_ref[...] - doc_lse)

    def store(cols, term):
        send_ref[:, cols] = term.astype(jnp.bfloat16)

    mass = weighted_sums(chunk, factor, docs_ref, part_ref, resp_ref, store)
    send_ref[:, docs_ref.shape[1]:] = mass_lanes(mass)


def keep_kernel(chunk, factor_ref, docs_ref, part_ref, keep_ref, keep_mass_ref, resp_ref):
    def store(cols, term):
        keep_ref[:, cols] = term

    mass = weighted_sums(chunk, factor_ref[...], docs_ref, part_ref, resp_ref, store)
    keep_mass_ref[...] = jnp.broadcast_to(mass, keep_mass_ref.shape)


def fold_kernel(keep_ref, keep_mass_ref, got_ref, own_ref, own_mass_ref, *send_refs):
    rows, width = own_ref.shape
    for slot in range(keep_ref.shape[0] // rows):
        here = slice(slot * rows, (slot + 1) * rows)
        got, got_mass = read_rows(got_ref[here], width)
        term = keep_ref[here] + got
        mass = keep_mass_ref[here, :1] + got_mass
        if slot == 0:
            own_ref[...] = term
            own_mass_ref[...] = jnp.broadcast_to(mass, own_mass_ref.shape)
        else:
            send_refs[slot - 1][:, :width] = term.astype(jnp.bfloat16)
            send_refs[slot - 1][:, width:] = mass_lanes(mass)


def final_kernel(own_ref, own_mass_ref, cent_ref, *refs):
    *got_refs, next_ref, mass_ref = refs
    width = own_ref.shape[1]
    got = [read_rows(r[...], width) for r in got_refs]
    term = tree([own_ref[...]] + [a for a, _ in got], jnp.add)
    mass = tree([own_mass_ref[:, :1]] + [b for _, b in got], jnp.add)
    next_ref[...] = (term + cent_ref[...]) / (mass + 1.0)
    mass_ref[...] = jnp.broadcast_to(mass, (mass.shape[0], LANES)).T[:1]


def shape(dims, dtype=jnp.float32):
    return jax.ShapeDtypeStruct(dims, dtype)


def make_body(n, g):
    def body(docs, centroids):
        rows, width = centroids.shape
        count = docs.shape[0]
        half = rows * n // 2
        chunk = 256
        plan = group_plan(g)
        limit = (4 << 20) + half * (48 << 10)

        def call(kernel, outs, *args, scratch=(), flops=0):
            nbytes = sum(x.nbytes for x in args)
            return pl.pallas_call(
                kernel,
                out_shape=outs,
                in_specs=[SMEM if x.dtype == jnp.int32 else VMEM for x in args],
                out_specs=[VMEM] * len(outs),
                scratch_shapes=scratch,
                compiler_params=pltpu.CompilerParams(vmem_limit_bytes=limit),
                cost_estimate=pl.CostEstimate(
                    flops=flops, bytes_accessed=nbytes, transcendentals=0
                ),
            )(*args)

        flops = 2 * half * count * width
        stats = [shape((half, count)), shape((1, count)), shape((1, count))]
        resp = [pltpu.VMEM((half, count), jnp.bfloat16)]
        rounded = centroids.astype(jnp.bfloat16)
        routes = chip_plan(n)
        blocks = [lax.ppermute(rounded, "dev", pairs) for pairs in routes]
        docs_t, own = load(docs, rounded, chunk)
        mine = jnp.concatenate([own] + blocks, axis=0)
        theirs = swap(mine, "dev", n, 1)
        part, top, total = call(
            functools.partial(scores_kernel, chunk), stats, docs_t, mine, flops=flops
        )
        other_part, other_top, lse = call(
            functools.partial(last_scores_kernel, chunk), stats,
            docs_t, theirs, top, total, flops=flops,
        )
        others = [lax.ppermute(lse, "cgrp", pairs) for pairs in plan]
        docs, lse = load(docs, lse)
        doc_lse, factor, send = call(
            functools.partial(send_kernel, g, plan, chunk),
            [shape((1, count)), shape((1, count)), shape((half, width + LANES), jnp.bfloat16)],
            lax.axis_index("cgrp").reshape(1), lse, *others, docs, other_part, other_top, top,
            scratch=resp, flops=flops,
        )
        got = swap(send, "dev", n, 1)
        keep, keep_mass = call(
            functools.partial(keep_kernel, chunk),
            [shape((half, width)), shape((half, LANES))],
            factor, docs, part, scratch=resp, flops=flops,
        )
        own, own_mass, *sends = call(
            fold_kernel,
            [shape((rows, width)), shape((rows, LANES))]
            + [shape((rows, width + LANES), jnp.bfloat16)] * (n // 2 - 1),
            keep, keep_mass, got,
        )
        arrived = [
            lax.ppermute(x, "dev", [(target, source) for source, target in pairs])
            for x, pairs in zip(sends[-1:] + sends[:-1], routes[-1:] + routes[:-1])
        ]
        result, mass = call(
            final_kernel, [shape((rows, width)), shape((1, rows))],
            own, own_mass, centroids, *arrived,
        )
        return (result, mass.reshape(rows), doc_lse.reshape(count))

    return body


def solution(mesh):
    in_specs = (P("dev", None), P(("cgrp", "dev"), None))
    out_specs = (P(("cgrp", "dev"), None), P(("cgrp", "dev")), P("dev"))
    return jax.shard_map(
        make_body(mesh.shape["dev"], mesh.shape["cgrp"]),
        mesh=mesh, in_specs=in_specs, out_specs=out_specs, check_vma=False,
    )
```

```python
import functools
import math

import jax
import jax.numpy as jnp
from jax import lax
from jax.experimental import pallas as pl
from jax.experimental.pallas import tpu as pltpu
from jax.sharding import PartitionSpec as P

LANES = 128
VMEM = pl.BlockSpec(memory_space=pltpu.VMEM)
SMEM = pl.BlockSpec(memory_space=pltpu.SMEM)


def swap(x, axis, size, mask):
    return lax.ppermute(x, axis, [(i, i ^ mask) for i in range(size)])


def chip_plan(n):
    near = list(range(2, n - 2, 2))
    turned = near[len(near) // 2:] + near[:len(near) // 2]
    masks = [(n - 2, n - 2)] + list(zip(near, turned))
    return [[(i, i ^ pair[i % 2] ^ 1) for i in range(n)] for pair in masks]


def group_plan(g):
    if g == 4:
        return [
            [(0, 2), (1, 3), (2, 1), (3, 0)],
            [(0, 3), (1, 2), (2, 0), (3, 1)],
            [(0, 1), (1, 0), (2, 3), (3, 2)],
        ]
    return [[(i, i ^ m) for i in range(g)] for m in range(1, g)]


def tree(parts, op):
    while len(parts) > 1:
        parts = [op(parts[i], parts[i + 1]) for i in range(0, len(parts), 2)]
    return parts[0]


def transpose_kernel(chunk, source_ref, follow_ref, docs_ref, own_ref, landing, sems):
    copies = []
    for i, start in enumerate(range(0, source_ref.shape[0], chunk)):
        here = pl.ds(start, chunk)
        copies.append(pltpu.make_async_copy(source_ref.at[here], landing.at[here], sems.at[i]))
        copies[-1].start()
    own_ref[...] = follow_ref[...]
    for i, copy in enumerate(copies):
        copy.wait()
        here = slice(i * chunk, (i + 1) * chunk)
        docs_ref[:, here] = landing[here, :].T


def load_kernel(*refs):
    half = len(refs) // 2
    sources, follow_ref = refs[:half - 1], refs[half - 1]
    targets, own_ref, sems = refs[half:-2], refs[-2], refs[-1]
    copies = [
        pltpu.make_async_copy(source, target, sems.at[i])
        for i, (source, target) in enumerate(zip(sources, targets))
    ]
    for copy in copies:
        copy.start()
    own_ref[...] = follow_ref[...]
    for copy in copies:
        copy.wait()


def load(sources, follow, chunk=0):
    kernel, dims = load_kernel, sources[0].shape
    scratch = [pltpu.SemaphoreType.DMA((len(sources),))]
    if chunk:
        kernel, (count, width) = functools.partial(transpose_kernel, chunk), dims
        dims = (width, count)
        scratch = [
            pltpu.VMEM((count, width), follow.dtype),
            pltpu.SemaphoreType.DMA((count // chunk,)),
        ]
    size = sum(x.nbytes for x in sources)
    return pl.pallas_call(
        kernel,
        out_shape=[shape(dims, x.dtype) for x in sources] + [shape(follow.shape, follow.dtype)],
        in_specs=[pl.BlockSpec(memory_space=pltpu.HBM)] * len(sources) + [VMEM],
        out_specs=[VMEM] * (len(sources) + 1),
        scratch_shapes=scratch,
        compiler_params=pltpu.CompilerParams(
            vmem_limit_bytes=(4 << 20) + (2 * size if chunk else 0)
        ),
        cost_estimate=pl.CostEstimate(flops=0, bytes_accessed=2 * size, transcendentals=0),
    )(*[pltpu.with_memory_space_constraint(x, pltpu.HBM) for x in sources], follow)


def scores_kernel(chunk, docs_ref, table_ref, part_ref, top_ref, sum_ref):
    width, count = docs_ref.shape
    scale = 4.0 / math.sqrt(width)
    table = table_ref[...]
    wide = table.astype(jnp.float32)
    half_norms = 0.5 * jnp.sum(wide * wide, axis=1, keepdims=True)
    for start in range(0, count, chunk):
        cols = slice(start, start + chunk)
        dots = jnp.dot(table, docs_ref[:, cols], preferred_element_type=jnp.float32)
        scores = (dots - half_norms) * scale
        top = jnp.max(scores, axis=0, keepdims=True)
        part = jnp.exp(scores - top)
        part_ref[:, cols] = part.astype(part_ref.dtype)
        top_ref[:, cols] = top
        sum_ref[:, cols] = jnp.sum(part, axis=0, keepdims=True)


def last_scores_kernel(
    chunk, docs_ref, table_ref, first_top_ref, first_sum_ref, part_ref, top_ref, lse_ref
):
    scores_kernel(chunk, docs_ref, table_ref, part_ref, top_ref, lse_ref)
    top = jnp.maximum(first_top_ref[...], top_ref[...])
    total = first_sum_ref[...] * jnp.exp(first_top_ref[...] - top)
    total += lse_ref[...] * jnp.exp(top_ref[...] - top)
    lse_ref[...] = top + jnp.log(total)


def weighted_sums(chunk, factor, docs_ref, part_ref, resp_ref, store):
    rows, count = part_ref.shape
    mass = jnp.zeros((rows, 1), jnp.float32)
    for start in range(0, count, chunk):
        cols = slice(start, start + chunk)
        resp = part_ref[:, cols].astype(jnp.float32) * factor[:, cols]
        mass += jnp.sum(resp, axis=1, keepdims=True)
        resp_ref[:, cols] = resp.astype(jnp.bfloat16)
    for start in range(0, docs_ref.shape[1], chunk):
        cols = slice(start, start + chunk)
        store(cols, jnp.dot(resp_ref[...], docs_ref[:, cols], preferred_element_type=jnp.float32))
    return mass


def mass_lanes(mass):
    high = mass.astype(jnp.bfloat16).astype(jnp.float32)
    lane = lax.broadcasted_iota(jnp.int32, (mass.shape[0], LANES), 1)
    lanes = jnp.where(lane == 0, high, jnp.where(lane == 1, mass - high, 0.0))
    return lanes.astype(jnp.bfloat16)


def read_rows(rows, width):
    wide = rows.astype(jnp.float32)
    return wide[:, :width], wide[:, width:width + 1] + wide[:, width + 1:width + 2]


def factors_kernel(groups, plan, me_ref, lse_ref, *refs):
    got_refs = refs[:len(plan)]
    top_ref, their_top_ref, doc_lse_ref, factor_ref, send_ref = refs[len(plan):]
    me = me_ref[0]
    parts = [lse_ref[...]] * groups
    for got_ref, pairs in zip(got_refs, plan):
        got = got_ref[...]
        for source, target in pairs:
            parts[source] = jnp.where(me == target, got, parts[source])
    best = tree(parts, jnp.maximum)
    doc_lse = best + jnp.log(tree([jnp.exp(x - best) for x in parts], jnp.add))
    doc_lse_ref[...] = doc_lse
    factor_ref[...] = jnp.exp(top_ref[...] - doc_lse)
    send_ref[...] = jnp.exp(their_top_ref[...] - doc_lse)


def first_sums_kernel(chunk, factor_ref, docs_ref, part_ref, sum_ref, mass_ref, resp_ref):
    def store(cols, term):
        sum_ref[:, cols] = term

    mass = weighted_sums(chunk, factor_ref[...], docs_ref, part_ref, resp_ref, store)
    mass_ref[...] = jnp.broadcast_to(mass, mass_ref.shape)


def second_sums_kernel(
    chunk, factor_ref, docs_ref, part_ref, sum_ref, mass_ref, own_ref, own_mass_ref, *refs
):
    *send_refs, resp_ref = refs
    rows, width = own_ref.shape

    def store(cols, term):
        if cols.start < width:
            term += sum_ref[:, cols]
            own_ref[:, cols] = term[:rows]
        for slot, ref in enumerate(send_refs, 1):
            ref[:, cols] = term[slot * rows:(slot + 1) * rows].astype(jnp.bfloat16)

    mass = weighted_sums(chunk, factor_ref[...], docs_ref, part_ref, resp_ref, store)
    mass += mass_ref[:, :1]
    own_mass_ref[...] = jnp.broadcast_to(mass[:rows], own_mass_ref.shape)
    store(slice(width, width + LANES), mass_lanes(mass))


def final_kernel(own_ref, own_mass_ref, cent_ref, *refs):
    *got_refs, next_ref, mass_ref = refs
    width = own_ref.shape[1]
    got = [read_rows(r[...], width) for r in got_refs]
    term = tree([own_ref[...]] + [a for a, _ in got], jnp.add)
    mass = tree([own_mass_ref[:, :1]] + [b for _, b in got], jnp.add)
    next_ref[...] = (term + cent_ref[...]) / (mass + 1.0)
    mass_ref[...] = jnp.broadcast_to(mass, (mass.shape[0], LANES)).T[:1]


def shape(dims, dtype=jnp.float32):
    return jax.ShapeDtypeStruct(dims, dtype)


def make_body(n, g):
    def body(docs, centroids):
        rows, width = centroids.shape
        count = docs.shape[0]
        half = rows * n // 2
        chunk = 256
        plan = group_plan(g)
        limit = (4 << 20) + half * (48 << 10)

        def call(kernel, outs, *args, scratch=(), flops=0):
            nbytes = sum(x.nbytes for x in args)
            return pl.pallas_call(
                kernel,
                out_shape=outs,
                in_specs=[SMEM if x.dtype == jnp.int32 else VMEM for x in args],
                out_specs=[VMEM] * len(outs),
                scratch_shapes=scratch,
                compiler_params=pltpu.CompilerParams(vmem_limit_bytes=limit),
                cost_estimate=pl.CostEstimate(
                    flops=flops, bytes_accessed=nbytes, transcendentals=0
                ),
            )(*args)

        flops = 2 * half * count * width
        stats = [shape((1, count)), shape((1, count))]
        resp = [pltpu.VMEM((half, count), jnp.bfloat16)]
        rounded = centroids.astype(jnp.bfloat16)
        routes = chip_plan(n)
        blocks = [lax.ppermute(rounded, "dev", pairs) for pairs in routes]
        their_docs = swap(docs, "dev", n, 1)
        docs_t, own = load([docs], rounded, chunk)
        mine = jnp.concatenate([own] + blocks, axis=0)
        theirs = swap(mine, "dev", n, 1)
        part, top, total = call(
            functools.partial(scores_kernel, chunk), [shape((half, count))] + stats,
            docs_t, mine, flops=flops,
        )
        other_part, other_top, lse = call(
            functools.partial(last_scores_kernel, chunk),
            [shape((half, count), jnp.bfloat16)] + stats,
            docs_t, theirs, top, total, flops=flops,
        )
        others = [lax.ppermute(lse, "cgrp", pairs) for pairs in plan]
        their_part = swap(other_part, "dev", n, 1)
        docs, lse = load([docs], lse)
        doc_lse, factor, their_factor = call(
            functools.partial(factors_kernel, g, plan), [shape((1, count))] * 3,
            lax.axis_index("cgrp").reshape(1), lse, *others, top, other_top,
        )
        their_factor = swap(their_factor, "dev", n, 1)
        sums, mass = call(
            functools.partial(first_sums_kernel, chunk),
            [shape((half, width)), shape((half, LANES))],
            factor, docs, part, scratch=resp, flops=flops,
        )
        own, own_mass, *sends = call(
            functools.partial(second_sums_kernel, chunk),
            [shape((rows, width)), shape((rows, LANES))]
            + [shape((rows, width + LANES), jnp.bfloat16)] * (n // 2 - 1),
            their_factor, their_docs, their_part, sums, mass, scratch=resp, flops=flops,
        )
        arrived = [
            lax.ppermute(x, "dev", [(target, source) for source, target in pairs])
            for x, pairs in zip(sends, routes)
        ]
        result, mass = call(
            final_kernel, [shape((rows, width)), shape((1, rows))],
            own, own_mass, centroids, *arrived,
        )
        return (result, mass.reshape(rows), doc_lse.reshape(count))

    return body


def solution(mesh):
    in_specs = (P("dev", None), P(("cgrp", "dev"), None))
    out_specs = (P(("cgrp", "dev"), None), P(("cgrp", "dev")), P("dev"))
    return jax.shard_map(
        make_body(mesh.shape["dev"], mesh.shape["cgrp"]),
        mesh=mesh, in_specs=in_specs, out_specs=out_specs, check_vma=False,
    )
```

```python
import functools
import math

import jax
import jax.numpy as jnp
from jax import lax
from jax.experimental import pallas as pl
from jax.experimental.pallas import tpu as pltpu
from jax.sharding import PartitionSpec as P

LANES = 128
VMEM = pl.BlockSpec(memory_space=pltpu.VMEM)
SMEM = pl.BlockSpec(memory_space=pltpu.SMEM)


def swap(x, axis, size, mask):
    return lax.ppermute(x, axis, [(i, i ^ mask) for i in range(size)])


def chip_plan(n):
    near = list(range(2, n - 2, 2))
    turned = near[len(near) // 2:] + near[:len(near) // 2]
    masks = list(zip(near, turned)) + [(n - 2, n - 2)]
    return [[(i, i ^ pair[i % 2] ^ 1) for i in range(n)] for pair in masks]


def group_plan(g):
    if g == 4:
        return [
            [(0, 1), (1, 0), (2, 3), (3, 2)],
            [(0, 3), (1, 2), (2, 0), (3, 1)],
            [(0, 2), (1, 3), (2, 1), (3, 0)],
        ]
    return [[(i, i ^ m) for i in range(g)] for m in range(1, g)]


def tree(parts, op):
    while len(parts) > 1:
        parts = [op(parts[i], parts[i + 1]) for i in range(0, len(parts), 2)]
    return parts[0]


def transpose_kernel(chunk, source_ref, follow_ref, docs_ref, own_ref, landing, sems):
    copies = []
    for i, start in enumerate(range(0, source_ref.shape[0], chunk)):
        here = pl.ds(start, chunk)
        copies.append(pltpu.make_async_copy(source_ref.at[here], landing.at[here], sems.at[i]))
        copies[-1].start()
    own_ref[...] = follow_ref[...]
    for i, copy in enumerate(copies):
        copy.wait()
        here = slice(i * chunk, (i + 1) * chunk)
        docs_ref[:, here] = landing[here, :].T


def load_kernel(source_ref, follow_ref, docs_ref, own_ref, sem):
    copy = pltpu.make_async_copy(source_ref, docs_ref, sem)
    copy.start()
    own_ref[...] = follow_ref[...]
    copy.wait()


def load(source, follow, chunk=0):
    count, width = source.shape
    kernel, dims, scratch = load_kernel, (count, width), [pltpu.SemaphoreType.DMA]
    if chunk:
        kernel, dims = functools.partial(transpose_kernel, chunk), (width, count)
        scratch = [
            pltpu.VMEM((count, width), source.dtype),
            pltpu.SemaphoreType.DMA((count // chunk,)),
        ]
    return pl.pallas_call(
        kernel,
        out_shape=[shape(dims, source.dtype), shape(follow.shape, follow.dtype)],
        in_specs=[pl.BlockSpec(memory_space=pltpu.HBM), VMEM],
        out_specs=[VMEM, VMEM],
        scratch_shapes=scratch,
        compiler_params=pltpu.CompilerParams(
            vmem_limit_bytes=(4 << 20) + (2 * source.nbytes if chunk else 0)
        ),
        cost_estimate=pl.CostEstimate(
            flops=0, bytes_accessed=2 * source.nbytes, transcendentals=0
        ),
    )(pltpu.with_memory_space_constraint(source, pltpu.HBM), follow)


def put_row(ref, start, row):
    for i in range(row.shape[1] // LANES):
        at = start // LANES + i
        ref[at:at + 1, :] = row[:, i * LANES:(i + 1) * LANES]


def scores_kernel(chunk, docs_ref, table_ref, part_ref, top_ref, sum_ref):
    width, count = docs_ref.shape
    scale = 4.0 / math.sqrt(width)
    table = table_ref[...]
    wide = table.astype(jnp.float32)
    half_norms = 0.5 * jnp.sum(wide * wide, axis=1, keepdims=True)
    for start in range(0, count, chunk):
        cols = slice(start, start + chunk)
        dots = jnp.dot(table, docs_ref[:, cols], preferred_element_type=jnp.float32)
        scores = (dots - half_norms) * scale
        top = jnp.max(scores, axis=0, keepdims=True)
        part = jnp.exp(scores - top)
        part_ref[:, cols] = part
        put_row(top_ref, start, top)
        put_row(sum_ref, start, jnp.sum(part, axis=0, keepdims=True))


def last_scores_kernel(
    chunk, docs_ref, table_ref, first_top_ref, first_sum_ref, part_ref, top_ref, lse_ref
):
    scores_kernel(chunk, docs_ref, table_ref, part_ref, top_ref, lse_ref)
    top = jnp.maximum(first_top_ref[...], top_ref[...])
    total = first_sum_ref[...] * jnp.exp(first_top_ref[...] - top)
    total += lse_ref[...] * jnp.exp(top_ref[...] - top)
    lse_ref[...] = top + jnp.log(total)


def weighted_sums(chunk, factor, docs_ref, part_ref, resp_ref, store):
    rows, count = part_ref.shape
    mass = jnp.zeros((rows, LANES), jnp.float32)
    for i in range(count // LANES):
        cols = slice(i * LANES, (i + 1) * LANES)
        resp = part_ref[:, cols] * factor[i:i + 1]
        mass += resp
        resp_ref[:, cols] = resp.astype(jnp.bfloat16)
    for start in range(0, docs_ref.shape[1], chunk):
        cols = slice(start, start + chunk)
        store(cols, jnp.dot(resp_ref[...], docs_ref[:, cols], preferred_element_type=jnp.float32))
    return jnp.sum(mass, axis=1, keepdims=True)


def mass_lanes(mass):
    high = mass.astype(jnp.bfloat16).astype(jnp.float32)
    lane = lax.broadcasted_iota(jnp.int32, (mass.shape[0], LANES), 1)
    lanes = jnp.where(lane == 0, high, jnp.where(lane == 1, mass - high, 0.0))
    return lanes.astype(jnp.bfloat16)


def read_rows(rows, width):
    wide = rows.astype(jnp.float32)
    return wide[:, :width], wide[:, width:width + 1] + wide[:, width + 1:width + 2]


def send_kernel(groups, plan, chunk, me_ref, lse_ref, *refs):
    got_refs = refs[:len(plan)]
    docs_ref, part_ref, top_ref, keep_top_ref = refs[len(plan):len(plan) + 4]
    doc_lse_ref, factor_ref, send_ref, resp_ref = refs[len(plan) + 4:]
    me = me_ref[0]
    parts = [lse_ref[...]] * groups
    for got_ref, pairs in zip(got_refs, plan):
        got = got_ref[...]
        for source, target in pairs:
            parts[source] = jnp.where(me == target, got, parts[source])
    best = tree(parts, jnp.maximum)
    doc_lse = best + jnp.log(tree([jnp.exp(x - best) for x in parts], jnp.add))
    doc_lse_ref[...] = doc_lse
    factor_ref[...] = jnp.exp(keep_top_ref[...] - doc_lse)
    factor = jnp.exp(top_ref[...] - doc_lse)

    def store(cols, term):
        send_ref[:, cols] = term.astype(jnp.bfloat16)

    mass = weighted_sums(chunk, factor, docs_ref, part_ref, resp_ref, store)
    send_ref[:, docs_ref.shape[1]:] = mass_lanes(mass)


def keep_kernel(chunk, factor_ref, docs_ref, part_ref, keep_ref, keep_mass_ref, resp_ref):
    def store(cols, term):
        keep_ref[:, cols] = term

    mass = weighted_sums(chunk, factor_ref[...], docs_ref, part_ref, resp_ref, store)
    keep_mass_ref[...] = jnp.broadcast_to(mass, keep_mass_ref.shape)


def fold_kernel(keep_ref, keep_mass_ref, got_ref, own_ref, own_mass_ref, *send_refs):
    rows, width = own_ref.shape
    for slot in range(keep_ref.shape[0] // rows):
        here = slice(slot * rows, (slot + 1) * rows)
        got, got_mass = read_rows(got_ref[here], width)
        term = keep_ref[here] + got
        mass = keep_mass_ref[here, :1] + got_mass
        if slot == 0:
            own_ref[...] = term
            own_mass_ref[...] = jnp.broadcast_to(mass, own_mass_ref.shape)
        else:
            send_refs[slot - 1][:, :width] = term.astype(jnp.bfloat16)
            send_refs[slot - 1][:, width:] = mass_lanes(mass)


def final_kernel(own_ref, own_mass_ref, cent_ref, *refs):
    *got_refs, next_ref, mass_ref = refs
    width = own_ref.shape[1]
    got = [read_rows(r[...], width) for r in got_refs]
    term = tree([own_ref[...]] + [a for a, _ in got], jnp.add)
    mass = tree([own_mass_ref[:, :1]] + [b for _, b in got], jnp.add)
    next_ref[...] = (term + cent_ref[...]) / (mass + 1.0)
    mass_ref[...] = jnp.broadcast_to(mass, (mass.shape[0], LANES)).T[:1]


def shape(dims, dtype=jnp.float32):
    return jax.ShapeDtypeStruct(dims, dtype)


def make_body(n, g):
    def body(docs, centroids):
        rows, width = centroids.shape
        count = docs.shape[0]
        half = rows * n // 2
        chunk = 256
        plan = group_plan(g)
        limit = (4 << 20) + half * (48 << 10)

        def call(kernel, outs, *args, scratch=(), flops=0):
            nbytes = sum(x.nbytes for x in args)
            return pl.pallas_call(
                kernel,
                out_shape=outs,
                in_specs=[SMEM if x.dtype == jnp.int32 else VMEM for x in args],
                out_specs=[VMEM] * len(outs),
                scratch_shapes=scratch,
                compiler_params=pltpu.CompilerParams(vmem_limit_bytes=limit),
                cost_estimate=pl.CostEstimate(
                    flops=flops, bytes_accessed=nbytes, transcendentals=0
                ),
            )(*args)

        flops = 2 * half * count * width
        stats = [shape((half, count)), shape((count // LANES, LANES)), shape((count // LANES, LANES))]
        resp = [pltpu.VMEM((half, count), jnp.bfloat16)]
        rounded = centroids.astype(jnp.bfloat16)
        routes = chip_plan(n)
        blocks = [lax.ppermute(rounded, "dev", pairs) for pairs in routes]
        docs_t, own = load(docs, rounded, chunk)
        mine = jnp.concatenate([own] + blocks, axis=0)
        theirs = swap(mine, "dev", n, 1)
        part, top, total = call(
            functools.partial(scores_kernel, chunk), stats, docs_t, mine, flops=flops
        )
        other_part, other_top, lse = call(
            functools.partial(last_scores_kernel, chunk), stats,
            docs_t, theirs, top, total, flops=flops,
        )
        others = [lax.ppermute(lse, "cgrp", pairs) for pairs in plan]
        docs, lse = load(docs, lse)
        doc_lse, factor, send = call(
            functools.partial(send_kernel, g, plan, chunk),
            [shape((count // LANES, LANES)), shape((count // LANES, LANES)), shape((half, width + LANES), jnp.bfloat16)],
            lax.axis_index("cgrp").reshape(1), lse, *others, docs, other_part, other_top, top,
            scratch=resp, flops=flops,
        )
        got = swap(send, "dev", n, 1)
        keep, keep_mass = call(
            functools.partial(keep_kernel, chunk),
            [shape((half, width)), shape((half, LANES))],
            factor, docs, part, scratch=resp, flops=flops,
        )
        own, own_mass, *sends = call(
            fold_kernel,
            [shape((rows, width)), shape((rows, LANES))]
            + [shape((rows, width + LANES), jnp.bfloat16)] * (n // 2 - 1),
            keep, keep_mass, got,
        )
        arrived = [
            lax.ppermute(x, "dev", [(target, source) for source, target in pairs])
            for x, pairs in zip(sends[-1:] + sends[:-1], routes[-1:] + routes[:-1])
        ]
        result, mass = call(
            final_kernel, [shape((rows, width)), shape((1, rows))],
            own, own_mass, centroids, *arrived,
        )
        return (result, mass.reshape(rows), doc_lse.reshape(count))

    return body


def solution(mesh):
    in_specs = (P("dev", None), P(("cgrp", "dev"), None))
    out_specs = (P(("cgrp", "dev"), None), P(("cgrp", "dev")), P("dev"))
    return jax.shard_map(
        make_body(mesh.shape["dev"], mesh.shape["cgrp"]),
        mesh=mesh, in_specs=in_specs, out_specs=out_specs, check_vma=False,
    )
```

```python
import functools
import math

import jax
import jax.numpy as jnp
from jax import lax
from jax.experimental import pallas as pl
from jax.experimental.pallas import tpu as pltpu
from jax.sharding import PartitionSpec as P

LANES = 128
VMEM = pl.BlockSpec(memory_space=pltpu.VMEM)
SMEM = pl.BlockSpec(memory_space=pltpu.SMEM)


def swap(x, axis, size, mask):
    return lax.ppermute(x, axis, [(i, i ^ mask) for i in range(size)])


def chip_plan(n):
    near = list(range(2, n - 2, 2))
    turned = near[len(near) // 2:] + near[:len(near) // 2]
    masks = [(n - 2, n - 2)] + list(zip(near, turned))
    return [[(i, i ^ pair[i % 2] ^ 1) for i in range(n)] for pair in masks]


def group_plan(g):
    if g == 4:
        return [
            [(0, 1), (1, 3), (2, 0), (3, 2)],
            [(0, 3), (1, 2), (2, 1), (3, 0)],
            [(0, 2), (1, 0), (2, 3), (3, 1)],
        ]
    return [[(i, i ^ m) for i in range(g)] for m in range(1, g)]


def tree(parts, op):
    while len(parts) > 1:
        parts = [op(parts[i], parts[i + 1]) for i in range(0, len(parts), 2)]
    return parts[0]


def load_kernel(chunk, source_ref, follow_ref, docs_t_ref, own_ref, *refs):
    *docs_refs, sems = refs
    size = docs_refs[0].shape[0]
    copies = []
    for start in range(0, source_ref.shape[0], chunk):
        target = docs_refs[start // size].at[pl.ds(start % size, chunk)]
        sem = sems.at[start // chunk]
        copies.append(pltpu.make_async_copy(source_ref.at[pl.ds(start, chunk)], target, sem))
        copies[-1].start()
    own_ref[...] = follow_ref[...]
    for i, copy in enumerate(copies):
        copy.wait()
        start = i * chunk
        landed = docs_refs[start // size][start % size:start % size + chunk, :]
        docs_t_ref[:, start:start + chunk] = landed.T


def load(source, follow, chunk, pieces):
    count, width = source.shape
    piece = shape((count // pieces, width), source.dtype)
    outs = [shape((width, count), source.dtype), shape(follow.shape, follow.dtype)]
    return pl.pallas_call(
        functools.partial(load_kernel, chunk),
        out_shape=outs + [piece] * pieces,
        in_specs=[pl.BlockSpec(memory_space=pltpu.HBM), VMEM],
        out_specs=[VMEM] * (2 + pieces),
        scratch_shapes=[pltpu.SemaphoreType.DMA((count // chunk,))],
        compiler_params=pltpu.CompilerParams(vmem_limit_bytes=(4 << 20) + 2 * source.nbytes),
        cost_estimate=pl.CostEstimate(
            flops=0, bytes_accessed=2 * source.nbytes, transcendentals=0
        ),
    )(pltpu.with_memory_space_constraint(source, pltpu.HBM), follow)


def put_row(ref, start, row):
    for i in range(row.shape[1] // LANES):
        at = start // LANES + i
        ref[at:at + 1, :] = row[:, i * LANES:(i + 1) * LANES]


def scores_kernel(chunk, docs_ref, table_ref, part_ref, top_ref, sum_ref):
    width, count = docs_ref.shape
    scale = 4.0 / math.sqrt(width)
    table = table_ref[...]
    wide = table.astype(jnp.float32)
    half_norms = 0.5 * jnp.sum(wide * wide, axis=1, keepdims=True)
    for start in range(0, count, chunk):
        cols = slice(start, start + chunk)
        dots = jnp.dot(table, docs_ref[:, cols], preferred_element_type=jnp.float32)
        scores = (dots - half_norms) * scale
        top = jnp.max(scores, axis=0, keepdims=True)
        part = jnp.exp(scores - top)
        part_ref[:, cols] = part
        put_row(top_ref, start, top)
        put_row(sum_ref, start, jnp.sum(part, axis=0, keepdims=True))


def last_scores_kernel(
    chunk, docs_ref, table_ref, first_top_ref, first_sum_ref, part_ref, top_ref, lse_ref
):
    scores_kernel(chunk, docs_ref, table_ref, part_ref, top_ref, lse_ref)
    top = jnp.maximum(first_top_ref[...], top_ref[...])
    total = first_sum_ref[...] * jnp.exp(first_top_ref[...] - top)
    total += lse_ref[...] * jnp.exp(top_ref[...] - top)
    lse_ref[...] = top + jnp.log(total)


def weighted_sums(chunk, factor, docs_refs, part_ref, resp_ref, store):
    rows, count = part_ref.shape
    mass = jnp.zeros((rows, LANES), jnp.float32)
    for i in range(count // LANES):
        cols = slice(i * LANES, (i + 1) * LANES)
        resp = part_ref[:, cols] * factor[i:i + 1]
        mass += resp
        resp_ref[:, cols] = resp.astype(jnp.bfloat16)
    size, width = docs_refs[0].shape
    for start in range(0, width, chunk):
        cols = slice(start, start + chunk)
        terms = [
            jnp.dot(
                resp_ref[:, i * size:(i + 1) * size], ref[:, cols],
                preferred_element_type=jnp.float32,
            )
            for i, ref in enumerate(docs_refs)
        ]
        store(cols, tree(terms, jnp.add))
    return jnp.sum(mass, axis=1, keepdims=True)


def mass_lanes(mass):
    high = mass.astype(jnp.bfloat16).astype(jnp.float32)
    lane = lax.broadcasted_iota(jnp.int32, (mass.shape[0], LANES), 1)
    lanes = jnp.where(lane == 0, high, jnp.where(lane == 1, mass - high, 0.0))
    return lanes.astype(jnp.bfloat16)


def read_rows(rows, width):
    wide = rows.astype(jnp.float32)
    return wide[:, :width], wide[:, width:width + 1] + wide[:, width + 1:width + 2]


def send_kernel(groups, plan, chunk, me_ref, lse_ref, part_ref, top_ref, keep_top_ref, *refs):
    got_refs, docs_refs = refs[:len(plan)], refs[len(plan):-4]
    doc_lse_ref, factor_ref, send_ref, resp_ref = refs[-4:]
    me = me_ref[0]
    parts = [lse_ref[...]] * groups
    for got_ref, pairs in zip(got_refs, plan):
        got = got_ref[...]
        for source, target in pairs:
            parts[source] = jnp.where(me == target, got, parts[source])
    best = tree(parts, jnp.maximum)
    doc_lse = best + jnp.log(tree([jnp.exp(x - best) for x in parts], jnp.add))
    doc_lse_ref[...] = doc_lse
    factor_ref[...] = jnp.exp(keep_top_ref[...] - doc_lse)
    factor = jnp.exp(top_ref[...] - doc_lse)

    def store(cols, term):
        send_ref[:, cols] = term.astype(jnp.bfloat16)

    mass = weighted_sums(chunk, factor, docs_refs, part_ref, resp_ref, store)
    send_ref[:, docs_refs[0].shape[1]:] = mass_lanes(mass)


def keep_kernel(chunk, factor_ref, part_ref, *refs):
    *docs_refs, keep_ref, keep_mass_ref, resp_ref = refs

    def store(cols, term):
        keep_ref[:, cols] = term

    mass = weighted_sums(chunk, factor_ref[...], docs_refs, part_ref, resp_ref, store)
    keep_mass_ref[...] = jnp.broadcast_to(mass, keep_mass_ref.shape)


def fold_kernel(keep_ref, keep_mass_ref, got_ref, own_ref, own_mass_ref, *send_refs):
    rows, width = own_ref.shape
    for slot in range(keep_ref.shape[0] // rows):
        here = slice(slot * rows, (slot + 1) * rows)
        got, got_mass = read_rows(got_ref[here], width)
        term = keep_ref[here] + got
        mass = keep_mass_ref[here, :1] + got_mass
        if slot == 0:
            own_ref[...] = term
            own_mass_ref[...] = jnp.broadcast_to(mass, own_mass_ref.shape)
        else:
            send_refs[slot - 1][:, :width] = term.astype(jnp.bfloat16)
            send_refs[slot - 1][:, width:] = mass_lanes(mass)


def final_kernel(own_ref, own_mass_ref, cent_ref, *refs):
    *got_refs, next_ref, mass_ref = refs
    width = own_ref.shape[1]
    got = [read_rows(r[...], width) for r in got_refs]
    term = tree([own_ref[...]] + [a for a, _ in got], jnp.add)
    mass = tree([own_mass_ref[:, :1]] + [b for _, b in got], jnp.add)
    next_ref[...] = (term + cent_ref[...]) / (mass + 1.0)
    mass_ref[...] = jnp.broadcast_to(mass, (mass.shape[0], LANES)).T[:1]


def shape(dims, dtype=jnp.float32):
    return jax.ShapeDtypeStruct(dims, dtype)


def make_body(n, g):
    def body(docs, centroids):
        rows, width = centroids.shape
        count = docs.shape[0]
        half = rows * n // 2
        chunk = 256
        plan = group_plan(g)
        limit = (4 << 20) + half * (48 << 10)

        def call(kernel, outs, *args, scratch=(), flops=0):
            nbytes = sum(x.nbytes for x in args)
            return pl.pallas_call(
                kernel,
                out_shape=outs,
                in_specs=[SMEM if x.dtype == jnp.int32 else VMEM for x in args],
                out_specs=[VMEM] * len(outs),
                scratch_shapes=scratch,
                compiler_params=pltpu.CompilerParams(vmem_limit_bytes=limit),
                cost_estimate=pl.CostEstimate(
                    flops=flops, bytes_accessed=nbytes, transcendentals=0
                ),
            )(*args)

        flops = 2 * half * count * width
        stats = [shape((half, count)), shape((count // LANES, LANES)), shape((count // LANES, LANES))]
        resp = [pltpu.VMEM((half, count), jnp.bfloat16)]
        rounded = centroids.astype(jnp.bfloat16)
        routes = chip_plan(n)
        blocks = [lax.ppermute(rounded, "dev", pairs) for pairs in routes]
        docs_t, own, *docs = load(docs, rounded, chunk, 4)
        mine = jnp.concatenate([own] + blocks, axis=0)
        theirs = swap(mine, "dev", n, 1)
        part, top, total = call(
            functools.partial(scores_kernel, chunk), stats, docs_t, mine, flops=flops
        )
        other_part, other_top, lse = call(
            functools.partial(last_scores_kernel, chunk), stats,
            docs_t, theirs, top, total, flops=flops,
        )
        others = [lax.ppermute(lse, "cgrp", pairs) for pairs in plan]
        doc_lse, factor, send = call(
            functools.partial(send_kernel, g, plan, chunk),
            [shape((count // LANES, LANES)), shape((count // LANES, LANES)), shape((half, width + LANES), jnp.bfloat16)],
            lax.axis_index("cgrp").reshape(1), lse, other_part, other_top, top, *others, *docs,
            scratch=resp, flops=flops,
        )
        got = swap(send, "dev", n, 1)
        keep, keep_mass = call(
            functools.partial(keep_kernel, chunk),
            [shape((half, width)), shape((half, LANES))],
            factor, part, *docs, scratch=resp, flops=flops,
        )
        own, own_mass, *sends = call(
            fold_kernel,
            [shape((rows, width)), shape((rows, LANES))]
            + [shape((rows, width + LANES), jnp.bfloat16)] * (n // 2 - 1),
            keep, keep_mass, got,
        )
        arrived = [
            lax.ppermute(x, "dev", [(target, source) for source, target in pairs])
            for x, pairs in zip(sends, routes)
        ]
        result, mass = call(
            final_kernel, [shape((rows, width)), shape((1, rows))],
            own, own_mass, centroids, *arrived,
        )
        return (result, mass.reshape(rows), doc_lse.reshape(count))

    return body


def solution(mesh):
    in_specs = (P("dev", None), P(("cgrp", "dev"), None))
    out_specs = (P(("cgrp", "dev"), None), P(("cgrp", "dev")), P("dev"))
    return jax.shard_map(
        make_body(mesh.shape["dev"], mesh.shape["cgrp"]),
        mesh=mesh, in_specs=in_specs, out_specs=out_specs, check_vma=False,
    )
```

```python
import functools
import math

import jax
import jax.numpy as jnp
from jax import lax
from jax.experimental import pallas as pl
from jax.experimental.pallas import tpu as pltpu
from jax.sharding import PartitionSpec as P

LANES = 128
VMEM = pl.BlockSpec(memory_space=pltpu.VMEM)
SMEM = pl.BlockSpec(memory_space=pltpu.SMEM)


def swap(x, axis, size, mask):
    return lax.ppermute(x, axis, [(i, i ^ mask) for i in range(size)])


def permute(x, n, even_mask, odd_mask):
    masks = (even_mask ^ 1, odd_mask ^ 1)
    return lax.ppermute(x, "dev", [(i, i ^ masks[i % 2]) for i in range(n)])


def group_plan(g):
    if g == 4:
        return [
            [(0, 1), (1, 0), (2, 3), (3, 2)],
            [(0, 3), (1, 2), (2, 0), (3, 1)],
            [(0, 2), (1, 3), (2, 1), (3, 0)],
        ]
    return [[(i, i ^ m) for i in range(g)] for m in range(1, g)]


def tree(parts, op):
    while len(parts) > 1:
        parts = [op(parts[i], parts[i + 1]) for i in range(0, len(parts), 2)]
    return parts[0]


def transpose_kernel(chunk, source_ref, follow_ref, docs_ref, own_ref, landing, sems):
    copies = []
    for i, start in enumerate(range(0, source_ref.shape[0], chunk)):
        here = pl.ds(start, chunk)
        copies.append(pltpu.make_async_copy(source_ref.at[here], landing.at[here], sems.at[i]))
        copies[-1].start()
    own_ref[...] = follow_ref[...]
    for i, copy in enumerate(copies):
        copy.wait()
        here = slice(i * chunk, (i + 1) * chunk)
        docs_ref[:, here] = landing[here, :].T


def load_kernel(source_ref, follow_ref, docs_ref, own_ref, sem):
    copy = pltpu.make_async_copy(source_ref, docs_ref, sem)
    copy.start()
    own_ref[...] = follow_ref[...]
    copy.wait()


def load(source, follow, chunk=0):
    count, width = source.shape
    kernel, dims, scratch = load_kernel, (count, width), [pltpu.SemaphoreType.DMA]
    if chunk:
        kernel, dims = functools.partial(transpose_kernel, chunk), (width, count)
        scratch = [
            pltpu.VMEM((count, width), source.dtype),
            pltpu.SemaphoreType.DMA((count // chunk,)),
        ]
    return pl.pallas_call(
        kernel,
        out_shape=[shape(dims, source.dtype), shape(follow.shape, follow.dtype)],
        in_specs=[pl.BlockSpec(memory_space=pltpu.HBM), VMEM],
        out_specs=[VMEM, VMEM],
        scratch_shapes=scratch,
        compiler_params=pltpu.CompilerParams(
            vmem_limit_bytes=(4 << 20) + (2 * source.nbytes if chunk else 0)
        ),
        cost_estimate=pl.CostEstimate(
            flops=0, bytes_accessed=2 * source.nbytes, transcendentals=0
        ),
    )(pltpu.with_memory_space_constraint(source, pltpu.HBM), follow)


def pair_kernel(own_ref, peer_ref, pair_ref, out_ref):
    rows = own_ref.shape[0]
    peer = peer_ref[...].astype(jnp.bfloat16)
    pair_ref[:rows, :] = own_ref[...]
    pair_ref[rows:, :] = peer
    out_ref[...] = peer


def put_row(ref, start, row):
    for i in range(row.shape[1] // LANES):
        at = start // LANES + i
        ref[at:at + 1, :] = row[:, i * LANES:(i + 1) * LANES]


def scores_kernel(chunk, docs_ref, *refs):
    *table_refs, part_ref, top_ref, sum_ref = refs
    width, count = docs_ref.shape
    scale = 4.0 / math.sqrt(width)
    table = jnp.concatenate([r[...] for r in table_refs], axis=0)
    wide = table.astype(jnp.float32)
    half_norms = 0.5 * jnp.sum(wide * wide, axis=1, keepdims=True)
    for start in range(0, count, chunk):
        cols = slice(start, start + chunk)
        dots = jnp.dot(table, docs_ref[:, cols], preferred_element_type=jnp.float32)
        scores = (dots - half_norms) * scale
        top = jnp.max(scores, axis=0, keepdims=True)
        part = jnp.exp(scores - top)
        part_ref[:, cols] = part
        put_row(top_ref, start, top)
        put_row(sum_ref, start, jnp.sum(part, axis=0, keepdims=True))


def last_scores_kernel(
    chunk, docs_ref, table_ref, first_top_ref, first_sum_ref, part_ref, top_ref, lse_ref
):
    scores_kernel(chunk, docs_ref, table_ref, part_ref, top_ref, lse_ref)
    top = jnp.maximum(first_top_ref[...], top_ref[...])
    total = first_sum_ref[...] * jnp.exp(first_top_ref[...] - top)
    total += lse_ref[...] * jnp.exp(top_ref[...] - top)
    lse_ref[...] = top + jnp.log(total)


def weighted_sums(chunk, blocks, docs_ref, resp_ref, store):
    masses, at = [], 0
    for part_ref, first, rows, factor in blocks:
        mass = jnp.zeros((rows, LANES), jnp.float32)
        for i in range(part_ref.shape[1] // LANES):
            cols = slice(i * LANES, (i + 1) * LANES)
            resp = part_ref[first:first + rows, cols] * factor[i:i + 1]
            mass += resp
            resp_ref[at:at + rows, cols] = resp.astype(jnp.bfloat16)
        masses.append(jnp.sum(mass, axis=1, keepdims=True))
        at += rows
    for start in range(0, docs_ref.shape[1], chunk):
        cols = slice(start, start + chunk)
        store(cols, jnp.dot(resp_ref[...], docs_ref[:, cols], preferred_element_type=jnp.float32))
    return jnp.concatenate(masses, axis=0)


def layout(rows, pairs):
    send = [(0, 1)] + [(1, 2 * k) for k in range(pairs)]
    send += [(0, 3 + 2 * k) for k in range(pairs)] + [(1, 2 * pairs)]
    keep = [(0, 0)] + [(0, 2 + 2 * k) for k in range(pairs)]
    keep += [(1, 1 + 2 * k) for k in range(pairs)] + [(0, 2 + 2 * pairs)]
    return [[(which, i * rows) for which, i in blocks] for blocks in (send, keep)]


def mass_lanes(mass):
    high = mass.astype(jnp.bfloat16).astype(jnp.float32)
    lane = lax.broadcasted_iota(jnp.int32, (mass.shape[0], LANES), 1)
    lanes = jnp.where(lane == 0, high, jnp.where(lane == 1, mass - high, 0.0))
    return lanes.astype(jnp.bfloat16)


def read_rows(rows, width):
    wide = rows.astype(jnp.float32)
    return wide[:, :width], wide[:, width:width + 1] + wide[:, width + 1:width + 2]


def send_kernel(groups, plan, chunk, rows, blocks, me_ref, lse_ref, *refs):
    got_refs = refs[:len(plan)]
    docs_ref, a_ref, b_ref, a_top_ref, b_top_ref = refs[len(plan):len(plan) + 5]
    doc_lse_ref, a_factor_ref, b_factor_ref, send_ref, resp_ref = refs[len(plan) + 5:]
    me = me_ref[0]
    parts = [lse_ref[...]] * groups
    for got_ref, pairs in zip(got_refs, plan):
        got = got_ref[...]
        for source, target in pairs:
            parts[source] = jnp.where(me == target, got, parts[source])
    best = tree(parts, jnp.maximum)
    doc_lse = best + jnp.log(tree([jnp.exp(x - best) for x in parts], jnp.add))
    doc_lse_ref[...] = doc_lse
    factors = [jnp.exp(r[...] - doc_lse) for r in (a_top_ref, b_top_ref)]
    a_factor_ref[...], b_factor_ref[...] = factors

    def store(cols, term):
        send_ref[:, cols] = term.astype(jnp.bfloat16)

    blocks = [((a_ref, b_ref)[which], first, rows, factors[which]) for which, first in blocks]
    mass = weighted_sums(chunk, blocks, docs_ref, resp_ref, store)
    send_ref[:, docs_ref.shape[1]:] = mass_lanes(mass)


def keep_kernel(
    chunk, rows, blocks, a_factor_ref, b_factor_ref, docs_ref, a_ref, b_ref,
    keep_ref, keep_mass_ref, resp_ref,
):
    factors = (a_factor_ref[...], b_factor_ref[...])

    def store(cols, term):
        keep_ref[:, cols] = term

    blocks = [((a_ref, b_ref)[which], first, rows, factors[which]) for which, first in blocks]
    mass = weighted_sums(chunk, blocks, docs_ref, resp_ref, store)
    keep_mass_ref[...] = jnp.broadcast_to(mass, keep_mass_ref.shape)


def fold_kernel(keep_ref, keep_mass_ref, got_ref, own_ref, own_mass_ref, *send_refs):
    rows, width = own_ref.shape
    for slot in range(keep_ref.shape[0] // rows):
        here = slice(slot * rows, (slot + 1) * rows)
        got, got_mass = read_rows(got_ref[here], width)
        term = keep_ref[here] + got
        mass = keep_mass_ref[here, :1] + got_mass
        if slot == 0:
            own_ref[...] = term
            own_mass_ref[...] = jnp.broadcast_to(mass, own_mass_ref.shape)
        else:
            send_refs[slot - 1][:, :width] = term.astype(jnp.bfloat16)
            send_refs[slot - 1][:, width:] = mass_lanes(mass)


def final_kernel(own_ref, own_mass_ref, cent_ref, *refs):
    *got_refs, next_ref, mass_ref = refs
    width = own_ref.shape[1]
    got = [read_rows(r[...], width) for r in got_refs]
    term = tree([own_ref[...]] + [a for a, _ in got], jnp.add)
    mass = tree([own_mass_ref[:, :1]] + [b for _, b in got], jnp.add)
    next_ref[...] = (term + cent_ref[...]) / (mass + 1.0)
    mass_ref[...] = jnp.broadcast_to(mass, (mass.shape[0], LANES)).T[:1]


def shape(dims, dtype=jnp.float32):
    return jax.ShapeDtypeStruct(dims, dtype)


def make_body(n, g):
    def body(docs, centroids):
        rows, width = centroids.shape
        count = docs.shape[0]
        half = rows * n // 2
        chunk = 256
        plan = group_plan(g)
        limit = (4 << 20) + half * (48 << 10)

        def call(kernel, outs, *args, scratch=(), flops=0):
            nbytes = sum(x.nbytes for x in args)
            return pl.pallas_call(
                kernel,
                out_shape=outs,
                in_specs=[SMEM if x.dtype == jnp.int32 else VMEM for x in args],
                out_specs=[VMEM] * len(outs),
                scratch_shapes=scratch,
                compiler_params=pltpu.CompilerParams(vmem_limit_bytes=limit),
                cost_estimate=pl.CostEstimate(
                    flops=flops, bytes_accessed=nbytes, transcendentals=0
                ),
            )(*args)

        flops = 2 * half * count * width
        stats = [shape((count // LANES, LANES))] * 2
        resp = [pltpu.VMEM((half, count), jnp.bfloat16)]
        rounded = centroids.astype(jnp.bfloat16)
        near = list(range(2, n - 2, 2))
        pairs = len(near) // 2
        near_even, near_odd = near[:pairs], near[pairs:]
        pair, peer = call(
            pair_kernel, [shape((2 * rows, width), jnp.bfloat16), shape(rounded.shape, jnp.bfloat16)],
            rounded, swap(centroids, "dev", n, 1),
        )
        far = permute(rounded, n, n - 2, n - 2)
        came = [permute(pair, n, x, y) for x, y in zip(near_even, near_odd)]
        docs_t, own = load(docs, rounded, chunk)
        came = jnp.concatenate(came + [far], axis=0)
        came, own = lax.optimization_barrier((came, own))
        theirs = swap(came, "dev", n, 1)
        a_rows, b_rows = 2 * rows + came.shape[0], came.shape[0]
        part_a, top_a, total = call(
            functools.partial(scores_kernel, chunk), [shape((a_rows, count))] + stats,
            docs_t, own, peer, came, flops=flops,
        )
        part_b, top_b, lse = call(
            functools.partial(last_scores_kernel, chunk), [shape((b_rows, count))] + stats,
            docs_t, theirs, top_a, total, flops=flops,
        )
        others = [lax.ppermute(lse, "cgrp", x) for x in plan]
        docs, lse = load(docs, lse)
        to_send, to_keep = layout(rows, pairs)
        doc_lse, factor_a, factor_b, send = call(
            functools.partial(send_kernel, g, plan, chunk, rows, to_send),
            [shape((count // LANES, LANES))] * 3 + [shape((half, width + LANES), jnp.bfloat16)],
            lax.axis_index("cgrp").reshape(1), lse, *others, docs, part_a, part_b, top_a, top_b,
            scratch=resp, flops=flops,
        )
        got = swap(send, "dev", n, 1)
        keep, keep_mass = call(
            functools.partial(keep_kernel, chunk, rows, to_keep),
            [shape((half, width)), shape((half, LANES))],
            factor_a, factor_b, docs, part_a, part_b, scratch=resp, flops=flops,
        )
        own, own_mass, *sends = call(
            fold_kernel,
            [shape((rows, width)), shape((rows, LANES))]
            + [shape((rows, width + LANES), jnp.bfloat16)] * (n // 2 - 1),
            keep, keep_mass, got,
        )
        masks = list(zip(near_odd + near_even, near_even + near_odd))
        masks = [(n - 2, n - 2)] + masks
        arrived = [permute(x, n, *m) for x, m in zip(sends[-1:] + sends[:-1], masks)]
        result, mass = call(
            final_kernel, [shape((rows, width)), shape((1, rows))],
            own, own_mass, centroids, *arrived,
        )
        return (result, mass.reshape(rows), doc_lse.reshape(count))

    return body


def solution(mesh):
    in_specs = (P("dev", None), P(("cgrp", "dev"), None))
    out_specs = (P(("cgrp", "dev"), None), P(("cgrp", "dev")), P("dev"))
    return jax.shard_map(
        make_body(mesh.shape["dev"], mesh.shape["cgrp"]),
        mesh=mesh, in_specs=in_specs, out_specs=out_specs, check_vma=False,
    )
```

```python
import functools
import math

import jax
import jax.numpy as jnp
from jax import lax
from jax.experimental import pallas as pl
from jax.experimental.pallas import tpu as pltpu
from jax.sharding import PartitionSpec as P

LANES = 128
VMEM = pl.BlockSpec(memory_space=pltpu.VMEM)
SMEM = pl.BlockSpec(memory_space=pltpu.SMEM)


def swap(x, axis, size, mask):
    return lax.ppermute(x, axis, [(i, i ^ mask) for i in range(size)])


def chip_plan(n):
    near = list(range(2, n - 2, 2))
    turned = near[len(near) // 2:] + near[:len(near) // 2]
    masks = list(zip(near, turned)) + [(n - 2, n - 2)]
    return [[(i, i ^ pair[i % 2] ^ 1) for i in range(n)] for pair in masks]


def group_plan(g):
    if g == 4:
        return [
            [(0, 1), (1, 0), (2, 3), (3, 2)],
            [(0, 3), (1, 2), (2, 0), (3, 1)],
            [(0, 2), (1, 3), (2, 1), (3, 0)],
        ]
    return [[(i, i ^ m) for i in range(g)] for m in range(1, g)]


def tree(parts, op):
    while len(parts) > 1:
        parts = [op(parts[i], parts[i + 1]) for i in range(0, len(parts), 2)]
    return parts[0]


def transpose_kernel(chunk, source_ref, follow_ref, docs_ref, own_ref, landing, sems):
    copies = []
    for i, start in enumerate(range(0, source_ref.shape[0], chunk)):
        here = pl.ds(start, chunk)
        copies.append(pltpu.make_async_copy(source_ref.at[here], landing.at[here], sems.at[i]))
        copies[-1].start()
    own_ref[...] = follow_ref[...]
    for i, copy in enumerate(copies):
        copy.wait()
        here = slice(i * chunk, (i + 1) * chunk)
        docs_ref[:, here] = landing[here, :].T


def load_kernel(source_ref, follow_ref, docs_ref, own_ref, sem):
    copy = pltpu.make_async_copy(source_ref, docs_ref, sem)
    copy.start()
    own_ref[...] = follow_ref[...]
    copy.wait()


def load(source, follow, chunk=0):
    count, width = source.shape
    kernel, dims, scratch = load_kernel, (count, width), [pltpu.SemaphoreType.DMA]
    if chunk:
        kernel, dims = functools.partial(transpose_kernel, chunk), (width, count)
        scratch = [
            pltpu.VMEM((count, width), source.dtype),
            pltpu.SemaphoreType.DMA((count // chunk,)),
        ]
    return pl.pallas_call(
        kernel,
        out_shape=[shape(dims, source.dtype), shape(follow.shape, follow.dtype)],
        in_specs=[pl.BlockSpec(memory_space=pltpu.HBM), VMEM],
        out_specs=[VMEM, VMEM],
        scratch_shapes=scratch,
        compiler_params=pltpu.CompilerParams(
            vmem_limit_bytes=(4 << 20) + (2 * source.nbytes if chunk else 0)
        ),
        cost_estimate=pl.CostEstimate(
            flops=0, bytes_accessed=2 * source.nbytes, transcendentals=0
        ),
    )(pltpu.with_memory_space_constraint(source, pltpu.HBM), follow)


def put_row(ref, start, row):
    for i in range(row.shape[1] // LANES):
        at = start // LANES + i
        ref[at:at + 1, :] = row[:, i * LANES:(i + 1) * LANES]


def scores_kernel(chunk, docs_ref, *refs):
    *table_refs, part_ref, top_ref, sum_ref = refs
    width, count = docs_ref.shape
    scale = 4.0 / math.sqrt(width)
    table = jnp.concatenate([r[...] for r in table_refs], axis=0)
    wide = table.astype(jnp.float32)
    half_norms = 0.5 * jnp.sum(wide * wide, axis=1, keepdims=True)
    for start in range(0, count, chunk):
        cols = slice(start, start + chunk)
        dots = jnp.dot(table, docs_ref[:, cols], preferred_element_type=jnp.float32)
        scores = (dots - half_norms) * scale
        top = jnp.max(scores, axis=0, keepdims=True)
        part = jnp.exp(scores - top)
        part_ref[:, cols] = part
        put_row(top_ref, start, top)
        put_row(sum_ref, start, jnp.sum(part, axis=0, keepdims=True))


def last_scores_kernel(
    chunk, docs_ref, one_ref, two_ref, first_top_ref, first_sum_ref, part_ref, top_ref, lse_ref
):
    scores_kernel(chunk, docs_ref, one_ref, two_ref, part_ref, top_ref, lse_ref)
    top = jnp.maximum(first_top_ref[...], top_ref[...])
    total = first_sum_ref[...] * jnp.exp(first_top_ref[...] - top)
    total += lse_ref[...] * jnp.exp(top_ref[...] - top)
    lse_ref[...] = top + jnp.log(total)


def weighted_sums(chunk, factor, docs_ref, part_ref, resp_ref, store):
    rows, count = part_ref.shape
    mass = jnp.zeros((rows, LANES), jnp.float32)
    for i in range(count // LANES):
        cols = slice(i * LANES, (i + 1) * LANES)
        resp = part_ref[:, cols] * factor[i:i + 1]
        mass += resp
        resp_ref[:, cols] = resp.astype(jnp.bfloat16)
    for start in range(0, docs_ref.shape[1], chunk):
        cols = slice(start, start + chunk)
        store(cols, jnp.dot(resp_ref[...], docs_ref[:, cols], preferred_element_type=jnp.float32))
    return jnp.sum(mass, axis=1, keepdims=True)


def mass_lanes(mass):
    high = mass.astype(jnp.bfloat16).astype(jnp.float32)
    lane = lax.broadcasted_iota(jnp.int32, (mass.shape[0], LANES), 1)
    lanes = jnp.where(lane == 0, high, jnp.where(lane == 1, mass - high, 0.0))
    return lanes.astype(jnp.bfloat16)


def read_rows(rows, width):
    wide = rows.astype(jnp.float32)
    return wide[:, :width], wide[:, width:width + 1] + wide[:, width + 1:width + 2]


def send_kernel(groups, plan, chunk, me_ref, lse_ref, *refs):
    got_refs = refs[:len(plan)]
    docs_ref, part_ref, top_ref, keep_top_ref = refs[len(plan):len(plan) + 4]
    doc_lse_ref, factor_ref, one_ref, two_ref, resp_ref = refs[len(plan) + 4:]
    me = me_ref[0]
    parts = [lse_ref[...]] * groups
    for got_ref, pairs in zip(got_refs, plan):
        got = got_ref[...]
        for source, target in pairs:
            parts[source] = jnp.where(me == target, got, parts[source])
    best = tree(parts, jnp.maximum)
    doc_lse = best + jnp.log(tree([jnp.exp(x - best) for x in parts], jnp.add))
    doc_lse_ref[...] = doc_lse
    factor_ref[...] = jnp.exp(keep_top_ref[...] - doc_lse)
    factor = jnp.exp(top_ref[...] - doc_lse)

    def store(cols, term):
        term = term.astype(jnp.bfloat16)
        one_ref[:, cols] = term[:one_ref.shape[0]]
        two_ref[:, cols] = term[one_ref.shape[0]:]

    mass = weighted_sums(chunk, factor, docs_ref, part_ref, resp_ref, store)
    width = docs_ref.shape[1]
    store(slice(width, width + LANES), mass_lanes(mass))


def keep_kernel(chunk, factor_ref, docs_ref, part_ref, keep_ref, keep_mass_ref, resp_ref):
    def store(cols, term):
        keep_ref[:, cols] = term

    mass = weighted_sums(chunk, factor_ref[...], docs_ref, part_ref, resp_ref, store)
    keep_mass_ref[...] = jnp.broadcast_to(mass, keep_mass_ref.shape)


def fold_kernel(keep_ref, keep_mass_ref, one_ref, two_ref, own_ref, own_mass_ref, *send_refs):
    rows, width = own_ref.shape
    for slot in range(keep_ref.shape[0] // rows):
        here = slice(slot * rows, (slot + 1) * rows)
        first = one_ref.shape[0]
        there = here if here.start < first else slice(here.start - first, here.stop - first)
        got_ref = one_ref if here.start < first else two_ref
        got, got_mass = read_rows(got_ref[there], width)
        term = keep_ref[here] + got
        mass = keep_mass_ref[here, :1] + got_mass
        if slot == 0:
            own_ref[...] = term
            own_mass_ref[...] = jnp.broadcast_to(mass, own_mass_ref.shape)
        else:
            send_refs[slot - 1][:, :width] = term.astype(jnp.bfloat16)
            send_refs[slot - 1][:, width:] = mass_lanes(mass)


def final_kernel(own_ref, own_mass_ref, cent_ref, *refs):
    *got_refs, next_ref, mass_ref = refs
    width = own_ref.shape[1]
    got = [read_rows(r[...], width) for r in got_refs]
    term = tree([own_ref[...]] + [a for a, _ in got], jnp.add)
    mass = tree([own_mass_ref[:, :1]] + [b for _, b in got], jnp.add)
    next_ref[...] = (term + cent_ref[...]) / (mass + 1.0)
    mass_ref[...] = jnp.broadcast_to(mass, (mass.shape[0], LANES)).T[:1]


def shape(dims, dtype=jnp.float32):
    return jax.ShapeDtypeStruct(dims, dtype)


def make_body(n, g):
    def body(docs, centroids):
        rows, width = centroids.shape
        count = docs.shape[0]
        half = rows * n // 2
        chunk = 256
        plan = group_plan(g)
        limit = (4 << 20) + half * (48 << 10)

        def call(kernel, outs, *args, scratch=(), flops=0):
            nbytes = sum(x.nbytes for x in args)
            return pl.pallas_call(
                kernel,
                out_shape=outs,
                in_specs=[SMEM if x.dtype == jnp.int32 else VMEM for x in args],
                out_specs=[VMEM] * len(outs),
                scratch_shapes=scratch,
                compiler_params=pltpu.CompilerParams(vmem_limit_bytes=limit),
                cost_estimate=pl.CostEstimate(
                    flops=flops, bytes_accessed=nbytes, transcendentals=0
                ),
            )(*args)

        flops = 2 * half * count * width
        stats = [shape((half, count)), shape((count // LANES, LANES)), shape((count // LANES, LANES))]
        resp = [pltpu.VMEM((half, count), jnp.bfloat16)]
        rounded = centroids.astype(jnp.bfloat16)
        routes = chip_plan(n)
        blocks = [lax.ppermute(rounded, "dev", pairs) for pairs in routes]
        docs_t, own = load(docs, rounded, chunk)
        blocks = [own] + blocks
        mine = [jnp.concatenate(x, axis=0) for x in (blocks[:n // 4], blocks[n // 4:])]
        theirs = [swap(x, "dev", n, 1) for x in mine]
        part, top, total = call(
            functools.partial(scores_kernel, chunk), stats, docs_t, *mine, flops=flops
        )
        other_part, other_top, lse = call(
            functools.partial(last_scores_kernel, chunk), stats,
            docs_t, *theirs, top, total, flops=flops,
        )
        others = [lax.ppermute(lse, "cgrp", pairs) for pairs in plan]
        docs, lse = load(docs, lse)
        doc_lse, factor, *send = call(
            functools.partial(send_kernel, g, plan, chunk),
            [shape((count // LANES, LANES)), shape((count // LANES, LANES))]
            + [shape((half // 2, width + LANES), jnp.bfloat16)] * 2,
            lax.axis_index("cgrp").reshape(1), lse, *others, docs, other_part, other_top, top,
            scratch=resp, flops=flops,
        )
        got = [swap(x, "dev", n, 1) for x in send]
        keep, keep_mass = call(
            functools.partial(keep_kernel, chunk),
            [shape((half, width)), shape((half, LANES))],
            factor, docs, part, scratch=resp, flops=flops,
        )
        own, own_mass, *sends = call(
            fold_kernel,
            [shape((rows, width)), shape((rows, LANES))]
            + [shape((rows, width + LANES), jnp.bfloat16)] * (n // 2 - 1),
            keep, keep_mass, *got,
        )
        arrived = [
            lax.ppermute(x, "dev", [(target, source) for source, target in pairs])
            for x, pairs in zip(sends[-1:] + sends[:-1], routes[-1:] + routes[:-1])
        ]
        result, mass = call(
            final_kernel, [shape((rows, width)), shape((1, rows))],
            own, own_mass, centroids, *arrived,
        )
        return (result, mass.reshape(rows), doc_lse.reshape(count))

    return body


def solution(mesh):
    in_specs = (P("dev", None), P(("cgrp", "dev"), None))
    out_specs = (P(("cgrp", "dev"), None), P(("cgrp", "dev")), P("dev"))
    return jax.shard_map(
        make_body(mesh.shape["dev"], mesh.shape["cgrp"]),
        mesh=mesh, in_specs=in_specs, out_specs=out_specs, check_vma=False,
    )
```

```python
import functools
import math

import jax
import jax.numpy as jnp
from jax import lax
from jax.experimental import pallas as pl
from jax.experimental.pallas import tpu as pltpu
from jax.sharding import PartitionSpec as P

LANES = 128
VMEM = pl.BlockSpec(memory_space=pltpu.VMEM)
SMEM = pl.BlockSpec(memory_space=pltpu.SMEM)


def swap(x, axis, size, mask):
    return lax.ppermute(x, axis, [(i, i ^ mask) for i in range(size)])


def chip_plan(n):
    near = list(range(2, n - 2, 2))
    turned = near[len(near) // 2:] + near[:len(near) // 2]
    masks = [(n - 2, n - 2)] + list(zip(near, turned))
    return [[(i, i ^ pair[i % 2] ^ 1) for i in range(n)] for pair in masks]


def group_plan(g):
    if g == 4:
        return [
            [(0, 2), (1, 3), (2, 1), (3, 0)],
            [(0, 3), (1, 2), (2, 0), (3, 1)],
            [(0, 1), (1, 0), (2, 3), (3, 2)],
        ]
    return [[(i, i ^ m) for i in range(g)] for m in range(1, g)]


def tree(parts, op):
    while len(parts) > 1:
        parts = [op(parts[i], parts[i + 1]) for i in range(0, len(parts), 2)]
    return parts[0]


def transpose_kernel(chunk, source_ref, follow_ref, docs_ref, own_ref, landing, sems):
    copies = []
    for i, start in enumerate(range(0, source_ref.shape[0], chunk)):
        here = pl.ds(start, chunk)
        copies.append(pltpu.make_async_copy(source_ref.at[here], landing.at[here], sems.at[i]))
        copies[-1].start()
    own_ref[...] = follow_ref[...]
    for i, copy in enumerate(copies):
        copy.wait()
        here = slice(i * chunk, (i + 1) * chunk)
        docs_ref[:, here] = landing[here, :].T


def load_kernel(*refs):
    half = len(refs) // 2
    sources, follow_ref = refs[:half - 1], refs[half - 1]
    targets, own_ref, sems = refs[half:-2], refs[-2], refs[-1]
    copies = [
        pltpu.make_async_copy(source, target, sems.at[i])
        for i, (source, target) in enumerate(zip(sources, targets))
    ]
    for copy in copies:
        copy.start()
    own_ref[...] = follow_ref[...]
    for copy in copies:
        copy.wait()


def load(sources, follow, chunk=0):
    kernel, dims = load_kernel, sources[0].shape
    scratch = [pltpu.SemaphoreType.DMA((len(sources),))]
    if chunk:
        kernel, (count, width) = functools.partial(transpose_kernel, chunk), dims
        dims = (width, count)
        scratch = [
            pltpu.VMEM((count, width), follow.dtype),
            pltpu.SemaphoreType.DMA((count // chunk,)),
        ]
    size = sum(x.nbytes for x in sources)
    return pl.pallas_call(
        kernel,
        out_shape=[shape(dims, x.dtype) for x in sources] + [shape(follow.shape, follow.dtype)],
        in_specs=[pl.BlockSpec(memory_space=pltpu.HBM)] * len(sources) + [VMEM],
        out_specs=[VMEM] * (len(sources) + 1),
        scratch_shapes=scratch,
        compiler_params=pltpu.CompilerParams(
            vmem_limit_bytes=(4 << 20) + (2 * size if chunk else 0)
        ),
        cost_estimate=pl.CostEstimate(flops=0, bytes_accessed=2 * size, transcendentals=0),
    )(*[pltpu.with_memory_space_constraint(x, pltpu.HBM) for x in sources], follow)


def put_row(ref, start, row):
    for i in range(row.shape[1] // LANES):
        at = start // LANES + i
        ref[at:at + 1, :] = row[:, i * LANES:(i + 1) * LANES]


def scores_kernel(chunk, docs_ref, table_ref, part_ref, top_ref, sum_ref):
    width, count = docs_ref.shape
    scale = 4.0 / math.sqrt(width)
    table = table_ref[...]
    wide = table.astype(jnp.float32)
    half_norms = 0.5 * jnp.sum(wide * wide, axis=1, keepdims=True)
    for start in range(0, count, chunk):
        cols = slice(start, start + chunk)
        dots = jnp.dot(table, docs_ref[:, cols], preferred_element_type=jnp.float32)
        scores = (dots - half_norms) * scale
        top = jnp.max(scores, axis=0, keepdims=True)
        part = jnp.exp(scores - top)
        part_ref[:, cols] = part.astype(part_ref.dtype)
        put_row(top_ref, start, top)
        put_row(sum_ref, start, jnp.sum(part, axis=0, keepdims=True))


def last_scores_kernel(
    chunk, docs_ref, table_ref, first_top_ref, first_sum_ref, part_ref, top_ref, lse_ref
):
    scores_kernel(chunk, docs_ref, table_ref, part_ref, top_ref, lse_ref)
    top = jnp.maximum(first_top_ref[...], top_ref[...])
    total = first_sum_ref[...] * jnp.exp(first_top_ref[...] - top)
    total += lse_ref[...] * jnp.exp(top_ref[...] - top)
    lse_ref[...] = top + jnp.log(total)


def weighted_sums(chunk, factor, docs_ref, part_ref, resp_ref, store):
    rows, count = part_ref.shape
    mass = jnp.zeros((rows, LANES), jnp.float32)
    for i in range(count // LANES):
        cols = slice(i * LANES, (i + 1) * LANES)
        resp = part_ref[:, cols].astype(jnp.float32) * factor[i:i + 1]
        mass += resp
        resp_ref[:, cols] = resp.astype(jnp.bfloat16)
    for start in range(0, docs_ref.shape[1], chunk):
        cols = slice(start, start + chunk)
        store(cols, jnp.dot(resp_ref[...], docs_ref[:, cols], preferred_element_type=jnp.float32))
    return jnp.sum(mass, axis=1, keepdims=True)


def mass_lanes(mass):
    high = mass.astype(jnp.bfloat16).astype(jnp.float32)
    lane = lax.broadcasted_iota(jnp.int32, (mass.shape[0], LANES), 1)
    lanes = jnp.where(lane == 0, high, jnp.where(lane == 1, mass - high, 0.0))
    return lanes.astype(jnp.bfloat16)


def read_rows(rows, width):
    wide = rows.astype(jnp.float32)
    return wide[:, :width], wide[:, width:width + 1] + wide[:, width + 1:width + 2]


def factors_kernel(groups, plan, me_ref, lse_ref, *refs):
    got_refs = refs[:len(plan)]
    top_ref, their_top_ref, doc_lse_ref, factor_ref, send_ref = refs[len(plan):]
    me = me_ref[0]
    parts = [lse_ref[...]] * groups
    for got_ref, pairs in zip(got_refs, plan):
        got = got_ref[...]
        for source, target in pairs:
            parts[source] = jnp.where(me == target, got, parts[source])
    best = tree(parts, jnp.maximum)
    doc_lse = best + jnp.log(tree([jnp.exp(x - best) for x in parts], jnp.add))
    doc_lse_ref[...] = doc_lse
    factor_ref[...] = jnp.exp(top_ref[...] - doc_lse)
    send_ref[...] = jnp.exp(their_top_ref[...] - doc_lse)


def first_sums_kernel(chunk, factor_ref, docs_ref, part_ref, sum_ref, mass_ref, resp_ref):
    def store(cols, term):
        sum_ref[:, cols] = term

    mass = weighted_sums(chunk, factor_ref[...], docs_ref, part_ref, resp_ref, store)
    mass_ref[...] = jnp.broadcast_to(mass, mass_ref.shape)


def second_sums_kernel(
    chunk, factor_ref, docs_ref, part_ref, sum_ref, mass_ref, own_ref, own_mass_ref, *refs
):
    *send_refs, resp_ref = refs
    rows, width = own_ref.shape

    def store(cols, term):
        if cols.start < width:
            term += sum_ref[:, cols]
            own_ref[:, cols] = term[:rows]
        for slot, ref in enumerate(send_refs, 1):
            ref[:, cols] = term[slot * rows:(slot + 1) * rows].astype(jnp.bfloat16)

    mass = weighted_sums(chunk, factor_ref[...], docs_ref, part_ref, resp_ref, store)
    mass += mass_ref[:, :1]
    own_mass_ref[...] = jnp.broadcast_to(mass[:rows], own_mass_ref.shape)
    store(slice(width, width + LANES), mass_lanes(mass))


def final_kernel(own_ref, own_mass_ref, cent_ref, lse_ref, *refs):
    *got_refs, next_ref, mass_ref, doc_lse_ref = refs
    doc_lse_ref[...] = lse_ref[...]
    width = own_ref.shape[1]
    got = [read_rows(r[...], width) for r in got_refs]
    term = tree([own_ref[...]] + [a for a, _ in got], jnp.add)
    mass = tree([own_mass_ref[:, :1]] + [b for _, b in got], jnp.add)
    next_ref[...] = (term + cent_ref[...]) / (mass + 1.0)
    mass_ref[...] = jnp.broadcast_to(mass, (mass.shape[0], LANES)).T[:1]


def shape(dims, dtype=jnp.float32):
    return jax.ShapeDtypeStruct(dims, dtype)


def make_body(n, g):
    def body(docs, centroids):
        rows, width = centroids.shape
        count = docs.shape[0]
        half = rows * n // 2
        chunk = 256
        plan = group_plan(g)
        limit = (4 << 20) + half * (48 << 10)

        def call(kernel, outs, *args, scratch=(), flops=0):
            nbytes = sum(x.nbytes for x in args)
            return pl.pallas_call(
                kernel,
                out_shape=outs,
                in_specs=[SMEM if x.dtype == jnp.int32 else VMEM for x in args],
                out_specs=[VMEM] * len(outs),
                scratch_shapes=scratch,
                compiler_params=pltpu.CompilerParams(vmem_limit_bytes=limit),
                cost_estimate=pl.CostEstimate(
                    flops=flops, bytes_accessed=nbytes, transcendentals=0
                ),
            )(*args)

        flops = 2 * half * count * width
        stats = [shape((count // LANES, LANES)), shape((count // LANES, LANES))]
        resp = [pltpu.VMEM((half, count), jnp.bfloat16)]
        rounded = centroids.astype(jnp.bfloat16)
        routes = chip_plan(n)
        blocks = [lax.ppermute(rounded, "dev", pairs) for pairs in routes]
        their_docs = swap(docs, "dev", n, 1)
        docs_t, own = load([docs], rounded, chunk)
        mine = jnp.concatenate([own] + blocks, axis=0)
        theirs = swap(mine, "dev", n, 1)
        part, top, total = call(
            functools.partial(scores_kernel, chunk), [shape((half, count))] + stats,
            docs_t, mine, flops=flops,
        )
        other_part, other_top, lse = call(
            functools.partial(last_scores_kernel, chunk),
            [shape((half, count), jnp.bfloat16)] + stats,
            docs_t, theirs, top, total, flops=flops,
        )
        others = [lax.ppermute(lse, "cgrp", pairs) for pairs in plan]
        their_part = swap(other_part, "dev", n, 1)
        docs, their_docs, lse = load([docs, their_docs], lse)
        doc_lse, factor, their_factor = call(
            functools.partial(factors_kernel, g, plan), [shape((count // LANES, LANES))] * 3,
            lax.axis_index("cgrp").reshape(1), lse, *others, top, other_top,
        )
        their_factor = swap(their_factor, "dev", n, 1)
        sums, mass = call(
            functools.partial(first_sums_kernel, chunk),
            [shape((half, width)), shape((half, LANES))],
            factor, docs, part, scratch=resp, flops=flops,
        )
        own, own_mass, *sends = call(
            functools.partial(second_sums_kernel, chunk),
            [shape((rows, width)), shape((rows, LANES))]
            + [shape((rows, width + LANES), jnp.bfloat16)] * (n // 2 - 1),
            their_factor, their_docs, their_part, sums, mass, scratch=resp, flops=flops,
        )
        arrived = [
            lax.ppermute(x, "dev", [(target, source) for source, target in pairs])
            for x, pairs in zip(sends, routes)
        ]
        result, mass, doc_lse = call(
            final_kernel, [shape((rows, width)), shape((1, rows)), shape(doc_lse.shape)],
            own, own_mass, centroids, doc_lse, *arrived,
        )
        return (result, mass.reshape(rows), doc_lse.reshape(count))

    return body


def solution(mesh):
    in_specs = (P("dev", None), P(("cgrp", "dev"), None))
    out_specs = (P(("cgrp", "dev"), None), P(("cgrp", "dev")), P("dev"))
    return jax.shard_map(
        make_body(mesh.shape["dev"], mesh.shape["cgrp"]),
        mesh=mesh, in_specs=in_specs, out_specs=out_specs, check_vma=False,
    )
```

```python
import functools
import math

import jax
import jax.numpy as jnp
from jax import lax
from jax.experimental import pallas as pl
from jax.experimental.pallas import tpu as pltpu
from jax.sharding import PartitionSpec as P

LANES = 128
VMEM = pl.BlockSpec(memory_space=pltpu.VMEM)
SMEM = pl.BlockSpec(memory_space=pltpu.SMEM)


def swap(x, axis, size, mask):
    return lax.ppermute(x, axis, [(i, i ^ mask) for i in range(size)])


def chip_plan(n):
    near = list(range(2, n - 2, 2))
    turned = near[len(near) // 2:] + near[:len(near) // 2]
    masks = list(zip(near, turned)) + [(n - 2, n - 2)]
    return [[(i, i ^ pair[i % 2] ^ 1) for i in range(n)] for pair in masks]


def group_plan(g):
    if g == 4:
        return [
            [(0, 1), (1, 0), (2, 3), (3, 2)],
            [(0, 3), (1, 2), (2, 0), (3, 1)],
            [(0, 2), (1, 3), (2, 1), (3, 0)],
        ]
    return [[(i, i ^ m) for i in range(g)] for m in range(1, g)]


def tree(parts, op):
    while len(parts) > 1:
        parts = [op(parts[i], parts[i + 1]) for i in range(0, len(parts), 2)]
    return parts[0]


def transpose_kernel(chunk, source_ref, follow_ref, docs_ref, own_ref, landing, sems):
    copies = []
    for i, start in enumerate(range(0, source_ref.shape[0], chunk)):
        here = pl.ds(start, chunk)
        copies.append(pltpu.make_async_copy(source_ref.at[here], landing.at[here], sems.at[i]))
        copies[-1].start()
    own_ref[...] = follow_ref[...]
    for i, copy in enumerate(copies):
        copy.wait()
        here = slice(i * chunk, (i + 1) * chunk)
        docs_ref[:, here] = landing[here, :].T


def load_kernel(*refs):
    half = len(refs) // 2
    sources, follow_ref = refs[:half - 1], refs[half - 1]
    targets, own_ref, sems = refs[half:-2], refs[-2], refs[-1]
    copies = [
        pltpu.make_async_copy(source.at[pl.ds(0, target.shape[0])], target, sems.at[i])
        for i, (source, target) in enumerate(zip(sources, targets))
    ]
    for copy in copies:
        copy.start()
    own_ref[...] = follow_ref[...]
    for copy in copies:
        copy.wait()


def load(sources, follow, chunk=0, last_rows=0):
    kernel, dims = load_kernel, sources[0].shape
    scratch = [pltpu.SemaphoreType.DMA((len(sources),))]
    if chunk:
        kernel, (count, width) = functools.partial(transpose_kernel, chunk), dims
        dims = (width, count)
        scratch = [
            pltpu.VMEM((count, width), follow.dtype),
            pltpu.SemaphoreType.DMA((count // chunk,)),
        ]
    outs = [shape(dims, x.dtype) for x in sources]
    if last_rows:
        outs[-1] = shape((last_rows, dims[1]), sources[-1].dtype)
    size = sum(x.nbytes for x in sources)
    return pl.pallas_call(
        kernel,
        out_shape=outs + [shape(follow.shape, follow.dtype)],
        in_specs=[pl.BlockSpec(memory_space=pltpu.HBM)] * len(sources) + [VMEM],
        out_specs=[VMEM] * (len(sources) + 1),
        scratch_shapes=scratch,
        compiler_params=pltpu.CompilerParams(
            vmem_limit_bytes=(4 << 20) + (2 * size if chunk else 0)
        ),
        cost_estimate=pl.CostEstimate(flops=0, bytes_accessed=2 * size, transcendentals=0),
    )(*[pltpu.with_memory_space_constraint(x, pltpu.HBM) for x in sources], follow)


def put_row(ref, start, row):
    for i in range(row.shape[1] // LANES):
        at = start // LANES + i
        ref[at:at + 1, :] = row[:, i * LANES:(i + 1) * LANES]


def scores_kernel(chunk, docs_ref, table_ref, part_ref, top_ref, sum_ref):
    width, count = docs_ref.shape
    scale = 4.0 / math.sqrt(width)
    table = table_ref[...]
    wide = table.astype(jnp.float32)
    half_norms = 0.5 * jnp.sum(wide * wide, axis=1, keepdims=True)
    for start in range(0, count, chunk):
        cols = slice(start, start + chunk)
        dots = jnp.dot(table, docs_ref[:, cols], preferred_element_type=jnp.float32)
        scores = (dots - half_norms) * scale
        top = jnp.max(scores, axis=0, keepdims=True)
        part = jnp.exp(scores - top)
        part_ref[:, cols] = part.astype(part_ref.dtype)
        put_row(top_ref, start, top)
        put_row(sum_ref, start, jnp.sum(part, axis=0, keepdims=True))


def last_scores_kernel(
    chunk, docs_ref, table_ref, first_top_ref, first_sum_ref, part_ref, top_ref, lse_ref
):
    scores_kernel(chunk, docs_ref, table_ref, part_ref, top_ref, lse_ref)
    top = jnp.maximum(first_top_ref[...], top_ref[...])
    total = first_sum_ref[...] * jnp.exp(first_top_ref[...] - top)
    total += lse_ref[...] * jnp.exp(top_ref[...] - top)
    lse_ref[...] = top + jnp.log(total)


def weighted_sums(chunk, factor, docs_refs, part_ref, resp_ref, store):
    rows, count = part_ref.shape
    mass = jnp.zeros((rows, LANES), jnp.float32)
    for i in range(count // LANES):
        cols = slice(i * LANES, (i + 1) * LANES)
        resp = part_ref[:, cols].astype(jnp.float32) * factor[i:i + 1]
        mass += resp
        resp_ref[:, cols] = resp.astype(jnp.bfloat16)
    for start in range(0, docs_refs[0].shape[1], chunk):
        cols = slice(start, start + chunk)
        term, first = 0.0, 0
        for ref in docs_refs:
            here = slice(first, first + ref.shape[0])
            term += jnp.dot(resp_ref[:, here], ref[:, cols], preferred_element_type=jnp.float32)
            first = here.stop
        store(cols, term)
    return jnp.sum(mass, axis=1, keepdims=True)


def mass_lanes(mass):
    high = mass.astype(jnp.bfloat16).astype(jnp.float32)
    lane = lax.broadcasted_iota(jnp.int32, (mass.shape[0], LANES), 1)
    lanes = jnp.where(lane == 0, high, jnp.where(lane == 1, mass - high, 0.0))
    return lanes.astype(jnp.bfloat16)


def read_rows(rows, width):
    wide = rows.astype(jnp.float32)
    return wide[:, :width], wide[:, width:width + 1] + wide[:, width + 1:width + 2]


def factors_kernel(groups, plan, me_ref, lse_ref, *refs):
    got_refs = refs[:len(plan)]
    top_ref, their_top_ref, doc_lse_ref, factor_ref, send_ref = refs[len(plan):]
    me = me_ref[0]
    parts = [lse_ref[...]] * groups
    for got_ref, pairs in zip(got_refs, plan):
        got = got_ref[...]
        for source, target in pairs:
            parts[source] = jnp.where(me == target, got, parts[source])
    best = tree(parts, jnp.maximum)
    doc_lse = best + jnp.log(tree([jnp.exp(x - best) for x in parts], jnp.add))
    doc_lse_ref[...] = doc_lse
    factor_ref[...] = jnp.exp(top_ref[...] - doc_lse)
    send_ref[...] = jnp.exp(their_top_ref[...] - doc_lse)


def first_sums_kernel(
    chunk, factor_ref, docs_ref, part_ref, source_ref, sum_ref, mass_ref, rest_ref, resp_ref, sem
):
    rest = rest_ref.shape[0]
    rest_rows = pl.ds(source_ref.shape[0] - rest, rest)
    copy = pltpu.make_async_copy(source_ref.at[rest_rows], rest_ref, sem)
    copy.start()

    def store(cols, term):
        sum_ref[:, cols] = term

    mass = weighted_sums(chunk, factor_ref[...], [docs_ref], part_ref, resp_ref, store)
    mass_ref[...] = jnp.broadcast_to(mass, mass_ref.shape)
    copy.wait()


def second_sums_kernel(
    chunk, factor_ref, docs_ref, rest_ref, part_ref, sum_ref, mass_ref, own_ref, own_mass_ref, *refs
):
    *send_refs, resp_ref = refs
    rows, width = own_ref.shape

    def store(cols, term):
        if cols.start < width:
            term += sum_ref[:, cols]
            own_ref[:, cols] = term[:rows]
        for slot, ref in enumerate(send_refs, 1):
            ref[:, cols] = term[slot * rows:(slot + 1) * rows].astype(jnp.bfloat16)

    mass = weighted_sums(chunk, factor_ref[...], [docs_ref, rest_ref], part_ref, resp_ref, store)
    mass += mass_ref[:, :1]
    own_mass_ref[...] = jnp.broadcast_to(mass[:rows], own_mass_ref.shape)
    store(slice(width, width + LANES), mass_lanes(mass))


def final_kernel(own_ref, own_mass_ref, cent_ref, lse_ref, *refs):
    *got_refs, next_ref, mass_ref, doc_lse_ref = refs
    doc_lse_ref[...] = lse_ref[...]
    width = own_ref.shape[1]
    got = [read_rows(r[...], width) for r in got_refs]
    term = tree([own_ref[...]] + [a for a, _ in got], jnp.add)
    mass = tree([own_mass_ref[:, :1]] + [b for _, b in got], jnp.add)
    next_ref[...] = (term + cent_ref[...]) / (mass + 1.0)
    mass_ref[...] = jnp.broadcast_to(mass, (mass.shape[0], LANES)).T[:1]


def shape(dims, dtype=jnp.float32):
    return jax.ShapeDtypeStruct(dims, dtype)


def make_body(n, g):
    def body(docs, centroids):
        rows, width = centroids.shape
        count = docs.shape[0]
        half = rows * n // 2
        chunk = 256
        plan = group_plan(g)
        limit = (4 << 20) + half * (48 << 10)

        def call(kernel, outs, *args, scratch=(), flops=0, specs=None):
            nbytes = sum(x.nbytes for x in args)
            return pl.pallas_call(
                kernel,
                out_shape=outs,
                in_specs=specs or [SMEM if x.dtype == jnp.int32 else VMEM for x in args],
                out_specs=[VMEM] * len(outs),
                scratch_shapes=scratch,
                compiler_params=pltpu.CompilerParams(vmem_limit_bytes=limit),
                cost_estimate=pl.CostEstimate(
                    flops=flops, bytes_accessed=nbytes, transcendentals=0
                ),
            )(*args)

        flops = 2 * half * count * width
        stats = [shape((count // LANES, LANES)), shape((count // LANES, LANES))]
        resp = [pltpu.VMEM((half, count), jnp.bfloat16)]
        rounded = centroids.astype(jnp.bfloat16)
        routes = chip_plan(n)
        blocks = [lax.ppermute(rounded, "dev", pairs) for pairs in routes]
        their_docs = swap(docs, "dev", n, 1)
        docs_t, own = load([docs], rounded, chunk)
        mine = jnp.concatenate([own] + blocks, axis=0)
        theirs = swap(mine, "dev", n, 1)
        part, top, total = call(
            functools.partial(scores_kernel, chunk), [shape((half, count))] + stats,
            docs_t, mine, flops=flops,
        )
        other_part, other_top, lse = call(
            functools.partial(last_scores_kernel, chunk),
            [shape((half, count), jnp.bfloat16)] + stats,
            docs_t, theirs, top, total, flops=flops,
        )
        others = [lax.ppermute(lse, "cgrp", pairs) for pairs in plan]
        their_part = swap(other_part, "dev", n, 1)
        rest = count // 4
        docs, their_first, lse = load([docs, their_docs], lse, last_rows=count - rest)
        doc_lse, factor, their_factor = call(
            functools.partial(factors_kernel, g, plan), [shape((count // LANES, LANES))] * 3,
            lax.axis_index("cgrp").reshape(1), lse, *others, top, other_top,
        )
        their_factor = swap(their_factor, "dev", n, 1)
        sums, mass, their_rest = call(
            functools.partial(first_sums_kernel, chunk),
            [shape((half, width)), shape((half, LANES)), shape((rest, width), docs.dtype)],
            factor, docs, part, pltpu.with_memory_space_constraint(their_docs, pltpu.HBM),
            scratch=resp + [pltpu.SemaphoreType.DMA], flops=flops,
            specs=[VMEM] * 3 + [pl.BlockSpec(memory_space=pltpu.HBM)],
        )
        own, own_mass, *sends = call(
            functools.partial(second_sums_kernel, chunk),
            [shape((rows, width)), shape((rows, LANES))]
            + [shape((rows, width + LANES), jnp.bfloat16)] * (n // 2 - 1),
            their_factor, their_first, their_rest, their_part, sums, mass, scratch=resp, flops=flops,
        )
        arrived = [
            lax.ppermute(x, "dev", [(target, source) for source, target in pairs])
            for x, pairs in zip(sends[-1:] + sends[:-1], routes[-1:] + routes[:-1])
        ]
        result, mass, doc_lse = call(
            final_kernel, [shape((rows, width)), shape((1, rows)), shape(doc_lse.shape)],
            own, own_mass, centroids, doc_lse, *arrived,
        )
        return (result, mass.reshape(rows), doc_lse.reshape(count))

    return body


def solution(mesh):
    in_specs = (P("dev", None), P(("cgrp", "dev"), None))
    out_specs = (P(("cgrp", "dev"), None), P(("cgrp", "dev")), P("dev"))
    return jax.shard_map(
        make_body(mesh.shape["dev"], mesh.shape["cgrp"]),
        mesh=mesh, in_specs=in_specs, out_specs=out_specs, check_vma=False,
    )
```

```python
import functools
import math

import jax
import jax.numpy as jnp
from jax import lax
from jax.experimental import pallas as pl
from jax.experimental.pallas import tpu as pltpu
from jax.sharding import PartitionSpec as P

LANES = 128
VMEM = pl.BlockSpec(memory_space=pltpu.VMEM)
SMEM = pl.BlockSpec(memory_space=pltpu.SMEM)


def swap(x, axis, size, mask):
    return lax.ppermute(x, axis, [(i, i ^ mask) for i in range(size)])


def chip_plan(n):
    near = list(range(2, n - 2, 2))
    turned = near[len(near) // 2:] + near[:len(near) // 2]
    masks = list(zip(near, turned)) + [(n - 2, n - 2)]
    return [[(i, i ^ pair[i % 2] ^ 1) for i in range(n)] for pair in masks]


def group_plan(g):
    if g == 4:
        return [
            [(0, 1), (1, 0), (2, 3), (3, 2)],
            [(0, 3), (1, 2), (2, 0), (3, 1)],
            [(0, 2), (1, 3), (2, 1), (3, 0)],
        ]
    return [[(i, i ^ m) for i in range(g)] for m in range(1, g)]


def tree(parts, op):
    while len(parts) > 1:
        parts = [op(parts[i], parts[i + 1]) for i in range(0, len(parts), 2)]
    return parts[0]


def transpose_kernel(chunk, source_ref, follow_ref, docs_ref, own_ref, landing, sems):
    copies = []
    for i, start in enumerate(range(0, source_ref.shape[0], chunk)):
        here = pl.ds(start, chunk)
        copies.append(pltpu.make_async_copy(source_ref.at[here], landing.at[here], sems.at[i]))
        copies[-1].start()
    own_ref[...] = follow_ref[...]
    for i, copy in enumerate(copies):
        copy.wait()
        here = slice(i * chunk, (i + 1) * chunk)
        docs_ref[:, here] = landing[here, :].T


def load_kernel(source_ref, follow_ref, docs_ref, own_ref, sem):
    copy = pltpu.make_async_copy(source_ref, docs_ref, sem)
    copy.start()
    own_ref[...] = follow_ref[...]
    copy.wait()


def load(source, follow, chunk=0):
    count, width = source.shape
    kernel, dims, scratch = load_kernel, (count, width), [pltpu.SemaphoreType.DMA]
    if chunk:
        kernel, dims = functools.partial(transpose_kernel, chunk), (width, count)
        scratch = [
            pltpu.VMEM((count, width), source.dtype),
            pltpu.SemaphoreType.DMA((count // chunk,)),
        ]
    return pl.pallas_call(
        kernel,
        out_shape=[shape(dims, source.dtype), shape(follow.shape, follow.dtype)],
        in_specs=[pl.BlockSpec(memory_space=pltpu.HBM), VMEM],
        out_specs=[VMEM, VMEM],
        scratch_shapes=scratch,
        compiler_params=pltpu.CompilerParams(
            vmem_limit_bytes=(4 << 20) + (2 * source.nbytes if chunk else 0)
        ),
        cost_estimate=pl.CostEstimate(
            flops=0, bytes_accessed=2 * source.nbytes, transcendentals=0
        ),
    )(pltpu.with_memory_space_constraint(source, pltpu.HBM), follow)


def put_row(ref, start, row):
    for i in range(row.shape[1] // LANES):
        at = start // LANES + i
        ref[at:at + 1, :] = row[:, i * LANES:(i + 1) * LANES]


def scores_kernel(chunk, docs_ref, table_ref, part_ref, top_ref, sum_ref):
    width, count = docs_ref.shape
    scale = 4.0 / math.sqrt(width)
    table = table_ref[...]
    wide = table.astype(jnp.float32)
    half_norms = 0.5 * jnp.sum(wide * wide, axis=1, keepdims=True)
    for start in range(0, count, chunk):
        cols = slice(start, start + chunk)
        dots = jnp.dot(table, docs_ref[:, cols], preferred_element_type=jnp.float32)
        scores = (dots - half_norms) * scale
        top = jnp.max(scores, axis=0, keepdims=True)
        part = jnp.exp(scores - top)
        part_ref[:, cols] = part
        put_row(top_ref, start, top)
        put_row(sum_ref, start, jnp.sum(part, axis=0, keepdims=True))


def last_scores_kernel(
    chunk, docs_ref, table_ref, first_top_ref, first_sum_ref, part_ref, top_ref, lse_ref
):
    scores_kernel(chunk, docs_ref, table_ref, part_ref, top_ref, lse_ref)
    top = jnp.maximum(first_top_ref[...], top_ref[...])
    total = first_sum_ref[...] * jnp.exp(first_top_ref[...] - top)
    total += lse_ref[...] * jnp.exp(top_ref[...] - top)
    lse_ref[...] = top + jnp.log(total)


def weighted_sums(chunk, factor, docs_ref, part_ref, resp_ref, store):
    rows, count = part_ref.shape
    mass = jnp.zeros((rows, LANES), jnp.float32)
    for i in range(count // LANES):
        cols = slice(i * LANES, (i + 1) * LANES)
        resp = part_ref[:, cols] * factor[i:i + 1]
        mass += resp
        resp_ref[:, cols] = resp.astype(jnp.bfloat16)
    for start in range(0, docs_ref.shape[1], chunk):
        cols = slice(start, start + chunk)
        store(cols, jnp.dot(resp_ref[...], docs_ref[:, cols], preferred_element_type=jnp.float32))
    return jnp.sum(mass, axis=1, keepdims=True)


def mass_lanes(mass):
    high = mass.astype(jnp.bfloat16).astype(jnp.float32)
    lane = lax.broadcasted_iota(jnp.int32, (mass.shape[0], LANES), 1)
    lanes = jnp.where(lane == 0, high, jnp.where(lane == 1, mass - high, 0.0))
    return lanes.astype(jnp.bfloat16)


def read_rows(rows, width):
    wide = rows.astype(jnp.float32)
    return wide[:, :width], wide[:, width:width + 1] + wide[:, width + 1:width + 2]


def send_kernel(groups, plan, chunk, me_ref, lse_ref, *refs):
    got_refs = refs[:len(plan)]
    docs_ref, part_ref, top_ref, keep_top_ref = refs[len(plan):len(plan) + 4]
    doc_lse_ref, factor_ref, send_ref, resp_ref = refs[len(plan) + 4:]
    me = me_ref[0]
    parts = [lse_ref[...]] * groups
    for got_ref, pairs in zip(got_refs, plan):
        got = got_ref[...]
        for source, target in pairs:
            parts[source] = jnp.where(me == target, got, parts[source])
    best = tree(parts, jnp.maximum)
    doc_lse = best + jnp.log(tree([jnp.exp(x - best) for x in parts], jnp.add))
    doc_lse_ref[...] = doc_lse
    factor_ref[...] = jnp.exp(keep_top_ref[...] - doc_lse)
    factor = jnp.exp(top_ref[...] - doc_lse)

    def store(cols, term):
        send_ref[:, cols] = term.astype(jnp.bfloat16)

    mass = weighted_sums(chunk, factor, docs_ref, part_ref, resp_ref, store)
    send_ref[:, docs_ref.shape[1]:] = mass_lanes(mass)


def keep_kernel(chunk, factor_ref, docs_ref, part_ref, keep_ref, keep_mass_ref, resp_ref):
    def store(cols, term):
        keep_ref[:, cols] = term

    mass = weighted_sums(chunk, factor_ref[...], docs_ref, part_ref, resp_ref, store)
    keep_mass_ref[...] = jnp.broadcast_to(mass, keep_mass_ref.shape)


def fold_kernel(keep_ref, keep_mass_ref, got_ref, own_ref, own_mass_ref, *send_refs):
    rows, width = own_ref.shape
    for slot in range(keep_ref.shape[0] // rows):
        here = slice(slot * rows, (slot + 1) * rows)
        got, got_mass = read_rows(got_ref[here], width)
        term = keep_ref[here] + got
        mass = keep_mass_ref[here, :1] + got_mass
        if slot == 0:
            own_ref[...] = term
            own_mass_ref[...] = jnp.broadcast_to(mass, own_mass_ref.shape)
        else:
            send_refs[slot - 1][:, :width] = term.astype(jnp.bfloat16)
            send_refs[slot - 1][:, width:] = mass_lanes(mass)


def final_kernel(own_ref, own_mass_ref, cent_ref, *refs):
    *got_refs, next_ref, mass_ref = refs
    width = own_ref.shape[1]
    got = [read_rows(r[...], width) for r in got_refs]
    term = tree([own_ref[...]] + [a for a, _ in got], jnp.add)
    mass = tree([own_mass_ref[:, :1]] + [b for _, b in got], jnp.add)
    next_ref[...] = (term + cent_ref[...]) / (mass + 1.0)
    mass_ref[...] = jnp.broadcast_to(mass, (mass.shape[0], LANES)).T[:1]


def shape(dims, dtype=jnp.float32):
    return jax.ShapeDtypeStruct(dims, dtype)


def make_body(n, g):
    def body(docs, centroids):
        rows, width = centroids.shape
        count = docs.shape[0]
        half = rows * n // 2
        chunk = 256
        plan = group_plan(g)
        limit = (4 << 20) + half * (48 << 10)

        def call(kernel, outs, *args, scratch=(), flops=0):
            nbytes = sum(x.nbytes for x in args)
            return pl.pallas_call(
                kernel,
                out_shape=outs,
                in_specs=[SMEM if x.dtype == jnp.int32 else VMEM for x in args],
                out_specs=[VMEM] * len(outs),
                scratch_shapes=scratch,
                compiler_params=pltpu.CompilerParams(vmem_limit_bytes=limit),
                cost_estimate=pl.CostEstimate(
                    flops=flops, bytes_accessed=nbytes, transcendentals=0
                ),
            )(*args)

        flops = 2 * half * count * width
        stats = [shape((half, count)), shape((count // LANES, LANES)), shape((count // LANES, LANES))]
        resp = [pltpu.VMEM((half, count), jnp.bfloat16)]
        rounded = centroids.astype(jnp.bfloat16)
        routes = chip_plan(n)
        blocks = [lax.ppermute(rounded, "dev", pairs) for pairs in routes]
        docs_t, own = load(docs, rounded, chunk)
        mine = jnp.concatenate([own] + blocks, axis=0)
        theirs = swap(mine, "dev", n, 1)
        part, top, total = call(
            functools.partial(scores_kernel, chunk), stats, docs_t, mine, flops=flops
        )
        other_part, other_top, lse = call(
            functools.partial(last_scores_kernel, chunk), stats,
            docs_t, theirs, top, total, flops=flops,
        )
        others = [lax.ppermute(lse, "cgrp", pairs) for pairs in plan]
        docs, lse = load(docs, lse)
        doc_lse, factor, send = call(
            functools.partial(send_kernel, g, plan, chunk),
            [shape((count // LANES, LANES)), shape((count // LANES, LANES)), shape((half, width + LANES), jnp.bfloat16)],
            lax.axis_index("cgrp").reshape(1), lse, *others, docs, other_part, other_top, top,
            scratch=resp, flops=flops,
        )
        got = swap(send, "dev", n, 1)
        keep, keep_mass = call(
            functools.partial(keep_kernel, chunk),
            [shape((half, width)), shape((half, LANES))],
            factor, docs, part, scratch=resp, flops=flops,
        )
        own, own_mass, *sends = call(
            fold_kernel,
            [shape((rows, width)), shape((rows, LANES))]
            + [shape((rows, width + LANES), jnp.bfloat16)] * (n // 2 - 1),
            keep, keep_mass, got,
        )
        arrived = [
            lax.ppermute(x, "dev", [(target, source) for source, target in pairs])
            for x, pairs in zip(sends[1:] + sends[:1], routes[1:] + routes[:1])
        ]
        result, mass = call(
            final_kernel, [shape((rows, width)), shape((1, rows))],
            own, own_mass, centroids, *arrived,
        )
        return (result, mass.reshape(rows), doc_lse.reshape(count))

    return body


def solution(mesh):
    in_specs = (P("dev", None), P(("cgrp", "dev"), None))
    out_specs = (P(("cgrp", "dev"), None), P(("cgrp", "dev")), P("dev"))
    return jax.shard_map(
        make_body(mesh.shape["dev"], mesh.shape["cgrp"]),
        mesh=mesh, in_specs=in_specs, out_specs=out_specs, check_vma=False,
    )
```

```python
import functools
import math

import jax
import jax.numpy as jnp
from jax import lax
from jax.experimental import pallas as pl
from jax.experimental.pallas import tpu as pltpu
from jax.sharding import PartitionSpec as P

LANES = 128
VMEM = pl.BlockSpec(memory_space=pltpu.VMEM)
SMEM = pl.BlockSpec(memory_space=pltpu.SMEM)


def swap(x, axis, size, mask):
    return lax.ppermute(x, axis, [(i, i ^ mask) for i in range(size)])


def chip_plan(n):
    near = list(range(2, n - 2, 2))
    turned = near[len(near) // 2:] + near[:len(near) // 2]
    masks = list(zip(near, turned)) + [(n - 2, n - 2)]
    return [[(i, i ^ pair[i % 2] ^ 1) for i in range(n)] for pair in masks]


def group_plan(g):
    if g == 4:
        return [
            [(0, 1), (1, 0), (2, 3), (3, 2)],
            [(0, 3), (1, 2), (2, 0), (3, 1)],
            [(0, 2), (1, 3), (2, 1), (3, 0)],
        ]
    return [[(i, i ^ m) for i in range(g)] for m in range(1, g)]


def tree(parts, op):
    while len(parts) > 1:
        parts = [op(parts[i], parts[i + 1]) for i in range(0, len(parts), 2)]
    return parts[0]


def transpose_kernel(chunk, source_ref, follow_ref, docs_ref, own_ref, landing, sems):
    copies = []
    for i, start in enumerate(range(0, source_ref.shape[0], chunk)):
        here = pl.ds(start, chunk)
        copies.append(pltpu.make_async_copy(source_ref.at[here], landing.at[here], sems.at[i]))
        copies[-1].start()
    own_ref[...] = follow_ref[...]
    for i, copy in enumerate(copies):
        copy.wait()
        here = slice(i * chunk, (i + 1) * chunk)
        docs_ref[:, here] = landing[here, :].T


def load_kernel(*refs):
    half = len(refs) // 2
    sources, follow_ref = refs[:half - 1], refs[half - 1]
    targets, own_ref, sems = refs[half:-2], refs[-2], refs[-1]
    copies = [
        pltpu.make_async_copy(source.at[pl.ds(0, target.shape[0])], target, sems.at[i])
        for i, (source, target) in enumerate(zip(sources, targets))
    ]
    for copy in copies:
        copy.start()
    own_ref[...] = follow_ref[...]
    for copy in copies:
        copy.wait()


def load(sources, follow, chunk=0, last_rows=0):
    kernel, dims = load_kernel, sources[0].shape
    scratch = [pltpu.SemaphoreType.DMA((len(sources),))]
    if chunk:
        kernel, (count, width) = functools.partial(transpose_kernel, chunk), dims
        dims = (width, count)
        scratch = [
            pltpu.VMEM((count, width), follow.dtype),
            pltpu.SemaphoreType.DMA((count // chunk,)),
        ]
    outs = [shape(dims, x.dtype) for x in sources]
    if last_rows:
        outs[-1] = shape((last_rows, dims[1]), sources[-1].dtype)
    size = sum(x.nbytes for x in sources)
    return pl.pallas_call(
        kernel,
        out_shape=outs + [shape(follow.shape, follow.dtype)],
        in_specs=[pl.BlockSpec(memory_space=pltpu.HBM)] * len(sources) + [VMEM],
        out_specs=[VMEM] * (len(sources) + 1),
        scratch_shapes=scratch,
        compiler_params=pltpu.CompilerParams(
            vmem_limit_bytes=(4 << 20) + (2 * size if chunk else 0)
        ),
        cost_estimate=pl.CostEstimate(flops=0, bytes_accessed=2 * size, transcendentals=0),
    )(*[pltpu.with_memory_space_constraint(x, pltpu.HBM) for x in sources], follow)


def put_row(ref, start, row):
    for i in range(row.shape[1] // LANES):
        at = start // LANES + i
        ref[at:at + 1, :] = row[:, i * LANES:(i + 1) * LANES]


def scores_kernel(chunk, docs_ref, table_ref, part_ref, top_ref, sum_ref):
    width, count = docs_ref.shape
    scale = 4.0 / math.sqrt(width)
    table = table_ref[...]
    wide = table.astype(jnp.float32)
    half_norms = 0.5 * jnp.sum(wide * wide, axis=1, keepdims=True)
    for start in range(0, count, chunk):
        cols = slice(start, start + chunk)
        dots = jnp.dot(table, docs_ref[:, cols], preferred_element_type=jnp.float32)
        scores = (dots - half_norms) * scale
        top = jnp.max(scores, axis=0, keepdims=True)
        part = jnp.exp(scores - top)
        part_ref[:, cols] = part.astype(part_ref.dtype)
        put_row(top_ref, start, top)
        put_row(sum_ref, start, jnp.sum(part, axis=0, keepdims=True))


def last_scores_kernel(
    chunk, docs_ref, table_ref, first_top_ref, first_sum_ref, part_ref, top_ref, lse_ref
):
    scores_kernel(chunk, docs_ref, table_ref, part_ref, top_ref, lse_ref)
    top = jnp.maximum(first_top_ref[...], top_ref[...])
    total = first_sum_ref[...] * jnp.exp(first_top_ref[...] - top)
    total += lse_ref[...] * jnp.exp(top_ref[...] - top)
    lse_ref[...] = top + jnp.log(total)


def weighted_sums(chunk, factor, docs_refs, part_ref, resp_ref, store):
    rows, count = part_ref.shape
    mass = jnp.zeros((rows, LANES), jnp.float32)
    for i in range(count // LANES):
        cols = slice(i * LANES, (i + 1) * LANES)
        resp = part_ref[:, cols].astype(jnp.float32) * factor[i:i + 1]
        mass += resp
        resp_ref[:, cols] = resp.astype(jnp.bfloat16)
    for start in range(0, docs_refs[0].shape[1], chunk):
        cols = slice(start, start + chunk)
        term, first = 0.0, 0
        for ref in docs_refs:
            here = slice(first, first + ref.shape[0])
            term += jnp.dot(resp_ref[:, here], ref[:, cols], preferred_element_type=jnp.float32)
            first = here.stop
        store(cols, term)
    return jnp.sum(mass, axis=1, keepdims=True)


def mass_lanes(mass):
    high = mass.astype(jnp.bfloat16).astype(jnp.float32)
    lane = lax.broadcasted_iota(jnp.int32, (mass.shape[0], LANES), 1)
    lanes = jnp.where(lane == 0, high, jnp.where(lane == 1, mass - high, 0.0))
    return lanes.astype(jnp.bfloat16)


def read_rows(rows, width):
    wide = rows.astype(jnp.float32)
    return wide[:, :width], wide[:, width:width + 1] + wide[:, width + 1:width + 2]


def factors_kernel(groups, plan, me_ref, lse_ref, *refs):
    got_refs = refs[:len(plan)]
    top_ref, their_top_ref, doc_lse_ref, factor_ref, send_ref = refs[len(plan):]
    me = me_ref[0]
    parts = [lse_ref[...]] * groups
    for got_ref, pairs in zip(got_refs, plan):
        got = got_ref[...]
        for source, target in pairs:
            parts[source] = jnp.where(me == target, got, parts[source])
    best = tree(parts, jnp.maximum)
    doc_lse = best + jnp.log(tree([jnp.exp(x - best) for x in parts], jnp.add))
    doc_lse_ref[...] = doc_lse
    factor_ref[...] = jnp.exp(top_ref[...] - doc_lse)
    send_ref[...] = jnp.exp(their_top_ref[...] - doc_lse)


def first_sums_kernel(
    chunk, factor_ref, docs_ref, part_ref, source_ref, sum_ref, mass_ref, rest_ref, resp_ref, sem
):
    rest = rest_ref.shape[0]
    rest_rows = pl.ds(source_ref.shape[0] - rest, rest)
    copy = pltpu.make_async_copy(source_ref.at[rest_rows], rest_ref, sem)
    copy.start()

    def store(cols, term):
        sum_ref[:, cols] = term

    mass = weighted_sums(chunk, factor_ref[...], [docs_ref], part_ref, resp_ref, store)
    mass_ref[...] = jnp.broadcast_to(mass, mass_ref.shape)
    copy.wait()


def second_sums_kernel(
    chunk, factor_ref, docs_ref, rest_ref, part_ref, sum_ref, mass_ref, own_ref, own_mass_ref, *refs
):
    *send_refs, resp_ref = refs
    rows, width = own_ref.shape

    def store(cols, term):
        if cols.start < width:
            term += sum_ref[:, cols]
            own_ref[:, cols] = term[:rows]
        for slot, ref in enumerate(send_refs, 1):
            ref[:, cols] = term[slot * rows:(slot + 1) * rows].astype(jnp.bfloat16)

    mass = weighted_sums(chunk, factor_ref[...], [docs_ref, rest_ref], part_ref, resp_ref, store)
    mass += mass_ref[:, :1]
    own_mass_ref[...] = jnp.broadcast_to(mass[:rows], own_mass_ref.shape)
    store(slice(width, width + LANES), mass_lanes(mass))


def final_kernel(own_ref, own_mass_ref, cent_ref, lse_ref, *refs):
    *got_refs, next_ref, mass_ref, doc_lse_ref = refs
    doc_lse_ref[...] = lse_ref[...]
    width = own_ref.shape[1]
    got = [read_rows(r[...], width) for r in got_refs]
    term = tree([own_ref[...]] + [a for a, _ in got], jnp.add)
    mass = tree([own_mass_ref[:, :1]] + [b for _, b in got], jnp.add)
    next_ref[...] = (term + cent_ref[...]) / (mass + 1.0)
    mass_ref[...] = jnp.broadcast_to(mass, (mass.shape[0], LANES)).T[:1]


def shape(dims, dtype=jnp.float32):
    return jax.ShapeDtypeStruct(dims, dtype)


def make_body(n, g):
    def body(docs, centroids):
        rows, width = centroids.shape
        count = docs.shape[0]
        half = rows * n // 2
        chunk = 256
        plan = group_plan(g)
        limit = (4 << 20) + half * (48 << 10)

        def call(kernel, outs, *args, scratch=(), flops=0, specs=None):
            nbytes = sum(x.nbytes for x in args)
            return pl.pallas_call(
                kernel,
                out_shape=outs,
                in_specs=specs or [SMEM if x.dtype == jnp.int32 else VMEM for x in args],
                out_specs=[VMEM] * len(outs),
                scratch_shapes=scratch,
                compiler_params=pltpu.CompilerParams(vmem_limit_bytes=limit),
                cost_estimate=pl.CostEstimate(
                    flops=flops, bytes_accessed=nbytes, transcendentals=0
                ),
            )(*args)

        flops = 2 * half * count * width
        stats = [shape((count // LANES, LANES)), shape((count // LANES, LANES))]
        resp = [pltpu.VMEM((half, count), jnp.bfloat16)]
        rounded = centroids.astype(jnp.bfloat16)
        routes = chip_plan(n)
        blocks = [lax.ppermute(rounded, "dev", pairs) for pairs in routes]
        their_docs = swap(docs, "dev", n, 1)
        docs_t, own = load([docs], rounded, chunk)
        mine = jnp.concatenate([own] + blocks, axis=0)
        theirs = swap(mine, "dev", n, 1)
        part, top, total = call(
            functools.partial(scores_kernel, chunk), [shape((half, count))] + stats,
            docs_t, mine, flops=flops,
        )
        other_part, other_top, lse = call(
            functools.partial(last_scores_kernel, chunk),
            [shape((half, count), jnp.bfloat16)] + stats,
            docs_t, theirs, top, total, flops=flops,
        )
        others = [lax.ppermute(lse, "cgrp", pairs) for pairs in plan]
        their_part = swap(other_part, "dev", n, 1)
        rest = count // 4
        docs, their_first, lse = load([docs, their_docs], lse, last_rows=count - rest)
        doc_lse, factor, their_factor = call(
            functools.partial(factors_kernel, g, plan), [shape((count // LANES, LANES))] * 3,
            lax.axis_index("cgrp").reshape(1), lse, *others, top, other_top,
        )
        their_factor = swap(their_factor, "dev", n, 1)
        sums, mass, their_rest = call(
            functools.partial(first_sums_kernel, chunk),
            [shape((half, width)), shape((half, LANES)), shape((rest, width), docs.dtype)],
            factor, docs, part, pltpu.with_memory_space_constraint(their_docs, pltpu.HBM),
            scratch=resp + [pltpu.SemaphoreType.DMA], flops=flops,
            specs=[VMEM] * 3 + [pl.BlockSpec(memory_space=pltpu.HBM)],
        )
        own, own_mass, *sends = call(
            functools.partial(second_sums_kernel, chunk),
            [shape((rows, width)), shape((rows, LANES))]
            + [shape((rows, width + LANES), jnp.bfloat16)] * (n // 2 - 1),
            their_factor, their_first, their_rest, their_part, sums, mass, scratch=resp, flops=flops,
        )
        arrived = [
            lax.ppermute(x, "dev", [(target, source) for source, target in pairs])
            for x, pairs in zip(sends[1:] + sends[:1], routes[1:] + routes[:1])
        ]
        result, mass, doc_lse = call(
            final_kernel, [shape((rows, width)), shape((1, rows)), shape(doc_lse.shape)],
            own, own_mass, centroids, doc_lse, *arrived,
        )
        return (result, mass.reshape(rows), doc_lse.reshape(count))

    return body


def solution(mesh):
    in_specs = (P("dev", None), P(("cgrp", "dev"), None))
    out_specs = (P(("cgrp", "dev"), None), P(("cgrp", "dev")), P("dev"))
    return jax.shard_map(
        make_body(mesh.shape["dev"], mesh.shape["cgrp"]),
        mesh=mesh, in_specs=in_specs, out_specs=out_specs, check_vma=False,
    )
```

```python
import functools
import math

import jax
import jax.numpy as jnp
from jax import lax
from jax.experimental import pallas as pl
from jax.experimental.pallas import tpu as pltpu
from jax.sharding import PartitionSpec as P

LANES = 128
VMEM = pl.BlockSpec(memory_space=pltpu.VMEM)
SMEM = pl.BlockSpec(memory_space=pltpu.SMEM)


def swap(x, axis, size, mask):
    return lax.ppermute(x, axis, [(i, i ^ mask) for i in range(size)])


def chip_plan(n):
    near = list(range(2, n - 2, 2))
    turned = near[len(near) // 2:] + near[:len(near) // 2]
    masks = list(zip(near, turned))
    masks = masks[:1] + [(n - 2, n - 2)] + masks[1:]
    return [[(i, i ^ pair[i % 2] ^ 1) for i in range(n)] for pair in masks]


def group_plan(g):
    if g == 4:
        return [
            [(0, 1), (1, 0), (2, 3), (3, 2)],
            [(0, 3), (1, 2), (2, 0), (3, 1)],
            [(0, 2), (1, 3), (2, 1), (3, 0)],
        ]
    return [[(i, i ^ m) for i in range(g)] for m in range(1, g)]


def tree(parts, op):
    while len(parts) > 1:
        parts = [op(parts[i], parts[i + 1]) for i in range(0, len(parts), 2)]
    return parts[0]


def transpose_kernel(chunk, source_ref, follow_ref, docs_ref, own_ref, landing, sems):
    copies = []
    for i, start in enumerate(range(0, source_ref.shape[0], chunk)):
        here = pl.ds(start, chunk)
        copies.append(pltpu.make_async_copy(source_ref.at[here], landing.at[here], sems.at[i]))
        copies[-1].start()
    own_ref[...] = follow_ref[...]
    for i, copy in enumerate(copies):
        copy.wait()
        here = slice(i * chunk, (i + 1) * chunk)
        docs_ref[:, here] = landing[here, :].T


def load_kernel(source_ref, follow_ref, docs_ref, own_ref, sem):
    copy = pltpu.make_async_copy(source_ref, docs_ref, sem)
    copy.start()
    own_ref[...] = follow_ref[...]
    copy.wait()


def load(source, follow, chunk=0):
    count, width = source.shape
    kernel, dims, scratch = load_kernel, (count, width), [pltpu.SemaphoreType.DMA]
    if chunk:
        kernel, dims = functools.partial(transpose_kernel, chunk), (width, count)
        scratch = [
            pltpu.VMEM((count, width), source.dtype),
            pltpu.SemaphoreType.DMA((count // chunk,)),
        ]
    return pl.pallas_call(
        kernel,
        out_shape=[shape(dims, source.dtype), shape(follow.shape, follow.dtype)],
        in_specs=[pl.BlockSpec(memory_space=pltpu.HBM), VMEM],
        out_specs=[VMEM, VMEM],
        scratch_shapes=scratch,
        compiler_params=pltpu.CompilerParams(
            vmem_limit_bytes=(4 << 20) + (2 * source.nbytes if chunk else 0)
        ),
        cost_estimate=pl.CostEstimate(
            flops=0, bytes_accessed=2 * source.nbytes, transcendentals=0
        ),
    )(pltpu.with_memory_space_constraint(source, pltpu.HBM), follow)


def put_row(ref, start, row):
    for i in range(row.shape[1] // LANES):
        at = start // LANES + i
        ref[at:at + 1, :] = row[:, i * LANES:(i + 1) * LANES]


def scores_kernel(chunk, docs_ref, table_ref, part_ref, top_ref, sum_ref):
    width, count = docs_ref.shape
    scale = 4.0 / math.sqrt(width)
    table = table_ref[...]
    wide = table.astype(jnp.float32)
    half_norms = 0.5 * jnp.sum(wide * wide, axis=1, keepdims=True)
    for start in range(0, count, chunk):
        cols = slice(start, start + chunk)
        dots = jnp.dot(table, docs_ref[:, cols], preferred_element_type=jnp.float32)
        scores = (dots - half_norms) * scale
        top = jnp.max(scores, axis=0, keepdims=True)
        part = jnp.exp(scores - top)
        part_ref[:, cols] = part
        put_row(top_ref, start, top)
        put_row(sum_ref, start, jnp.sum(part, axis=0, keepdims=True))


def last_scores_kernel(
    chunk, docs_ref, table_ref, first_top_ref, first_sum_ref, part_ref, top_ref, lse_ref
):
    scores_kernel(chunk, docs_ref, table_ref, part_ref, top_ref, lse_ref)
    top = jnp.maximum(first_top_ref[...], top_ref[...])
    total = first_sum_ref[...] * jnp.exp(first_top_ref[...] - top)
    total += lse_ref[...] * jnp.exp(top_ref[...] - top)
    lse_ref[...] = top + jnp.log(total)


def weighted_sums(chunk, factor, docs_ref, part_ref, resp_ref, store):
    rows, count = part_ref.shape
    mass = jnp.zeros((rows, LANES), jnp.float32)
    for i in range(count // LANES):
        cols = slice(i * LANES, (i + 1) * LANES)
        resp = part_ref[:, cols] * factor[i:i + 1]
        mass += resp
        resp_ref[:, cols] = resp.astype(jnp.bfloat16)
    for start in range(0, docs_ref.shape[1], chunk):
        cols = slice(start, start + chunk)
        store(cols, jnp.dot(resp_ref[...], docs_ref[:, cols], preferred_element_type=jnp.float32))
    return jnp.sum(mass, axis=1, keepdims=True)


def mass_lanes(mass):
    high = mass.astype(jnp.bfloat16).astype(jnp.float32)
    lane = lax.broadcasted_iota(jnp.int32, (mass.shape[0], LANES), 1)
    lanes = jnp.where(lane == 0, high, jnp.where(lane == 1, mass - high, 0.0))
    return lanes.astype(jnp.bfloat16)


def read_rows(rows, width):
    wide = rows.astype(jnp.float32)
    return wide[:, :width], wide[:, width:width + 1] + wide[:, width + 1:width + 2]


def send_kernel(groups, plan, chunk, me_ref, lse_ref, *refs):
    got_refs = refs[:len(plan)]
    docs_ref, part_ref, top_ref, keep_top_ref = refs[len(plan):len(plan) + 4]
    doc_lse_ref, factor_ref, send_ref, resp_ref = refs[len(plan) + 4:]
    me = me_ref[0]
    parts = [lse_ref[...]] * groups
    for got_ref, pairs in zip(got_refs, plan):
        got = got_ref[...]
        for source, target in pairs:
            parts[source] = jnp.where(me == target, got, parts[source])
    best = tree(parts, jnp.maximum)
    doc_lse = best + jnp.log(tree([jnp.exp(x - best) for x in parts], jnp.add))
    doc_lse_ref[...] = doc_lse
    factor_ref[...] = jnp.exp(keep_top_ref[...] - doc_lse)
    factor = jnp.exp(top_ref[...] - doc_lse)

    def store(cols, term):
        send_ref[:, cols] = term.astype(jnp.bfloat16)

    mass = weighted_sums(chunk, factor, docs_ref, part_ref, resp_ref, store)
    send_ref[:, docs_ref.shape[1]:] = mass_lanes(mass)


def keep_kernel(chunk, factor_ref, docs_ref, part_ref, keep_ref, keep_mass_ref, resp_ref):
    def store(cols, term):
        keep_ref[:, cols] = term

    mass = weighted_sums(chunk, factor_ref[...], docs_ref, part_ref, resp_ref, store)
    keep_mass_ref[...] = jnp.broadcast_to(mass, keep_mass_ref.shape)


def fold_kernel(keep_ref, keep_mass_ref, got_ref, own_ref, own_mass_ref, *send_refs):
    rows, width = own_ref.shape
    for slot in range(keep_ref.shape[0] // rows):
        here = slice(slot * rows, (slot + 1) * rows)
        got, got_mass = read_rows(got_ref[here], width)
        term = keep_ref[here] + got
        mass = keep_mass_ref[here, :1] + got_mass
        if slot == 0:
            own_ref[...] = term
            own_mass_ref[...] = jnp.broadcast_to(mass, own_mass_ref.shape)
        else:
            send_refs[slot - 1][:, :width] = term.astype(jnp.bfloat16)
            send_refs[slot - 1][:, width:] = mass_lanes(mass)


def final_kernel(own_ref, own_mass_ref, cent_ref, *refs):
    *got_refs, next_ref, mass_ref = refs
    width = own_ref.shape[1]
    got = [read_rows(r[...], width) for r in got_refs]
    term = tree([own_ref[...]] + [a for a, _ in got], jnp.add)
    mass = tree([own_mass_ref[:, :1]] + [b for _, b in got], jnp.add)
    next_ref[...] = (term + cent_ref[...]) / (mass + 1.0)
    mass_ref[...] = jnp.broadcast_to(mass, (mass.shape[0], LANES)).T[:1]


def shape(dims, dtype=jnp.float32):
    return jax.ShapeDtypeStruct(dims, dtype)


def make_body(n, g):
    def body(docs, centroids):
        rows, width = centroids.shape
        count = docs.shape[0]
        half = rows * n // 2
        chunk = 256
        plan = group_plan(g)
        limit = (4 << 20) + half * (48 << 10)

        def call(kernel, outs, *args, scratch=(), flops=0):
            nbytes = sum(x.nbytes for x in args)
            return pl.pallas_call(
                kernel,
                out_shape=outs,
                in_specs=[SMEM if x.dtype == jnp.int32 else VMEM for x in args],
                out_specs=[VMEM] * len(outs),
                scratch_shapes=scratch,
                compiler_params=pltpu.CompilerParams(vmem_limit_bytes=limit),
                cost_estimate=pl.CostEstimate(
                    flops=flops, bytes_accessed=nbytes, transcendentals=0
                ),
            )(*args)

        flops = 2 * half * count * width
        stats = [shape((half, count)), shape((count // LANES, LANES)), shape((count // LANES, LANES))]
        resp = [pltpu.VMEM((half, count), jnp.bfloat16)]
        rounded = centroids.astype(jnp.bfloat16)
        routes = chip_plan(n)
        blocks = [lax.ppermute(rounded, "dev", pairs) for pairs in routes]
        docs_t, own = load(docs, rounded, chunk)
        mine = jnp.concatenate([own] + blocks, axis=0)
        theirs = swap(mine, "dev", n, 1)
        part, top, total = call(
            functools.partial(scores_kernel, chunk), stats, docs_t, mine, flops=flops
        )
        other_part, other_top, lse = call(
            functools.partial(last_scores_kernel, chunk), stats,
            docs_t, theirs, top, total, flops=flops,
        )
        others = [lax.ppermute(lse, "cgrp", pairs) for pairs in plan]
        docs, lse = load(docs, lse)
        doc_lse, factor, send = call(
            functools.partial(send_kernel, g, plan, chunk),
            [shape((count // LANES, LANES)), shape((count // LANES, LANES)), shape((half, width + LANES), jnp.bfloat16)],
            lax.axis_index("cgrp").reshape(1), lse, *others, docs, other_part, other_top, top,
            scratch=resp, flops=flops,
        )
        got = swap(send, "dev", n, 1)
        keep, keep_mass = call(
            functools.partial(keep_kernel, chunk),
            [shape((half, width)), shape((half, LANES))],
            factor, docs, part, scratch=resp, flops=flops,
        )
        own, own_mass, *sends = call(
            fold_kernel,
            [shape((rows, width)), shape((rows, LANES))]
            + [shape((rows, width + LANES), jnp.bfloat16)] * (n // 2 - 1),
            keep, keep_mass, got,
        )
        arrived = [
            lax.ppermute(x, "dev", [(target, source) for source, target in pairs])
            for x, pairs in zip(sends[::-1], routes[::-1])
        ]
        result, mass = call(
            final_kernel, [shape((rows, width)), shape((1, rows))],
            own, own_mass, centroids, *arrived,
        )
        return (result, mass.reshape(rows), doc_lse.reshape(count))

    return body


def solution(mesh):
    in_specs = (P("dev", None), P(("cgrp", "dev"), None))
    out_specs = (P(("cgrp", "dev"), None), P(("cgrp", "dev")), P("dev"))
    return jax.shard_map(
        make_body(mesh.shape["dev"], mesh.shape["cgrp"]),
        mesh=mesh, in_specs=in_specs, out_specs=out_specs, check_vma=False,
    )
```

```python
import functools
import math

import jax
import jax.numpy as jnp
from jax import lax
from jax.experimental import pallas as pl
from jax.experimental.pallas import tpu as pltpu
from jax.sharding import PartitionSpec as P

LANES = 128
VMEM = pl.BlockSpec(memory_space=pltpu.VMEM)
SMEM = pl.BlockSpec(memory_space=pltpu.SMEM)


def swap(x, axis, size, mask):
    return lax.ppermute(x, axis, [(i, i ^ mask) for i in range(size)])


def chip_plan(n):
    near = list(range(2, n - 2, 2))
    turned = near[len(near) // 2:] + near[:len(near) // 2]
    masks = list(zip(near, turned))
    masks = masks[:1] + [(n - 2, n - 2)] + masks[1:]
    return [[(i, i ^ pair[i % 2] ^ 1) for i in range(n)] for pair in masks]


def group_plan(g):
    if g == 4:
        return [
            [(0, 1), (1, 0), (2, 3), (3, 2)],
            [(0, 3), (1, 2), (2, 0), (3, 1)],
            [(0, 2), (1, 3), (2, 1), (3, 0)],
        ]
    return [[(i, i ^ m) for i in range(g)] for m in range(1, g)]


def tree(parts, op):
    while len(parts) > 1:
        parts = [op(parts[i], parts[i + 1]) for i in range(0, len(parts), 2)]
    return parts[0]


def transpose_kernel(chunk, source_ref, follow_ref, docs_ref, own_ref, landing, sems):
    copies = []
    for i, start in enumerate(range(0, source_ref.shape[0], chunk)):
        here = pl.ds(start, chunk)
        copies.append(pltpu.make_async_copy(source_ref.at[here], landing.at[here], sems.at[i]))
        copies[-1].start()
    own_ref[...] = follow_ref[...]
    for i, copy in enumerate(copies):
        copy.wait()
        here = slice(i * chunk, (i + 1) * chunk)
        docs_ref[:, here] = landing[here, :].T


def load_kernel(*refs):
    half = len(refs) // 2
    sources, follow_ref = refs[:half - 1], refs[half - 1]
    targets, own_ref, sems = refs[half:-2], refs[-2], refs[-1]
    copies = [
        pltpu.make_async_copy(source.at[pl.ds(0, target.shape[0])], target, sems.at[i])
        for i, (source, target) in enumerate(zip(sources, targets))
    ]
    for copy in copies:
        copy.start()
    own_ref[...] = follow_ref[...]
    for copy in copies:
        copy.wait()


def load(sources, follow, chunk=0, last_rows=0):
    kernel, dims = load_kernel, sources[0].shape
    scratch = [pltpu.SemaphoreType.DMA((len(sources),))]
    if chunk:
        kernel, (count, width) = functools.partial(transpose_kernel, chunk), dims
        dims = (width, count)
        scratch = [
            pltpu.VMEM((count, width), follow.dtype),
            pltpu.SemaphoreType.DMA((count // chunk,)),
        ]
    outs = [shape(dims, x.dtype) for x in sources]
    if last_rows:
        outs[-1] = shape((last_rows, dims[1]), sources[-1].dtype)
    size = sum(x.nbytes for x in sources)
    return pl.pallas_call(
        kernel,
        out_shape=outs + [shape(follow.shape, follow.dtype)],
        in_specs=[pl.BlockSpec(memory_space=pltpu.HBM)] * len(sources) + [VMEM],
        out_specs=[VMEM] * (len(sources) + 1),
        scratch_shapes=scratch,
        compiler_params=pltpu.CompilerParams(
            vmem_limit_bytes=(4 << 20) + (2 * size if chunk else 0)
        ),
        cost_estimate=pl.CostEstimate(flops=0, bytes_accessed=2 * size, transcendentals=0),
    )(*[pltpu.with_memory_space_constraint(x, pltpu.HBM) for x in sources], follow)


def put_row(ref, start, row):
    for i in range(row.shape[1] // LANES):
        at = start // LANES + i
        ref[at:at + 1, :] = row[:, i * LANES:(i + 1) * LANES]


def scores_kernel(chunk, docs_ref, table_ref, part_ref, top_ref, sum_ref):
    width, count = docs_ref.shape
    scale = 4.0 / math.sqrt(width)
    table = table_ref[...]
    wide = table.astype(jnp.float32)
    half_norms = 0.5 * jnp.sum(wide * wide, axis=1, keepdims=True)
    for start in range(0, count, chunk):
        cols = slice(start, start + chunk)
        dots = jnp.dot(table, docs_ref[:, cols], preferred_element_type=jnp.float32)
        scores = (dots - half_norms) * scale
        top = jnp.max(scores, axis=0, keepdims=True)
        part = jnp.exp(scores - top)
        part_ref[:, cols] = part.astype(part_ref.dtype)
        put_row(top_ref, start, top)
        put_row(sum_ref, start, jnp.sum(part, axis=0, keepdims=True))


def last_scores_kernel(
    chunk, docs_ref, table_ref, first_top_ref, first_sum_ref, part_ref, top_ref, lse_ref
):
    scores_kernel(chunk, docs_ref, table_ref, part_ref, top_ref, lse_ref)
    top = jnp.maximum(first_top_ref[...], top_ref[...])
    total = first_sum_ref[...] * jnp.exp(first_top_ref[...] - top)
    total += lse_ref[...] * jnp.exp(top_ref[...] - top)
    lse_ref[...] = top + jnp.log(total)


def weighted_sums(chunk, factor, docs_refs, part_ref, resp_ref, store):
    rows, count = part_ref.shape
    mass = jnp.zeros((rows, LANES), jnp.float32)
    for i in range(count // LANES):
        cols = slice(i * LANES, (i + 1) * LANES)
        resp = part_ref[:, cols].astype(jnp.float32) * factor[i:i + 1]
        mass += resp
        resp_ref[:, cols] = resp.astype(jnp.bfloat16)
    for start in range(0, docs_refs[0].shape[1], chunk):
        cols = slice(start, start + chunk)
        term, first = 0.0, 0
        for ref in docs_refs:
            here = slice(first, first + ref.shape[0])
            term += jnp.dot(resp_ref[:, here], ref[:, cols], preferred_element_type=jnp.float32)
            first = here.stop
        store(cols, term)
    return jnp.sum(mass, axis=1, keepdims=True)


def mass_lanes(mass):
    high = mass.astype(jnp.bfloat16).astype(jnp.float32)
    lane = lax.broadcasted_iota(jnp.int32, (mass.shape[0], LANES), 1)
    lanes = jnp.where(lane == 0, high, jnp.where(lane == 1, mass - high, 0.0))
    return lanes.astype(jnp.bfloat16)


def read_rows(rows, width):
    wide = rows.astype(jnp.float32)
    return wide[:, :width], wide[:, width:width + 1] + wide[:, width + 1:width + 2]


def factors_kernel(groups, plan, me_ref, lse_ref, *refs):
    got_refs = refs[:len(plan)]
    top_ref, their_top_ref, doc_lse_ref, factor_ref, send_ref = refs[len(plan):]
    me = me_ref[0]
    parts = [lse_ref[...]] * groups
    for got_ref, pairs in zip(got_refs, plan):
        got = got_ref[...]
        for source, target in pairs:
            parts[source] = jnp.where(me == target, got, parts[source])
    best = tree(parts, jnp.maximum)
    doc_lse = best + jnp.log(tree([jnp.exp(x - best) for x in parts], jnp.add))
    doc_lse_ref[...] = doc_lse
    factor_ref[...] = jnp.exp(top_ref[...] - doc_lse)
    send_ref[...] = jnp.exp(their_top_ref[...] - doc_lse)


def first_sums_kernel(
    chunk, factor_ref, docs_ref, part_ref, source_ref, sum_ref, mass_ref, rest_ref, resp_ref, sem
):
    rest = rest_ref.shape[0]
    rest_rows = pl.ds(source_ref.shape[0] - rest, rest)
    copy = pltpu.make_async_copy(source_ref.at[rest_rows], rest_ref, sem)
    copy.start()

    def store(cols, term):
        sum_ref[:, cols] = term

    mass = weighted_sums(chunk, factor_ref[...], [docs_ref], part_ref, resp_ref, store)
    mass_ref[...] = jnp.broadcast_to(mass, mass_ref.shape)
    copy.wait()


def second_sums_kernel(
    chunk, factor_ref, docs_ref, rest_ref, part_ref, sum_ref, mass_ref, own_ref, own_mass_ref, *refs
):
    *send_refs, resp_ref = refs
    rows, width = own_ref.shape

    def store(cols, term):
        if cols.start < width:
            term += sum_ref[:, cols]
            own_ref[:, cols] = term[:rows]
        for slot, ref in enumerate(send_refs, 1):
            ref[:, cols] = term[slot * rows:(slot + 1) * rows].astype(jnp.bfloat16)

    mass = weighted_sums(chunk, factor_ref[...], [docs_ref, rest_ref], part_ref, resp_ref, store)
    mass += mass_ref[:, :1]
    own_mass_ref[...] = jnp.broadcast_to(mass[:rows], own_mass_ref.shape)
    store(slice(width, width + LANES), mass_lanes(mass))


def final_kernel(own_ref, own_mass_ref, cent_ref, lse_ref, *refs):
    *got_refs, next_ref, mass_ref, doc_lse_ref = refs
    doc_lse_ref[...] = lse_ref[...]
    width = own_ref.shape[1]
    got = [read_rows(r[...], width) for r in got_refs]
    term = tree([own_ref[...]] + [a for a, _ in got], jnp.add)
    mass = tree([own_mass_ref[:, :1]] + [b for _, b in got], jnp.add)
    next_ref[...] = (term + cent_ref[...]) / (mass + 1.0)
    mass_ref[...] = jnp.broadcast_to(mass, (mass.shape[0], LANES)).T[:1]


def shape(dims, dtype=jnp.float32):
    return jax.ShapeDtypeStruct(dims, dtype)


def make_body(n, g):
    def body(docs, centroids):
        rows, width = centroids.shape
        count = docs.shape[0]
        half = rows * n // 2
        chunk = 256
        plan = group_plan(g)
        limit = (4 << 20) + half * (48 << 10)

        def call(kernel, outs, *args, scratch=(), flops=0, specs=None):
            nbytes = sum(x.nbytes for x in args)
            return pl.pallas_call(
                kernel,
                out_shape=outs,
                in_specs=specs or [SMEM if x.dtype == jnp.int32 else VMEM for x in args],
                out_specs=[VMEM] * len(outs),
                scratch_shapes=scratch,
                compiler_params=pltpu.CompilerParams(vmem_limit_bytes=limit),
                cost_estimate=pl.CostEstimate(
                    flops=flops, bytes_accessed=nbytes, transcendentals=0
                ),
            )(*args)

        flops = 2 * half * count * width
        stats = [shape((count // LANES, LANES)), shape((count // LANES, LANES))]
        resp = [pltpu.VMEM((half, count), jnp.bfloat16)]
        rounded = centroids.astype(jnp.bfloat16)
        routes = chip_plan(n)
        blocks = [lax.ppermute(rounded, "dev", pairs) for pairs in routes]
        their_docs = swap(docs, "dev", n, 1)
        docs_t, own = load([docs], rounded, chunk)
        mine = jnp.concatenate([own] + blocks, axis=0)
        theirs = swap(mine, "dev", n, 1)
        part, top, total = call(
            functools.partial(scores_kernel, chunk), [shape((half, count))] + stats,
            docs_t, mine, flops=flops,
        )
        other_part, other_top, lse = call(
            functools.partial(last_scores_kernel, chunk),
            [shape((half, count), jnp.bfloat16)] + stats,
            docs_t, theirs, top, total, flops=flops,
        )
        others = [lax.ppermute(lse, "cgrp", pairs) for pairs in plan]
        their_part = swap(other_part, "dev", n, 1)
        rest = count // 4
        docs, their_first, lse = load([docs, their_docs], lse, last_rows=count - rest)
        doc_lse, factor, their_factor = call(
            functools.partial(factors_kernel, g, plan), [shape((count // LANES, LANES))] * 3,
            lax.axis_index("cgrp").reshape(1), lse, *others, top, other_top,
        )
        their_factor = swap(their_factor, "dev", n, 1)
        sums, mass, their_rest = call(
            functools.partial(first_sums_kernel, chunk),
            [shape((half, width)), shape((half, LANES)), shape((rest, width), docs.dtype)],
            factor, docs, part, pltpu.with_memory_space_constraint(their_docs, pltpu.HBM),
            scratch=resp + [pltpu.SemaphoreType.DMA], flops=flops,
            specs=[VMEM] * 3 + [pl.BlockSpec(memory_space=pltpu.HBM)],
        )
        own, own_mass, *sends = call(
            functools.partial(second_sums_kernel, chunk),
            [shape((rows, width)), shape((rows, LANES))]
            + [shape((rows, width + LANES), jnp.bfloat16)] * (n // 2 - 1),
            their_factor, their_first, their_rest, their_part, sums, mass, scratch=resp, flops=flops,
        )
        arrived = [
            lax.ppermute(x, "dev", [(target, source) for source, target in pairs])
            for x, pairs in zip(sends[::-1], routes[::-1])
        ]
        result, mass, doc_lse = call(
            final_kernel, [shape((rows, width)), shape((1, rows)), shape(doc_lse.shape)],
            own, own_mass, centroids, doc_lse, *arrived,
        )
        return (result, mass.reshape(rows), doc_lse.reshape(count))

    return body


def solution(mesh):
    in_specs = (P("dev", None), P(("cgrp", "dev"), None))
    out_specs = (P(("cgrp", "dev"), None), P(("cgrp", "dev")), P("dev"))
    return jax.shard_map(
        make_body(mesh.shape["dev"], mesh.shape["cgrp"]),
        mesh=mesh, in_specs=in_specs, out_specs=out_specs, check_vma=False,
    )
```

```python
import functools
import math

import jax
import jax.numpy as jnp
from jax import lax
from jax.experimental import pallas as pl
from jax.experimental.pallas import tpu as pltpu
from jax.sharding import PartitionSpec as P

LANES = 128
VMEM = pl.BlockSpec(memory_space=pltpu.VMEM)
SMEM = pl.BlockSpec(memory_space=pltpu.SMEM)


def swap(x, axis, size, mask):
    return lax.ppermute(x, axis, [(i, i ^ mask) for i in range(size)])


def chip_plan(n):
    near = list(range(2, n - 2, 2))
    turned = near[len(near) // 2:] + near[:len(near) // 2]
    masks = list(zip(near, turned))
    masks = masks[:1] + [(n - 2, n - 2)] + masks[1:]
    return [[(i, i ^ pair[i % 2] ^ 1) for i in range(n)] for pair in masks]


def group_plan(g):
    if g == 4:
        return [
            [(0, 1), (1, 0), (2, 3), (3, 2)],
            [(0, 3), (1, 2), (2, 0), (3, 1)],
            [(0, 2), (1, 3), (2, 1), (3, 0)],
        ]
    return [[(i, i ^ m) for i in range(g)] for m in range(1, g)]


def tree(parts, op):
    while len(parts) > 1:
        parts = [op(parts[i], parts[i + 1]) for i in range(0, len(parts), 2)]
    return parts[0]


def transpose_kernel(chunk, source_ref, follow_ref, docs_ref, own_ref, landing, sems):
    copies = []
    for i, start in enumerate(range(0, source_ref.shape[0], chunk)):
        here = pl.ds(start, chunk)
        copies.append(pltpu.make_async_copy(source_ref.at[here], landing.at[here], sems.at[i]))
        copies[-1].start()
    own_ref[...] = follow_ref[...]
    for i, copy in enumerate(copies):
        copy.wait()
        here = slice(i * chunk, (i + 1) * chunk)
        docs_ref[:, here] = landing[here, :].T


def load_kernel(source_ref, follow_ref, docs_ref, own_ref, sem):
    copy = pltpu.make_async_copy(source_ref, docs_ref, sem)
    copy.start()
    own_ref[...] = follow_ref[...]
    copy.wait()


def load(source, follow, chunk=0):
    count, width = source.shape
    kernel, dims, scratch = load_kernel, (count, width), [pltpu.SemaphoreType.DMA]
    if chunk:
        kernel, dims = functools.partial(transpose_kernel, chunk), (width, count)
        scratch = [
            pltpu.VMEM((count, width), source.dtype),
            pltpu.SemaphoreType.DMA((count // chunk,)),
        ]
    return pl.pallas_call(
        kernel,
        out_shape=[shape(dims, source.dtype), shape(follow.shape, follow.dtype)],
        in_specs=[pl.BlockSpec(memory_space=pltpu.HBM), VMEM],
        out_specs=[VMEM, VMEM],
        scratch_shapes=scratch,
        compiler_params=pltpu.CompilerParams(
            vmem_limit_bytes=(4 << 20) + (2 * source.nbytes if chunk else 0)
        ),
        cost_estimate=pl.CostEstimate(
            flops=0, bytes_accessed=2 * source.nbytes, transcendentals=0
        ),
    )(pltpu.with_memory_space_constraint(source, pltpu.HBM), follow)


def put_row(ref, start, row):
    for i in range(row.shape[1] // LANES):
        at = start // LANES + i
        ref[at:at + 1, :] = row[:, i * LANES:(i + 1) * LANES]


def scores_kernel(chunk, docs_ref, table_ref, part_ref, top_ref, sum_ref):
    width, count = docs_ref.shape
    scale = 4.0 / math.sqrt(width)
    table = table_ref[...]
    wide = table.astype(jnp.float32)
    half_norms = 0.5 * jnp.sum(wide * wide, axis=1, keepdims=True)
    for start in range(0, count, chunk):
        cols = slice(start, start + chunk)
        dots = jnp.dot(table, docs_ref[:, cols], preferred_element_type=jnp.float32)
        scores = (dots - half_norms) * scale
        top = jnp.max(scores, axis=0, keepdims=True)
        part = jnp.exp(scores - top)
        part_ref[:, cols] = part
        put_row(top_ref, start, top)
        put_row(sum_ref, start, jnp.sum(part, axis=0, keepdims=True))


def last_scores_kernel(
    chunk, docs_ref, table_ref, first_top_ref, first_sum_ref, part_ref, top_ref, lse_ref
):
    scores_kernel(chunk, docs_ref, table_ref, part_ref, top_ref, lse_ref)
    top = jnp.maximum(first_top_ref[...], top_ref[...])
    total = first_sum_ref[...] * jnp.exp(first_top_ref[...] - top)
    total += lse_ref[...] * jnp.exp(top_ref[...] - top)
    lse_ref[...] = top + jnp.log(total)


def weighted_sums(chunk, factor, docs_ref, part_ref, resp_ref, store):
    rows, count = part_ref.shape
    mass = jnp.zeros((rows, LANES), jnp.float32)
    for i in range(count // LANES):
        cols = slice(i * LANES, (i + 1) * LANES)
        resp = part_ref[:, cols] * factor[i:i + 1]
        mass += resp
        resp_ref[:, cols] = resp.astype(jnp.bfloat16)
    for start in range(0, docs_ref.shape[1], chunk):
        cols = slice(start, start + chunk)
        store(cols, jnp.dot(resp_ref[...], docs_ref[:, cols], preferred_element_type=jnp.float32))
    return jnp.sum(mass, axis=1, keepdims=True)


def mass_lanes(mass):
    high = mass.astype(jnp.bfloat16).astype(jnp.float32)
    lane = lax.broadcasted_iota(jnp.int32, (mass.shape[0], LANES), 1)
    lanes = jnp.where(lane == 0, high, jnp.where(lane == 1, mass - high, 0.0))
    return lanes.astype(jnp.bfloat16)


def read_rows(rows, width):
    wide = rows.astype(jnp.float32)
    return wide[:, :width], wide[:, width:width + 1] + wide[:, width + 1:width + 2]


def send_kernel(groups, plan, chunk, me_ref, lse_ref, *refs):
    got_refs = refs[:len(plan)]
    docs_ref, part_ref, top_ref, keep_top_ref = refs[len(plan):len(plan) + 4]
    doc_lse_ref, factor_ref, send_ref, resp_ref = refs[len(plan) + 4:]
    me = me_ref[0]
    parts = [lse_ref[...]] * groups
    for got_ref, pairs in zip(got_refs, plan):
        got = got_ref[...]
        for source, target in pairs:
            parts[source] = jnp.where(me == target, got, parts[source])
    best = tree(parts, jnp.maximum)
    doc_lse = best + jnp.log(tree([jnp.exp(x - best) for x in parts], jnp.add))
    doc_lse_ref[...] = doc_lse
    factor_ref[...] = jnp.exp(keep_top_ref[...] - doc_lse)
    factor = jnp.exp(top_ref[...] - doc_lse)

    def store(cols, term):
        send_ref[:, cols] = term.astype(jnp.bfloat16)

    mass = weighted_sums(chunk, factor, docs_ref, part_ref, resp_ref, store)
    send_ref[:, docs_ref.shape[1]:] = mass_lanes(mass)


def keep_kernel(chunk, factor_ref, docs_ref, part_ref, keep_ref, keep_mass_ref, resp_ref):
    def store(cols, term):
        keep_ref[:, cols] = term

    mass = weighted_sums(chunk, factor_ref[...], docs_ref, part_ref, resp_ref, store)
    keep_mass_ref[...] = jnp.broadcast_to(mass, keep_mass_ref.shape)


def fold_kernel(keep_ref, keep_mass_ref, got_ref, own_ref, own_mass_ref, *send_refs):
    rows, width = own_ref.shape
    for slot in range(keep_ref.shape[0] // rows):
        here = slice(slot * rows, (slot + 1) * rows)
        got, got_mass = read_rows(got_ref[here], width)
        term = keep_ref[here] + got
        mass = keep_mass_ref[here, :1] + got_mass
        if slot == 0:
            own_ref[...] = term
            own_mass_ref[...] = jnp.broadcast_to(mass, own_mass_ref.shape)
        else:
            send_refs[slot - 1][:, :width] = term.astype(jnp.bfloat16)
            send_refs[slot - 1][:, width:] = mass_lanes(mass)


def final_kernel(own_ref, own_mass_ref, cent_ref, lse_ref, *refs):
    *got_refs, next_ref, mass_ref, doc_lse_ref = refs
    doc_lse_ref[...] = lse_ref[...]
    width = own_ref.shape[1]
    got = [read_rows(r[...], width) for r in got_refs]
    term = tree([own_ref[...]] + [a for a, _ in got], jnp.add)
    mass = tree([own_mass_ref[:, :1]] + [b for _, b in got], jnp.add)
    next_ref[...] = (term + cent_ref[...]) / (mass + 1.0)
    mass_ref[...] = jnp.broadcast_to(mass, (mass.shape[0], LANES)).T[:1]


def shape(dims, dtype=jnp.float32):
    return jax.ShapeDtypeStruct(dims, dtype)


def make_body(n, g):
    def body(docs, centroids):
        rows, width = centroids.shape
        count = docs.shape[0]
        half = rows * n // 2
        chunk = 256
        plan = group_plan(g)
        limit = (4 << 20) + half * (48 << 10)

        def call(kernel, outs, *args, scratch=(), flops=0):
            nbytes = sum(x.nbytes for x in args)
            return pl.pallas_call(
                kernel,
                out_shape=outs,
                in_specs=[SMEM if x.dtype == jnp.int32 else VMEM for x in args],
                out_specs=[VMEM] * len(outs),
                scratch_shapes=scratch,
                compiler_params=pltpu.CompilerParams(vmem_limit_bytes=limit),
                cost_estimate=pl.CostEstimate(
                    flops=flops, bytes_accessed=nbytes, transcendentals=0
                ),
            )(*args)

        flops = 2 * half * count * width
        stats = [shape((half, count)), shape((count // LANES, LANES)), shape((count // LANES, LANES))]
        resp = [pltpu.VMEM((half, count), jnp.bfloat16)]
        rounded = centroids.astype(jnp.bfloat16)
        routes = chip_plan(n)
        blocks = [lax.ppermute(rounded, "dev", pairs) for pairs in routes]
        docs_t, own = load(docs, rounded, chunk)
        mine = jnp.concatenate([own] + blocks, axis=0)
        theirs = swap(mine, "dev", n, 1)
        part, top, total = call(
            functools.partial(scores_kernel, chunk), stats, docs_t, mine, flops=flops
        )
        other_part, other_top, lse = call(
            functools.partial(last_scores_kernel, chunk), stats,
            docs_t, theirs, top, total, flops=flops,
        )
        others = [lax.ppermute(lse, "cgrp", pairs) for pairs in plan]
        docs, lse = load(docs, lse)
        doc_lse, factor, send = call(
            functools.partial(send_kernel, g, plan, chunk),
            [shape((count // LANES, LANES)), shape((count // LANES, LANES)), shape((half, width + LANES), jnp.bfloat16)],
            lax.axis_index("cgrp").reshape(1), lse, *others, docs, other_part, other_top, top,
            scratch=resp, flops=flops,
        )
        got = swap(send, "dev", n, 1)
        keep, keep_mass = call(
            functools.partial(keep_kernel, chunk),
            [shape((half, width)), shape((half, LANES))],
            factor, docs, part, scratch=resp, flops=flops,
        )
        own, own_mass, *sends = call(
            fold_kernel,
            [shape((rows, width)), shape((rows, LANES))]
            + [shape((rows, width + LANES), jnp.bfloat16)] * (n // 2 - 1),
            keep, keep_mass, got,
        )
        arrived = [
            lax.ppermute(x, "dev", [(target, source) for source, target in pairs])
            for x, pairs in zip(sends[::-1], routes[::-1])
        ]
        result, mass, doc_lse = call(
            final_kernel, [shape((rows, width)), shape((1, rows)), shape(doc_lse.shape)],
            own, own_mass, centroids, doc_lse, *arrived,
        )
        return (result, mass.reshape(rows), doc_lse.reshape(count))

    return body


def solution(mesh):
    in_specs = (P("dev", None), P(("cgrp", "dev"), None))
    out_specs = (P(("cgrp", "dev"), None), P(("cgrp", "dev")), P("dev"))
    return jax.shard_map(
        make_body(mesh.shape["dev"], mesh.shape["cgrp"]),
        mesh=mesh, in_specs=in_specs, out_specs=out_specs, check_vma=False,
    )
```

```python
import functools
import math

import jax
import jax.numpy as jnp
from jax import lax
from jax.experimental import pallas as pl
from jax.experimental.pallas import tpu as pltpu
from jax.sharding import PartitionSpec as P

LANES = 128
VMEM = pl.BlockSpec(memory_space=pltpu.VMEM)
SMEM = pl.BlockSpec(memory_space=pltpu.SMEM)


def swap(x, axis, size, mask):
    return lax.ppermute(x, axis, [(i, i ^ mask) for i in range(size)])


def chip_plan(n):
    near = list(range(2, n - 2, 2))
    turned = near[len(near) // 2:] + near[:len(near) // 2]
    masks = list(zip(turned, near))
    masks = masks[:1] + [(n - 2, n - 2)] + masks[1:]
    return [[(i, i ^ pair[i % 2] ^ 1) for i in range(n)] for pair in masks]


def group_plan(g):
    if g == 4:
        return [
            [(0, 1), (1, 0), (2, 3), (3, 2)],
            [(0, 3), (1, 2), (2, 0), (3, 1)],
            [(0, 2), (1, 3), (2, 1), (3, 0)],
        ]
    return [[(i, i ^ m) for i in range(g)] for m in range(1, g)]


def tree(parts, op):
    while len(parts) > 1:
        parts = [op(parts[i], parts[i + 1]) for i in range(0, len(parts), 2)]
    return parts[0]


def transpose_kernel(chunk, source_ref, follow_ref, docs_ref, own_ref, landing, sems):
    copies = []
    for i, start in enumerate(range(0, source_ref.shape[0], chunk)):
        here = pl.ds(start, chunk)
        copies.append(pltpu.make_async_copy(source_ref.at[here], landing.at[here], sems.at[i]))
        copies[-1].start()
    own_ref[...] = follow_ref[...]
    for i, copy in enumerate(copies):
        copy.wait()
        here = slice(i * chunk, (i + 1) * chunk)
        docs_ref[:, here] = landing[here, :].T


def load_kernel(source_ref, follow_ref, docs_ref, own_ref, sem):
    copy = pltpu.make_async_copy(source_ref, docs_ref, sem)
    copy.start()
    own_ref[...] = follow_ref[...]
    copy.wait()


def load(source, follow, chunk=0):
    count, width = source.shape
    kernel, dims, scratch = load_kernel, (count, width), [pltpu.SemaphoreType.DMA]
    if chunk:
        kernel, dims = functools.partial(transpose_kernel, chunk), (width, count)
        scratch = [
            pltpu.VMEM((count, width), source.dtype),
            pltpu.SemaphoreType.DMA((count // chunk,)),
        ]
    return pl.pallas_call(
        kernel,
        out_shape=[shape(dims, source.dtype), shape(follow.shape, follow.dtype)],
        in_specs=[pl.BlockSpec(memory_space=pltpu.HBM), VMEM],
        out_specs=[VMEM, VMEM],
        scratch_shapes=scratch,
        compiler_params=pltpu.CompilerParams(
            vmem_limit_bytes=(4 << 20) + (2 * source.nbytes if chunk else 0)
        ),
        cost_estimate=pl.CostEstimate(
            flops=0, bytes_accessed=2 * source.nbytes, transcendentals=0
        ),
    )(pltpu.with_memory_space_constraint(source, pltpu.HBM), follow)


def put_row(ref, start, row):
    for i in range(row.shape[1] // LANES):
        at = start // LANES + i
        ref[at:at + 1, :] = row[:, i * LANES:(i + 1) * LANES]


def scores_kernel(chunk, docs_ref, table_ref, part_ref, top_ref, sum_ref):
    width, count = docs_ref.shape
    scale = 4.0 / math.sqrt(width)
    table = table_ref[...]
    wide = table.astype(jnp.float32)
    half_norms = 0.5 * jnp.sum(wide * wide, axis=1, keepdims=True)
    for start in range(0, count, chunk):
        cols = slice(start, start + chunk)
        dots = jnp.dot(table, docs_ref[:, cols], preferred_element_type=jnp.float32)
        scores = (dots - half_norms) * scale
        top = jnp.max(scores, axis=0, keepdims=True)
        part = jnp.exp(scores - top)
        part_ref[:, cols] = part
        put_row(top_ref, start, top)
        put_row(sum_ref, start, jnp.sum(part, axis=0, keepdims=True))


def last_scores_kernel(
    chunk, docs_ref, table_ref, first_top_ref, first_sum_ref, part_ref, top_ref, lse_ref
):
    scores_kernel(chunk, docs_ref, table_ref, part_ref, top_ref, lse_ref)
    top = jnp.maximum(first_top_ref[...], top_ref[...])
    total = first_sum_ref[...] * jnp.exp(first_top_ref[...] - top)
    total += lse_ref[...] * jnp.exp(top_ref[...] - top)
    lse_ref[...] = top + jnp.log(total)


def weighted_sums(chunk, factor, docs_ref, part_ref, resp_ref, store):
    rows, count = part_ref.shape
    mass = jnp.zeros((rows, LANES), jnp.float32)
    for i in range(count // LANES):
        cols = slice(i * LANES, (i + 1) * LANES)
        resp = part_ref[:, cols] * factor[i:i + 1]
        mass += resp
        resp_ref[:, cols] = resp.astype(jnp.bfloat16)
    for start in range(0, docs_ref.shape[1], chunk):
        cols = slice(start, start + chunk)
        store(cols, jnp.dot(resp_ref[...], docs_ref[:, cols], preferred_element_type=jnp.float32))
    return jnp.sum(mass, axis=1, keepdims=True)


def mass_lanes(mass):
    high = mass.astype(jnp.bfloat16).astype(jnp.float32)
    lane = lax.broadcasted_iota(jnp.int32, (mass.shape[0], LANES), 1)
    lanes = jnp.where(lane == 0, high, jnp.where(lane == 1, mass - high, 0.0))
    return lanes.astype(jnp.bfloat16)


def read_rows(rows, width):
    wide = rows.astype(jnp.float32)
    return wide[:, :width], wide[:, width:width + 1] + wide[:, width + 1:width + 2]


def send_kernel(groups, plan, chunk, me_ref, lse_ref, *refs):
    got_refs = refs[:len(plan)]
    docs_ref, part_ref, top_ref, keep_top_ref = refs[len(plan):len(plan) + 4]
    doc_lse_ref, factor_ref, send_ref, resp_ref = refs[len(plan) + 4:]
    me = me_ref[0]
    parts = [lse_ref[...]] * groups
    for got_ref, pairs in zip(got_refs, plan):
        got = got_ref[...]
        for source, target in pairs:
            parts[source] = jnp.where(me == target, got, parts[source])
    best = tree(parts, jnp.maximum)
    doc_lse = best + jnp.log(tree([jnp.exp(x - best) for x in parts], jnp.add))
    doc_lse_ref[...] = doc_lse
    factor_ref[...] = jnp.exp(keep_top_ref[...] - doc_lse)
    factor = jnp.exp(top_ref[...] - doc_lse)

    def store(cols, term):
        send_ref[:, cols] = term.astype(jnp.bfloat16)

    mass = weighted_sums(chunk, factor, docs_ref, part_ref, resp_ref, store)
    send_ref[:, docs_ref.shape[1]:] = mass_lanes(mass)


def keep_kernel(chunk, factor_ref, docs_ref, part_ref, keep_ref, keep_mass_ref, resp_ref):
    def store(cols, term):
        keep_ref[:, cols] = term

    mass = weighted_sums(chunk, factor_ref[...], docs_ref, part_ref, resp_ref, store)
    keep_mass_ref[...] = jnp.broadcast_to(mass, keep_mass_ref.shape)


def fold_kernel(keep_ref, keep_mass_ref, got_ref, own_ref, own_mass_ref, *send_refs):
    rows, width = own_ref.shape
    for slot in range(keep_ref.shape[0] // rows):
        here = slice(slot * rows, (slot + 1) * rows)
        got, got_mass = read_rows(got_ref[here], width)
        term = keep_ref[here] + got
        mass = keep_mass_ref[here, :1] + got_mass
        if slot == 0:
            own_ref[...] = term
            own_mass_ref[...] = jnp.broadcast_to(mass, own_mass_ref.shape)
        else:
            send_refs[slot - 1][:, :width] = term.astype(jnp.bfloat16)
            send_refs[slot - 1][:, width:] = mass_lanes(mass)


def final_kernel(own_ref, own_mass_ref, cent_ref, lse_ref, *refs):
    *got_refs, next_ref, mass_ref, doc_lse_ref = refs
    doc_lse_ref[...] = lse_ref[...]
    width = own_ref.shape[1]
    got = [read_rows(r[...], width) for r in got_refs]
    term = tree([own_ref[...]] + [a for a, _ in got], jnp.add)
    mass = tree([own_mass_ref[:, :1]] + [b for _, b in got], jnp.add)
    next_ref[...] = (term + cent_ref[...]) / (mass + 1.0)
    mass_ref[...] = jnp.broadcast_to(mass, (mass.shape[0], LANES)).T[:1]


def shape(dims, dtype=jnp.float32):
    return jax.ShapeDtypeStruct(dims, dtype)


def make_body(n, g):
    def body(docs, centroids):
        rows, width = centroids.shape
        count = docs.shape[0]
        half = rows * n // 2
        chunk = 256
        plan = group_plan(g)
        limit = (4 << 20) + half * (48 << 10)

        def call(kernel, outs, *args, scratch=(), flops=0):
            nbytes = sum(x.nbytes for x in args)
            return pl.pallas_call(
                kernel,
                out_shape=outs,
                in_specs=[SMEM if x.dtype == jnp.int32 else VMEM for x in args],
                out_specs=[VMEM] * len(outs),
                scratch_shapes=scratch,
                compiler_params=pltpu.CompilerParams(vmem_limit_bytes=limit),
                cost_estimate=pl.CostEstimate(
                    flops=flops, bytes_accessed=nbytes, transcendentals=0
                ),
            )(*args)

        flops = 2 * half * count * width
        stats = [shape((half, count)), shape((count // LANES, LANES)), shape((count // LANES, LANES))]
        resp = [pltpu.VMEM((half, count), jnp.bfloat16)]
        rounded = centroids.astype(jnp.bfloat16)
        routes = chip_plan(n)
        blocks = [lax.ppermute(rounded, "dev", pairs) for pairs in routes]
        docs_t, own = load(docs, rounded, chunk)
        mine = jnp.concatenate([own] + blocks, axis=0)
        theirs = swap(mine, "dev", n, 1)
        part, top, total = call(
            functools.partial(scores_kernel, chunk), stats, docs_t, mine, flops=flops
        )
        other_part, other_top, lse = call(
            functools.partial(last_scores_kernel, chunk), stats,
            docs_t, theirs, top, total, flops=flops,
        )
        others = [lax.ppermute(lse, "cgrp", pairs) for pairs in plan]
        docs, lse = load(docs, lse)
        doc_lse, factor, send = call(
            functools.partial(send_kernel, g, plan, chunk),
            [shape((count // LANES, LANES)), shape((count // LANES, LANES)), shape((half, width + LANES), jnp.bfloat16)],
            lax.axis_index("cgrp").reshape(1), lse, *others, docs, other_part, other_top, top,
            scratch=resp, flops=flops,
        )
        got = swap(send, "dev", n, 1)
        keep, keep_mass = call(
            functools.partial(keep_kernel, chunk),
            [shape((half, width)), shape((half, LANES))],
            factor, docs, part, scratch=resp, flops=flops,
        )
        own, own_mass, *sends = call(
            fold_kernel,
            [shape((rows, width)), shape((rows, LANES))]
            + [shape((rows, width + LANES), jnp.bfloat16)] * (n // 2 - 1),
            keep, keep_mass, got,
        )
        arrived = [
            lax.ppermute(x, "dev", [(target, source) for source, target in pairs])
            for x, pairs in zip(sends[::-1], routes[::-1])
        ]
        result, mass, doc_lse = call(
            final_kernel, [shape((rows, width)), shape((1, rows)), shape(doc_lse.shape)],
            own, own_mass, centroids, doc_lse, *arrived,
        )
        return (result, mass.reshape(rows), doc_lse.reshape(count))

    return body


def solution(mesh):
    in_specs = (P("dev", None), P(("cgrp", "dev"), None))
    out_specs = (P(("cgrp", "dev"), None), P(("cgrp", "dev")), P("dev"))
    return jax.shard_map(
        make_body(mesh.shape["dev"], mesh.shape["cgrp"]),
        mesh=mesh, in_specs=in_specs, out_specs=out_specs, check_vma=False,
    )
```
